32 devices in a mesh: lat: 4 (over y, core), lon: 8 (over z, x).
Axes of the slice: x: 2, y: 2, z: 4, core: 2. Of those that a mesh axis runs over, the one named last changes fastest.
Arguments:
- losses: float32 [8, 16, 512, 256], P('lat', 'lon'), may hold values from -6 to 6
- positions: float32 [8, 16, 2, 512], P('lat', 'lon'), may hold values from 0 to 1
- leaf_basis: float32 [8, 16, 512, 64], P('lat', 'lon'), may hold values from -0.25 to 0.25
- near_flags: int32 [8, 16, 9], P('lat', 'lon'), may hold values from 0 to 1, as said below
- leaf_coupling: bfloat16 [8, 16, 36, 64, 64], P('lat', 'lon'), may hold values from -0.75 to 0.75
- leaf_transfer: float32 [8, 16, 64, 64], P('lat', 'lon'), may hold values from -0.75 to 0.75
- device_coupling: bfloat16 [4, 8, 36, 64, 64], P('lat', 'lon'), may hold values from -0.1875 to 0.1875
- device_transfer: float32 [4, 8, 64, 64], replicated, may hold values from -0.75 to 0.75
- group_coupling: bfloat16 [2, 4, 2, 4, 64, 64], replicated, may hold values from -0.09375 to 0.09375
Outputs:
- applied: float32 [8, 16, 512, 256], P('lat', 'lon')
The draws below stay inside these ranges and needn't reach their ends.
Inputs may be any that keep to these rules, and one draw needn't show every extreme that they name: near_flags[i, j, 3 (di + 1) + dj + 1] is 1 when leaf (i + di, (j + dj) mod 16) forms a dense block with leaf (i, j); the flags of a pair agree seen from both leaves, the middle flag is always 1, and flags toward latitude indices outside the grid are 0.
All inputs are finite; a program needn't handle non-finite values.
Results may differ from the reference program's by a relative error of at most 0.0003.
Values sent between devices are 32-bit elements; how exact they have to be, the bound alone decides.
No kernel may reach another device: no remote copies, remote signals or barrier semaphores. Data moves between devices by JAX's collectives and lax.ppermute only.
A program may use at most 192 MiB of HBM per device.

```python
import jax
import jax.numpy as jnp
import numpy as np
from jax import lax

LEAF_PTS = 512
RANK = 64
COLS = 256
LEAF_LAT = 2
LEAF_LON = 2
LAT_LEAVES = 8
LON_LEAVES = 16
WINDOW = 36
GROUP_LAT = 2
GROUP_LON = 4
N_LAT = 4
N_LON = 8


def draw_near_flags(key, part):
    density = jax.random.randint(jax.random.fold_in(key, 11), (LAT_LEAVES, LON_LEAVES), 0, 4) * jax.random.randint(jax.random.fold_in(key, 31), (LAT_LEAVES, LON_LEAVES), 0, 2)
    pair_level = jax.random.randint(jax.random.fold_in(key, 23), (LAT_LEAVES, LON_LEAVES, 4), 0, 4)
    forward = ((0, 1), (1, -1), (1, 0), (1, 1))
    row_ids = jnp.arange(LAT_LEAVES, dtype=jnp.int32)
    flag_list = []
    for row_step in (-1, 0, 1):
        for col_step in (-1, 0, 1):
            if row_step == 0 and col_step == 0:
                flag_list.append(jnp.ones((LAT_LEAVES, LON_LEAVES), jnp.int32))
                continue
            other = jnp.roll(density, (-row_step, -col_step), (0, 1))
            if (row_step, col_step) in forward:
                level = pair_level[:, :, forward.index((row_step, col_step))]
            else:
                level = jnp.roll(pair_level[:, :, forward.index((-row_step, -col_step))], (-row_step, -col_step), (0, 1))
            inside = (row_ids + row_step >= 0) & (row_ids + row_step < LAT_LEAVES)
            dense_pair = (jnp.maximum(density, other) > level) & inside[:, None]
            flag_list.append(jnp.where(dense_pair, 1, 0).astype(jnp.int32))
    return jnp.stack(flag_list, -1)


def block_levels(rng, shape, pieces, low, high):
    def one(position, shards_of):
        steps = jax.random.uniform(jax.random.fold_in(jax.random.fold_in(rng, 6), position), (shards_of,), jnp.float32, low / len(pieces), high / len(pieces))
        return jnp.repeat(jnp.exp(steps), shape[position] // shards_of).reshape((-1,) + (1,) * (len(shape) - position - 1))

    loudness = one(*pieces[0])
    for cut in pieces[1:]:
        loudness = loudness * one(*cut)
    return loudness


def scatter_about(own_key, extent, scale, most, shards=(), held_as=jnp.bfloat16):
    gain = block_levels(own_key, extent, shards, -0.22, 0.18) if shards else 1.0
    drawn = jax.random.normal(own_key, extent, jnp.float32) * scale * gain
    return jnp.minimum(jnp.maximum(drawn, -most), most).astype(held_as)


def setup_inputs(seed: int = 0) -> dict:
    streams_of = jax.random.split(jax.random.key(seed), 10)
    return {
        "losses": scatter_about(streams_of[0], (LAT_LEAVES, LON_LEAVES, LEAF_PTS, COLS), 1.0, 6.0, ((0, 4), (1, 8)), jnp.float32),
        "positions": jnp.clip(1.0 * jax.random.uniform(streams_of[1], (LAT_LEAVES, LON_LEAVES, 2, LEAF_PTS), jnp.float32) ** block_levels(streams_of[1], (LAT_LEAVES, LON_LEAVES, 2, LEAF_PTS), ((0, 4), (1, 8)), -0.2, 0.2), 0.0, 1.0),
        "leaf_basis": scatter_about(streams_of[2], (LAT_LEAVES, LON_LEAVES, LEAF_PTS, RANK), LEAF_PTS ** -0.5, 0.25, ((0, 4), (1, 8)), jnp.float32),
        "near_flags": draw_near_flags(jax.random.fold_in(streams_of[9], 71), 0),
        "leaf_coupling": scatter_about(streams_of[4], (LAT_LEAVES, LON_LEAVES, WINDOW, RANK, RANK), RANK ** -0.5, 0.75, ((0, 4), (1, 8))),
        "leaf_transfer": scatter_about(streams_of[5], (LAT_LEAVES, LON_LEAVES, RANK, RANK), RANK ** -0.5, 0.75, ((0, 4), (1, 8)), jnp.float32),
        "device_coupling": scatter_about(streams_of[6], (N_LAT, N_LON, 36, RANK, RANK), (RANK * 16) ** -0.5, 0.1875, ((0, 4), (1, 8))),
        "device_transfer": scatter_about(streams_of[7], (N_LAT, N_LON, RANK, RANK), RANK ** -0.5, 0.75, (), jnp.float32),
        "group_coupling": scatter_about(streams_of[8], (GROUP_LAT, GROUP_LON, GROUP_LAT, GROUP_LON, RANK, RANK), (RANK * 64) ** -0.5, 0.09375),
    }


highest = lax.Precision.HIGHEST
length_scale = 0.15
nugget = 0.5
root_three = 1.7320508075688772

def matern(target, source, row_shift, col_shift):
    delta_row = target[0][:, None] - (source[0][None, :] + row_shift)
    delta_col = target[1][:, None] - (source[1][None, :] + col_shift)
    scaled = root_three / length_scale * jnp.sqrt(delta_row * delta_row + delta_col * delta_col)
    return (1.0 + scaled) * jnp.exp(-scaled)

def zone_table(rows_lat, rows_lon):
    one_hot = np.zeros((rows_lat, rows_lon, 9, 3 * rows_lat, 3 * rows_lon), np.float32)
    for row_leaf in range(rows_lat):
        for col_leaf in range(rows_lon):
            for row_step in range(3):
                for col_step in range(3):
                    one_hot[row_leaf, col_leaf, row_step * 3 + col_step, rows_lat + row_leaf + row_step - 1, rows_lon + col_leaf + col_step - 1] = 1.0
    return one_hot

def group_far(own_row, own_col, group_rows, group_cols):
    rows_far = jnp.abs(jnp.arange(group_rows, dtype=jnp.int32) - own_row) >= 2
    distance = (jnp.arange(group_cols, dtype=jnp.int32) - own_col) % group_cols
    cols_far = (distance >= 2) & (distance <= group_cols - 2)
    return jnp.where(rows_far[:, None] | cols_far[None, :], 1.0, 0.0).astype(jnp.float32)

def device_keep(lat_pos, lon_pos):
    step_ids = jnp.arange(6, dtype=jnp.int32)
    row_ids = 2 * (lat_pos // 2) - 2 + step_ids
    offsets = 2 * (lon_pos // 2) - 2 + step_ids - lon_pos
    inside = (jnp.abs(row_ids - lat_pos) <= 1)[:, None] & (jnp.abs(offsets) <= 1)[None, :]
    return jnp.where(inside, 0.0, 1.0).astype(jnp.float32).reshape(36)

def reference(losses, positions, leaf_basis, near_flags, leaf_coupling, leaf_transfer, device_coupling, device_transfer, group_coupling):
    flags_float = near_flags.astype(jnp.float32)
    loss_pad = jnp.pad(losses, ((1, 1), (0, 0), (0, 0), (0, 0)))
    place_pad = jnp.pad(positions, ((1, 1), (0, 0), (0, 0), (0, 0)))
    leaf_ids = jnp.arange(LAT_LEAVES * LON_LEAVES, dtype=jnp.int32)

    def near_leaf(leaf_index):
        row_leaf = leaf_index // LON_LEAVES
        col_leaf = leaf_index % LON_LEAVES
        own_place = positions[row_leaf, col_leaf]
        near_sum = nugget * losses[row_leaf, col_leaf]
        for row_step in (-1, 0, 1):
            for col_step in (-1, 0, 1):
                flag_value = near_flags[row_leaf, col_leaf, (row_step + 1) * 3 + col_step + 1]
                other_row = row_leaf + row_step + 1
                other_col = (col_leaf + col_step) % LON_LEAVES

                def dense_block(other_row=other_row, other_col=other_col, row_step=row_step, col_step=col_step):
                    kernel = matern(own_place, place_pad[other_row, other_col], float(row_step), float(col_step))
                    return jnp.dot(kernel, loss_pad[other_row, other_col], precision=highest)
                near_sum = near_sum + lax.cond(flag_value > 0, dense_block, lambda: jnp.zeros_like(losses[0, 0]))
        return near_sum
    near = lax.map(near_leaf, leaf_ids).reshape(LAT_LEAVES, LON_LEAVES, LEAF_PTS, COLS)
    leaf_coef = jnp.einsum('ijpr,ijpc->ijrc', leaf_basis, losses, precision=highest)
    coef_pad = jnp.pad(leaf_coef, ((LEAF_LAT, LEAF_LAT), (0, 0), (0, 0), (0, 0)))
    zone_mask = jnp.asarray(zone_table(LEAF_LAT, LEAF_LON)).astype(jnp.float32)

    def leaf_far_one(leaf_index):
        row_leaf = leaf_index // LON_LEAVES
        col_leaf = leaf_index % LON_LEAVES
        lat_pos = row_leaf // LEAF_LAT
        lon_pos = col_leaf // LEAF_LON
        lat_band = lax.dynamic_slice_in_dim(coef_pad, (lat_pos * LEAF_LAT).astype(jnp.int32), 3 * LEAF_LAT, 0)
        columns = ((LEAF_LON * (lon_pos - 1) + jnp.arange(3 * LEAF_LON, dtype=jnp.int32)) % LON_LEAVES).astype(jnp.int32)
        window = jnp.take(lat_band, columns, axis=1).reshape(WINDOW, RANK, COLS)
        covered = jnp.einsum('o,ouv->uv', flags_float[row_leaf, col_leaf], zone_mask[row_leaf % LEAF_LAT, col_leaf % LEAF_LON])
        keep_mask = (1.0 - covered).reshape(WINDOW)
        weights = leaf_coupling[row_leaf, col_leaf].astype(jnp.float32) * keep_mask[:, None, None]
        return jnp.einsum('wrk,wkc->rc', weights, window, precision=highest)
    leaf_far = lax.map(leaf_far_one, leaf_ids).reshape(LAT_LEAVES, LON_LEAVES, RANK, COLS)
    device_coef = jnp.einsum('pbqdkr,pbqdkc->pqrc', leaf_transfer.reshape(N_LAT, LEAF_LAT, N_LON, LEAF_LON, RANK, RANK), leaf_coef.reshape(N_LAT, LEAF_LAT, N_LON, LEAF_LON, RANK, COLS), precision=highest)
    device_pad = jnp.pad(device_coef, ((2, 2), (0, 0), (0, 0), (0, 0)))

    def device_far_one(device_index):
        lat_pos = device_index // N_LON
        lon_pos = device_index % N_LON
        lat_band = lax.dynamic_slice_in_dim(device_pad, (2 * (lat_pos // 2)).astype(jnp.int32), 6, 0)
        columns = ((2 * (lon_pos // 2) - 2 + jnp.arange(6, dtype=jnp.int32)) % N_LON).astype(jnp.int32)
        window = jnp.take(lat_band, columns, axis=1).reshape(36, RANK, COLS)
        weights = device_coupling[lat_pos, lon_pos].astype(jnp.float32) * device_keep(lat_pos, lon_pos)[:, None, None]
        return jnp.einsum('vrk,vkc->rc', weights, window, precision=highest)
    device_far = lax.map(device_far_one, jnp.arange(N_LAT * N_LON, dtype=jnp.int32)).reshape(N_LAT, N_LON, RANK, COLS)
    shares = jnp.einsum('pqkr,pqkc->pqrc', device_transfer, device_coef, precision=highest)
    group_coef = shares.reshape(N_LAT // 2, 2, N_LON // 2, 2, RANK, COLS).sum(axis=(1, 3))

    def group_one(group_index):
        own_row = group_index // (N_LON // 2)
        own_col = group_index % (N_LON // 2)
        far_mask = group_far(own_row, own_col, N_LAT // 2, N_LON // 2)
        weights = group_coupling[own_row, own_col].astype(jnp.float32) * far_mask[:, :, None, None]
        return jnp.einsum('xyrk,xykc->rc', weights, group_coef, precision=highest)
    group_field = lax.map(group_one, jnp.arange(N_LAT // 2 * (N_LON // 2), dtype=jnp.int32)).reshape(N_LAT // 2, N_LON // 2, RANK, COLS)
    spread = jnp.repeat(jnp.repeat(group_field, 2, axis=0), 2, axis=1)
    device_field = device_far + jnp.einsum('pqrk,pqkc->pqrc', device_transfer, spread, precision=highest)
    device_spread = jnp.repeat(jnp.repeat(device_field, LEAF_LAT, axis=0), LEAF_LON, axis=1)
    leaf_field = leaf_far + jnp.einsum('ijrk,ijkc->ijrc', leaf_transfer, device_spread, precision=highest)
    return near + jnp.einsum('ijpr,ijrc->ijpc', leaf_basis, leaf_field, precision=highest)
```

```python
import functools

import jax
import jax.numpy as jnp
from jax import lax
from jax.experimental import pallas as pl
from jax.experimental.pallas import tpu as pltpu
from jax.sharding import PartitionSpec as P

PTS = 512
RANK = 64
COLS = 256
HALF = 256

LN2 = 0.6931471805599453
UNIT = 1.7320508075688772 / 0.15 / LN2

f32 = jnp.float32
bf16 = jnp.bfloat16
VMEM = pltpu.VMEM
SMEM = pltpu.SMEM


def split(x):
    hi = x.astype(bf16)
    return hi, (x - hi.astype(f32)).astype(bf16)


def mm(a, b, dims=(1, 0)):
    return lax.dot_general(
        a, b, (((dims[0],), (dims[1],)), ((), ())), preferred_element_type=f32
    )


def mm3(a, b, dims=(1, 0)):
    a_hi, a_lo = split(a)
    b_hi, b_lo = split(b)
    return mm(a_hi, b_hi, dims) + (mm(a_lo, b_hi, dims) + mm(a_hi, b_lo, dims))


def mm2(a, b):
    b_hi, b_lo = split(b)
    return mm(a, b_hi) + mm(a, b_lo)


def vmem_spec(shape=None, index=None):
    if shape is None:
        return pl.BlockSpec(memory_space=VMEM)
    return pl.BlockSpec(shape, lambda *_: index)


def params(limit):
    return pltpu.CompilerParams(vmem_limit_bytes=limit * 1024 * 1024)


def coef_kernel(loss, basis, transfer, pos, msg, tpos, dev, to_y, to_c):
    leaf = pl.program_id(0)
    parity = lax.rem(lax.axis_index("lat"), 2)
    row = leaf // 2
    col = lax.rem(leaf, 2)
    values = loss[0]
    l_hi, l_lo = split(values)
    b_hi, b_lo = split(basis[0])
    coef = mm(
        jnp.concatenate([b_hi, b_lo, b_hi], 0), jnp.concatenate([l_hi, l_hi, l_lo], 0), (0, 0)
    )
    msg[pl.ds(leaf * RANK, RANK), :] = coef
    place = pos[0] * UNIT
    for coord in range(2):
        for half in range(2):
            msg[pl.ds(4 * RANK + 4 * leaf + 2 * coord + half, 1), :] = place[
                coord : coord + 1, half * HALF : (half + 1) * HALF
            ]
    tpos[0] = jnp.concatenate([place, jnp.zeros((6, PTS), f32)], 0).T
    part = mm3(transfer[0], coef, (0, 0))

    @pl.when(leaf == 0)
    def _():
        dev[...] = part

    @pl.when(leaf > 0)
    def _():
        dev[...] += part

    @pl.when(row == parity)
    def _():
        to_y[pl.ds(col * PTS, PTS), :] = values

    @pl.when(row != parity)
    def _():
        to_c[pl.ds(col * PTS, PTS), :] = values

    @pl.when(leaf == 3)
    def _():
        to_y[2 * PTS :, :] = msg[...]
        to_c[2 * PTS :, :] = msg[...]


def coefficients(losses, basis, transfer, positions):
    rows = 4 * RANK + 16
    return pl.pallas_call(
        coef_kernel,
        grid=(4,),
        in_specs=[
            pl.BlockSpec((1, PTS, COLS), lambda i: (i, 0, 0)),
            pl.BlockSpec((1, PTS, RANK), lambda i: (i, 0, 0)),
            pl.BlockSpec((1, RANK, RANK), lambda i: (i, 0, 0)),
            pl.BlockSpec((1, 2, PTS), lambda i: (i, 0, 0)),
        ],
        out_specs=[
            pl.BlockSpec((rows, COLS), lambda i: (0, 0)),
            pl.BlockSpec((1, PTS, 8), lambda i: (i, 0, 0)),
            pl.BlockSpec((RANK, COLS), lambda i: (0, 0)),
            pl.BlockSpec((2 * PTS + rows, COLS), lambda i: (0, 0)),
            pl.BlockSpec((2 * PTS + rows, COLS), lambda i: (0, 0)),
        ],
        out_shape=[
            jax.ShapeDtypeStruct((rows, COLS), f32),
            jax.ShapeDtypeStruct((4, PTS, 8), f32),
            jax.ShapeDtypeStruct((RANK, COLS), f32),
            jax.ShapeDtypeStruct((2 * PTS + rows, COLS), f32),
            jax.ShapeDtypeStruct((2 * PTS + rows, COLS), f32),
        ],
        compiler_params=params(32),
        cost_estimate=pl.CostEstimate(
            flops=1_000_000_000, bytes_accessed=6_000_000, transcendentals=0
        ),
        name="coefs",
    )(losses, basis, transfer, positions)


def near_kernel(n_src, n_pos, sources, slots, pairs, first, *refs):
    flags, tpos = refs[:2]
    places = refs[2 : 2 + n_pos]
    losses = refs[2 + n_pos : 2 + n_pos + n_src]
    rest = refs[2 + n_pos + n_src :]
    if first:
        acc, table, spos, stack = rest
    else:
        before, acc, table, spos, stack = rest
    parity = lax.rem(lax.axis_index("lat"), 2)
    for slot, (ref_id, pick, pos_id, pos_row) in enumerate(slots):
        values = losses[ref_id][pick]
        hi, lo = split(values)
        stack[slot, :PTS, :] = hi
        stack[slot, PTS : 2 * PTS, :] = hi
        stack[slot, 2 * PTS :, :] = lo
        base = pos_row(parity)
        for coord in range(2):
            for half in range(2):
                spos[slot, coord : coord + 1, half * HALF : (half + 1) * HALF] = places[pos_id][
                    pl.ds(base + 2 * coord + half, 1), :
                ]
    for index, pair in enumerate(pairs):
        slot, row, col, own_row, own_col = pair(parity)
        target = 2 * own_row + own_col
        table[index, 0] = slot
        table[index, 1] = target
        table[index, 2] = row - own_row
        table[index, 3] = col - own_col
        table[index, 4] = flags[target, 3 * (row - own_row + 1) + col - own_col + 1]
    if first:
        for leaf in range(4):
            acc[leaf] = 0.5 * losses[0][leaf]
    else:
        acc[...] = before[...]

    @pl.loop(0, len(pairs))
    def _(index):
        @pl.when(table[index, 4] > 0)
        def _():
            slot = table[index, 0]
            target = table[index, 1]
            src_row = spos[slot, 0:1, :] + table[index, 2].astype(f32) * UNIT
            src_col = spos[slot, 1:2, :] + table[index, 3].astype(f32) * UNIT
            right = stack[slot]
            for half in range(2):
                part = pl.ds(half * HALF, HALF)
                d_row = tpos[target, part, 0:1] - src_row
                d_col = tpos[target, part, 1:2] - src_col
                square = d_row * d_row + d_col * d_col
                dist = square * lax.rsqrt(jnp.maximum(square, 1e-30))
                decay = jnp.exp2(-dist)
                kern = decay + decay * (dist * LN2)
                hi, lo = split(kern)
                acc[target, part, :] += mm(jnp.concatenate([hi, lo, hi], 1), right)


def near(flags, tpos, places, losses, slots, pairs, before=None):
    first = before is None
    operands = [flags, tpos]
    specs = [pl.BlockSpec(memory_space=SMEM), vmem_spec()]
    for array, block, index in list(places) + list(losses):
        operands.append(array)
        specs.append(vmem_spec(block, index))
    aliases = {}
    if not first:
        aliases = {len(operands): 0}
        operands.append(before)
        specs.append(vmem_spec())
    n_slots = len(slots)
    return pl.pallas_call(
        functools.partial(near_kernel, len(losses), len(places), None, slots, pairs, first),
        grid=(1,),
        in_specs=specs,
        out_specs=pl.BlockSpec((4, PTS, COLS), lambda *_: (0, 0, 0)),
        out_shape=jax.ShapeDtypeStruct((4, PTS, COLS), f32),
        scratch_shapes=[
            SMEM((len(pairs), 8), jnp.int32),
            VMEM((n_slots, 8, PTS), f32),
            VMEM((n_slots, 3 * PTS, COLS), bf16),
        ],
        input_output_aliases=aliases,
        compiler_params=params(48),
        cost_estimate=pl.CostEstimate(
            flops=len(pairs) * 900_000_000,
            bytes_accessed=4_000_000,
            transcendentals=len(pairs) * 2 * PTS * PTS,
        ),
        name="near",
    )(*operands)


def leaf_far_kernel(flags, weights, own, left, right, y_mid, c_mid, y_ends, c_ends, out):
    parity = lax.rem(lax.axis_index("lat"), 2)
    y_base = 4 * parity
    c_base = 4 - 4 * parity
    total = jnp.zeros((4 * RANK, COLS), f32)
    bands = (
        (2, ((left, 0), (own, 0), (right, 0))),
        (y_base, ((y_ends, 0), (y_mid, 0), (y_ends, 4 * RANK))),
        (c_base, ((c_ends, 0), (c_mid, 0), (c_ends, 4 * RANK))),
    )
    for base, cells in bands:
        for v in range(6):
            ref, offset = cells[v // 2]
            for a in range(2):
                start = offset + (2 * a + v % 2) * RANK
                hi, lo = split(ref[start : start + RANK, :])
                u = base + a
                w = 6 * u + v
                rows = []
                for leaf in range(4):
                    block = weights[leaf, w]
                    d_row = u - 2 - leaf // 2
                    d_col = v - 2 - leaf % 2
                    if abs(d_col) <= 1:
                        inside = (d_row >= -1) & (d_row <= 1)
                        flag = flags[leaf, 3 * jnp.clip(d_row + 1, 0, 2) + d_col + 1]
                        keep = 1 - jnp.where(inside, flag, 0)
                        block = (block.astype(f32) * keep.astype(f32)).astype(bf16)
                    rows.append(block)
                stacked = jnp.concatenate(rows, 0)
                total = total + mm(stacked, hi) + mm(stacked, lo)
    out[...] = total


def leaf_far(flags, weights, own, left, right, from_y, from_c, y_ends, c_ends):
    quad = (4 * RANK, COLS)
    return pl.pallas_call(
        leaf_far_kernel,
        grid=(1,),
        in_specs=[
            pl.BlockSpec(memory_space=SMEM),
            vmem_spec(),
            vmem_spec(quad, (0, 0)),
            vmem_spec(quad, (0, 0)),
            vmem_spec(quad, (0, 0)),
            vmem_spec(quad, (4, 0)),
            vmem_spec(quad, (4, 0)),
            vmem_spec((8 * RANK, COLS), (2, 0)),
            vmem_spec((8 * RANK, COLS), (0, 0)),
        ],
        out_specs=pl.BlockSpec(quad, lambda *_: (0, 0)),
        out_shape=jax.ShapeDtypeStruct(quad, f32),
        compiler_params=params(32),
        cost_estimate=pl.CostEstimate(
            flops=4_000_000_000, bytes_accessed=5_000_000, transcendentals=0
        ),
        name="leaf_far",
    )(flags, weights, own, left, right, from_y, from_c, y_ends, c_ends)


def down_kernel(
    n_lat, n_lon, where, every, dev_w, dev_t, group_w, far, leaf_t, basis, before, acc
):
    lat = where[0]
    lon = where[1]
    group_row = lat // 2
    group_col = lon // 2
    n_gcol = n_lon // 2
    total = jnp.zeros((RANK, COLS), f32)
    for other in range(n_lat):
        u = other + 2 - 2 * group_row
        for v in range(6):
            shift = 2 * group_col - 2 + v
            col = lax.rem(shift + n_lon, n_lon)
            drop = (jnp.abs(other - lat) <= 1) & (jnp.abs(shift - lon) <= 1)
            scale = jnp.where(drop, 0.0, 1.0)
            total = total + scale * mm2(dev_w[6 * u + v], every[other * n_lon + col])

    def group_step(step, field):
        gcol = lax.rem(group_col + step, n_gcol)
        for grow in range(n_lat // 2):
            coef = jnp.zeros((RANK, COLS), f32)
            for e in range(2):
                for f in range(2):
                    cell = (2 * grow + e) * n_lon + 2 * gcol + f
                    coef = coef + mm3(dev_t[cell], every[cell], (0, 0))
            field = field + mm2(group_w[0, 0, grow, gcol], coef)
        return field

    field = lax.fori_loop(2, n_gcol - 1, group_step, jnp.zeros((RANK, COLS), f32))
    total = total + mm3(dev_t[lat * n_lon + lon], field)
    for leaf in range(4):
        local_field = far[leaf * RANK : (leaf + 1) * RANK, :] + mm3(leaf_t[leaf], total)
        acc[leaf] = before[leaf] + mm3(basis[leaf], local_field)


def down(n_lat, n_lon, where, every, dev_w, dev_t, group_w, far, leaf_t, basis, before):
    n_grow, n_gcol = n_lat // 2, n_lon // 2
    return pl.pallas_call(
        functools.partial(down_kernel, n_lat, n_lon),
        grid_spec=pltpu.PrefetchScalarGridSpec(
            num_scalar_prefetch=1,
            grid=(1,),
            in_specs=[
                vmem_spec(),
                vmem_spec(),
                vmem_spec(),
                pl.BlockSpec(
                    (1, 1, n_grow, n_gcol, RANK, RANK),
                    lambda i, where: (where[0] // 2, where[1] // 2, 0, 0, 0, 0),
                ),
                vmem_spec(),
                vmem_spec(),
                vmem_spec(),
                vmem_spec(),
            ],
            out_specs=pl.BlockSpec((4, PTS, COLS), lambda *_: (0, 0, 0)),
        ),
        out_shape=jax.ShapeDtypeStruct((4, PTS, COLS), f32),
        input_output_aliases={8: 0},
        compiler_params=params(48),
        cost_estimate=pl.CostEstimate(
            flops=2_000_000_000, bytes_accessed=9_000_000, transcendentals=0
        ),
        name="down",
    )(where, every, dev_w, dev_t, group_w, far, leaf_t, basis, before)


def local(
    losses,
    positions,
    leaf_basis,
    near_flags,
    leaf_coupling,
    leaf_transfer,
    device_coupling,
    device_transfer,
    group_coupling,
):
    n_lat = lax.axis_size("lat")
    n_lon = lax.axis_size("lon")
    lat = lax.axis_index("lat")
    lon = lax.axis_index("lon")
    parity = lat % 2

    flat = losses.reshape(4, PTS, COLS)
    basis = leaf_basis.reshape(4, PTS, RANK)
    flags = near_flags.reshape(4, 9)
    weights = leaf_coupling.reshape(4, 36, RANK, RANK)
    transfer = leaf_transfer.reshape(4, RANK, RANK)

    to_right = [(i, (i + 1) % n_lon) for i in range(n_lon)]
    to_left = [(i, (i - 1) % n_lon) for i in range(n_lon)]
    in_chip = [(i, i ^ 1) for i in range(n_lat)]
    across = [(i, i + 1 if i % 2 else i - 1) for i in range(n_lat)]
    across = [(a, b) for a, b in across if 0 <= b < n_lat]

    def leaf_of(row, col):
        return lax.dynamic_index_in_dim(flat, 2 * row + col, 0, keepdims=False)

    y_left = lax.ppermute(leaf_of(parity, 1), "lon", to_right)
    y_right = lax.ppermute(leaf_of(parity, 0), "lon", to_left)

    msg, tpos, dev, to_y, to_c = coefficients(
        flat, basis, transfer, positions.reshape(4, 2, PTS)
    )
    every = lax.all_gather(dev, ("lat", "lon"), axis=0)
    every = every.reshape(n_lat * n_lon, RANK, COLS)
    from_y = lax.ppermute(to_y, "lat", across)
    from_c = lax.ppermute(to_c, "lat", in_chip)
    msg_left = lax.ppermute(msg, "lon", to_right)
    msg_right = lax.ppermute(msg, "lon", to_left)
    c_left = lax.ppermute(leaf_of(1 - parity, 1), "lon", to_right)
    c_right = lax.ppermute(leaf_of(1 - parity, 0), "lon", to_left)

    whole = (4 * RANK + 16, COLS)
    own_place = (msg, (16, COLS), (16, 0))

    def pos_of(leaf):
        return lambda parity: 4 * leaf

    def y_row(col):
        return lambda parity: 8 * parity + 4 * col

    def c_row(col):
        return lambda parity: 8 - 8 * parity + 4 * col

    slots = [(0, leaf, 0, pos_of(leaf)) for leaf in range(4)]
    pairs = [
        lambda parity, s=s, t=t: (s, s // 2, s % 2, t // 2, t % 2)
        for s in range(4)
        for t in range(4)
    ]
    acc = near(flags, tpos, [own_place], [(flat, (4, PTS, COLS), (0, 0, 0))], slots, pairs)

    def y_side(parity):
        return 3 * parity - 1

    def c_side(parity):
        return 2 - 3 * parity

    top = slice(0, PTS)
    bottom = slice(PTS, 2 * PTS)
    y_mirror = [lambda parity, c=c: 8 - 8 * parity + 0 * parity + 4 * c for c in range(2)]
    slots = []
    pairs = []
    for ref_id in range(2):
        for col in range(2):
            place = (lambda parity, c=col: 8 - 8 * parity + 4 * c) if ref_id == 0 else (
                lambda parity, c=col: 8 * parity + 4 * c
            )
            slots.append((ref_id, top if col == 0 else bottom, ref_id, place))
            for own_col in range(2):
                if ref_id == 0:
                    pairs.append(
                        lambda parity, s=col, t=own_col: (s, y_side(parity), s, parity, t)
                    )
                else:
                    pairs.append(
                        lambda parity, s=col, t=own_col: (2 + s, c_side(parity), s, 1 - parity, t)
                    )
    side = (2 * PTS, COLS)
    acc = near(
        flags,
        tpos,
        [(from_y, (16, COLS), (80, 0)), (from_c, (16, COLS), (80, 0))],
        [(from_y, side, (0, 0)), (from_c, side, (0, 0))],
        slots,
        pairs,
        acc,
    )

    left_place = (msg_left, (16, COLS), (16, 0))
    right_place = (msg_right, (16, COLS), (16, 0))
    one = (PTS, COLS)

    def edge_pairs(row):
        return [
            lambda parity, s=s, i=i: (s, row(parity), 3 * s - 1, i, s)
            for s in range(2)
            for i in range(2)
        ]

    to_y_ends = jnp.concatenate(
        [y_left, y_right, msg_left[: 4 * RANK], msg_right[: 4 * RANK],
         msg_left[4 * RANK :], msg_right[4 * RANK :]], 0
    )
    to_c_ends = jnp.concatenate(
        [msg_left[: 4 * RANK], msg_right[: 4 * RANK], msg_left[4 * RANK :], msg_right[4 * RANK :]],
        0,
    )
    y_ends = lax.ppermute(to_y_ends, "lat", across)
    c_ends = lax.ppermute(to_c_ends, "lat", in_chip)
    acc = near(
        flags,
        tpos,
        [left_place, right_place],
        [(y_left, one, (0, 0)), (y_right, one, (0, 0))],
        [(0, slice(None), 0, y_row(1)), (1, slice(None), 1, y_row(0))],
        edge_pairs(lambda parity: parity),
        acc,
    )
    far = leaf_far(flags, weights, msg, msg_left, msg_right, from_y, from_c, y_ends, c_ends)
    where = jnp.stack([lat, lon]).astype(jnp.int32)
    acc = near(
        flags,
        tpos,
        [(y_ends, (32, COLS), (48, 0))],
        [(y_ends, (2 * PTS, COLS), (0, 0))],
        [
            (0, top, 0, lambda parity: 8 - 8 * parity + 4),
            (0, bottom, 0, lambda parity: 16 + 8 - 8 * parity),
        ],
        [lambda parity, s=s: (s, y_side(parity), 3 * s - 1, parity, s) for s in range(2)],
        acc,
    )
    acc = down(
        n_lat,
        n_lon,
        where,
        every,
        device_coupling.reshape(36, RANK, RANK),
        device_transfer.reshape(n_lat * n_lon, RANK, RANK),
        group_coupling,
        far,
        transfer,
        basis,
        acc,
    )

    c_left_end = lax.ppermute(c_left, "lat", in_chip)
    c_right_end = lax.ppermute(c_right, "lat", in_chip)
    acc = near(
        flags,
        tpos,
        [left_place, right_place],
        [(c_left, one, (0, 0)), (c_right, one, (0, 0))],
        [(0, slice(None), 0, c_row(1)), (1, slice(None), 1, c_row(0))],
        edge_pairs(lambda parity: 1 - parity),
        acc,
    )
    acc = near(
        flags,
        tpos,
        [(c_ends, (32, COLS), (16, 0))],
        [(c_left_end, one, (0, 0)), (c_right_end, one, (0, 0))],
        [
            (0, slice(None), 0, lambda parity: 8 * parity + 4),
            (1, slice(None), 0, lambda parity: 16 + 8 * parity),
        ],
        [lambda parity, s=s: (s, c_side(parity), 3 * s - 1, 1 - parity, s) for s in range(2)],
        acc,
    )
    return acc.reshape(2, 2, PTS, COLS)


def solution(mesh):
    placed = (
        P("lat", "lon", None, None),
        P("lat", "lon", None, None),
        P("lat", "lon", None, None),
        P("lat", "lon", None),
        P("lat", "lon", None, None, None),
        P("lat", "lon", None, None),
        P("lat", "lon", None, None, None),
        P(),
        P(),
    )
    return jax.shard_map(
        local, mesh=mesh, in_specs=placed, out_specs=P("lat", "lon", None, None), check_vma=False
    )
```

```python
import functools

import jax
import jax.numpy as jnp
from jax import lax
from jax.experimental import pallas as pl
from jax.experimental.pallas import tpu as pltpu
from jax.sharding import PartitionSpec as P

PTS = 512
RANK = 64
COLS = 256
HALF = 256
QUAD = 4 * RANK
MSG = QUAD + 16

LN2 = 0.6931471805599453
UNIT = 1.7320508075688772 / 0.15 / LN2

f32 = jnp.float32
bf16 = jnp.bfloat16
VMEM = pltpu.VMEM
SMEM = pltpu.SMEM
whole = pl.BlockSpec(memory_space=VMEM)
scalars = pl.BlockSpec(memory_space=SMEM)


def split(x):
    hi = x.astype(bf16)
    return hi, (x - hi.astype(f32)).astype(bf16)


def mm(a, b, dims=(1, 0)):
    return lax.dot_general(
        a, b, (((dims[0],), (dims[1],)), ((), ())), preferred_element_type=f32
    )


def mm3(a, b, dims=(1, 0)):
    a_hi, a_lo = split(a)
    b_hi, b_lo = split(b)
    return mm(a_hi, b_hi, dims) + (mm(a_lo, b_hi, dims) + mm(a_hi, b_lo, dims))


def mm2(a, b):
    b_hi, b_lo = split(b)
    return mm(a, b_hi) + mm(a, b_lo)


def params(limit=24):
    return pltpu.CompilerParams(vmem_limit_bytes=limit * 1024 * 1024)


def shape(*dims):
    return jax.ShapeDtypeStruct(dims, f32)


def lat_parity():
    return lax.rem(lax.axis_index("lat"), 2)


def coef_kernel(loss, basis, transfer, pos, a_right, a_left, b_right, b_left, to_y, to_c, tpos, dev):
    parity = lat_parity()
    total = None
    for leaf in range(4):
        row, col = leaf // 2, leaf % 2
        values = loss[leaf]
        l_hi, l_lo = split(values)
        b_hi, b_lo = split(basis[leaf])
        coef = mm(b_hi, l_hi) + (mm(b_lo, l_hi) + mm(b_hi, l_lo))
        place = pos[leaf] * UNIT
        tpos[leaf] = jnp.concatenate([place, jnp.zeros((6, PTS), f32)], 0).T
        for ref, base in ((a_right, PTS), (a_left, PTS), (to_y, 2 * PTS), (to_c, 2 * PTS)):
            ref[base + leaf * RANK : base + (leaf + 1) * RANK, :] = coef
            for coord in range(2):
                for half in range(2):
                    at = base + QUAD + 4 * leaf + 2 * coord + half
                    ref[at : at + 1, :] = place[
                        coord : coord + 1, half * HALF : (half + 1) * HALF
                    ]
        part = mm3(transfer[leaf], coef, (0, 0))
        total = part if leaf == 0 else total + part

        @pl.when(parity == row)
        def _():
            (a_right if col else a_left)[:PTS, :] = values
            to_y[col * PTS : (col + 1) * PTS, :] = values

        @pl.when(parity != row)
        def _():
            (b_right if col else b_left)[...] = values
            to_c[col * PTS : (col + 1) * PTS, :] = values

    dev[...] = total


def coefficients(losses, basis, transfer, positions):
    return pl.pallas_call(
        coef_kernel,
        in_specs=[whole] * 4,
        out_specs=[whole] * 8,
        out_shape=[
            shape(PTS + MSG, COLS),
            shape(PTS + MSG, COLS),
            shape(PTS, COLS),
            shape(PTS, COLS),
            shape(2 * PTS + MSG, COLS),
            shape(2 * PTS + MSG, COLS),
            shape(4, PTS, 8),
            shape(RANK, COLS),
        ],
        compiler_params=params(16),
        cost_estimate=pl.CostEstimate(
            flops=1_000_000_000, bytes_accessed=6_000_000, transcendentals=0
        ),
        name="coefs",
    )(losses, basis, transfer, positions)


def near_scratch(n_slots, n_pairs):
    return [
        SMEM((n_pairs + 1, 8), jnp.int32),
        VMEM((n_slots, 8, PTS), f32),
        VMEM((n_slots, 2 * PTS, COLS), bf16),
        VMEM((PTS, 2 * PTS), bf16),
        VMEM((PTS, 2 * PTS), bf16),
    ]


def near_blocks(flags, tpos, slots, pairs, acc, scratch):
    table, spos, stack, kern_a, kern_b = scratch
    for slot, (values, places, base) in enumerate(slots):
        hi, lo = split(values)
        stack[slot, :PTS, :] = hi
        stack[slot, PTS:, :] = lo
        for coord in range(2):
            for half in range(2):
                spos[slot, coord : coord + 1, half * HALF : (half + 1) * HALF] = places[
                    pl.ds(base + 2 * coord + half, 1), :
                ]
    count = 0
    for slot, row, col, own_row, own_col in pairs:
        target = 2 * own_row + own_col
        table[count, 0] = slot
        table[count, 1] = target
        table[count, 2] = row - own_row
        table[count, 3] = col - own_col
        flag = flags[target, 3 * (row - own_row + 1) + col - own_col + 1]
        count = count + jnp.where(flag > 0, 1, 0)

    def evaluate(index, half, kern):
        slot, target = table[index, 0], table[index, 1]
        src_row = spos[slot, 0:1, :] + table[index, 2].astype(f32) * UNIT
        src_col = spos[slot, 1:2, :] + table[index, 3].astype(f32) * UNIT
        part = slice(half * HALF, (half + 1) * HALF)
        d_row = tpos[target, part, 0:1] - src_row
        d_col = tpos[target, part, 1:2] - src_col
        square = d_row * d_row + d_col * d_col
        dist = square * lax.rsqrt(jnp.maximum(square, 1e-30))
        decay = jnp.exp2(-dist)
        hi, lo = split(decay + decay * (dist * LN2))
        kern[part, :PTS] = hi
        kern[part, PTS:] = lo

    def apply(index, half, kern):
        slot, target = table[index, 0], table[index, 1]
        part = slice(half * HALF, (half + 1) * HALF)
        l_hi = stack[slot, :PTS, :]
        l_lo = stack[slot, PTS:, :]
        k_hi = kern[part, :PTS]
        k_lo = kern[part, PTS:]
        acc[target, part, :] += mm(k_hi, l_hi) + mm(k_lo, l_hi) + mm(k_hi, l_lo)

    def step(index, kern, other):
        following = jnp.minimum(index + 1, count - 1)
        for half in range(2):
            evaluate(following, half, other)
            apply(index, half, kern)

    @pl.when(count > 0)
    def _():
        for half in range(2):
            evaluate(0, half, kern_a)

    @pl.loop(0, (count + 1) // 2)
    def _(pair):
        step(2 * pair, kern_a, kern_b)

        @pl.when(2 * pair + 1 < count)
        def _():
            step(2 * pair + 1, kern_b, kern_a)


def near_cost(n_pairs):
    return pl.CostEstimate(
        flops=n_pairs * 500_000_000,
        bytes_accessed=4_000_000,
        transcendentals=n_pairs * 2 * PTS * PTS,
    )


ACC = shape(4, PTS, COLS)


def own_kernel(flags, tpos, loss, msg, acc, *scratch):
    slots = [(loss[leaf], msg, PTS + QUAD + 4 * leaf) for leaf in range(4)]
    pairs = [(s, s // 2, s % 2, t // 2, t % 2) for s in range(4) for t in range(4)]
    for leaf in range(4):
        acc[leaf] = 0.5 * loss[leaf]
    near_blocks(flags, tpos, slots, pairs, acc, scratch)


def lat_kernel(flags, tpos, from_y, from_c, before, acc, *scratch):
    acc[...] = before[...]
    parity = lat_parity()
    base = 2 * PTS + QUAD
    slots, pairs = [], []
    for ref, place, row, own_row in (
        (from_y, 8 - 8 * parity, 3 * parity - 1, parity),
        (from_c, 8 * parity, 2 - 3 * parity, 1 - parity),
    ):
        for col in range(2):
            for own_col in range(2):
                pairs.append((len(slots), row, col, own_row, own_col))
            slots.append((ref[col * PTS : (col + 1) * PTS, :], ref, base + place + 4 * col))
    near_blocks(flags, tpos, slots, pairs, acc, scratch)


def lon_kernel(flags, tpos, left, right, before, acc, to_c, *scratch):
    acc[...] = before[...]
    parity = lat_parity()
    to_c[:QUAD, :] = left[PTS : PTS + QUAD, :]
    to_c[QUAD : 2 * QUAD, :] = right[PTS : PTS + QUAD, :]
    to_c[2 * QUAD : 2 * QUAD + 16, :] = left[PTS + QUAD :, :]
    to_c[2 * QUAD + 16 :, :] = right[PTS + QUAD :, :]
    base = PTS + QUAD + 8 * parity
    slots = [(left[:PTS, :], left, base + 4), (right[:PTS, :], right, base)]
    pairs = [(s, parity, 3 * s - 1, i, s) for s in range(2) for i in range(2)]
    near_blocks(flags, tpos, slots, pairs, acc, scratch)


def last_kernel(flags, tpos, a_left, a_right, left, right, c_ends, left_c, right_c, before, acc, *scratch):
    acc[...] = before[...]
    parity = lat_parity()
    base = PTS + QUAD + 8 - 8 * parity
    ends = 2 * QUAD + 8 * parity
    slots = [
        (left[...], a_left, base + 4),
        (right[...], a_right, base),
        (left_c[...], c_ends, ends + 4),
        (right_c[...], c_ends, ends + 16),
    ]
    pairs = [(s, 1 - parity, 3 * s - 1, i, s) for s in range(2) for i in range(2)]
    pairs += [(2 + s, 2 - 3 * parity, 3 * s - 1, 1 - parity, s) for s in range(2)]
    near_blocks(flags, tpos, slots, pairs, acc, scratch)


def near(kernel, name, n_slots, n_pairs, operands, more=(), chained=True):
    return pl.pallas_call(
        kernel,
        in_specs=[scalars] + [whole] * (len(operands) - 1),
        out_specs=[whole] * (1 + len(more)),
        out_shape=[ACC, *more],
        scratch_shapes=near_scratch(n_slots, n_pairs),
        input_output_aliases={len(operands) - 1: 0} if chained else {},
        compiler_params=params(),
        cost_estimate=near_cost(n_pairs),
        name=name,
    )(*operands)


def window_sum(flags, weights, bands):
    total = None
    for base, cells in bands:
        for v in range(6):
            if cells[v // 2] is None:
                continue
            ref, offset = cells[v // 2]
            for a in range(2):
                start = offset + (2 * a + v % 2) * RANK
                hi, lo = split(ref[start : start + RANK, :])
                u = base + a
                w = 6 * u + v
                rows = []
                for leaf in range(4):
                    block = weights[leaf, w]
                    d_row = u - 2 - leaf // 2
                    d_col = v - 2 - leaf % 2
                    if abs(d_col) <= 1:
                        inside = (d_row >= -1) & (d_row <= 1)
                        flag = flags[leaf, 3 * jnp.clip(d_row + 1, 0, 2) + d_col + 1]
                        keep = 1 - jnp.where(inside, flag, 0)
                        block = (block.astype(f32) * keep.astype(f32)).astype(bf16)
                    rows.append(block)
                stacked = jnp.concatenate(rows, 0)
                part = mm(stacked, hi) + mm(stacked, lo)
                total = part if total is None else total + part
    return total


def far_kernel(
    n_lat, n_lon, flags, weights, own, left, right, from_y, from_c, every, dev_w, dev_t, group_w,
    leaf_t, out, group_row_w,
):
    lat = lax.axis_index("lat")
    lon = lax.axis_index("lon")
    parity = lax.rem(lat, 2)
    group_row, group_col = lat // 2, lon // 2
    n_gcol = n_lon // 2
    pltpu.sync_copy(group_w.at[group_row, group_col], group_row_w)
    total = jnp.zeros((RANK, COLS), f32)
    for other in range(n_lat):
        u = other + 2 - 2 * group_row
        for v in range(6):
            shift = 2 * group_col - 2 + v
            col = lax.rem(shift + n_lon, n_lon)
            drop = (jnp.abs(other - lat) <= 1) & (jnp.abs(shift - lon) <= 1)
            scale = jnp.where(drop, 0.0, 1.0)
            total = total + scale * mm2(dev_w[6 * u + v], every[other * n_lon + col])

    def group_step(step, field):
        gcol = lax.rem(group_col + step, n_gcol)
        for grow in range(n_lat // 2):
            coef = jnp.zeros((RANK, COLS), f32)
            for e in range(2):
                for f in range(2):
                    cell = (2 * grow + e) * n_lon + 2 * gcol + f
                    coef = coef + mm3(dev_t[cell], every[cell], (0, 0))
            field = field + mm2(group_row_w[grow, gcol], coef)
        return field

    field = lax.fori_loop(2, n_gcol - 1, group_step, jnp.zeros((RANK, COLS), f32))
    total = total + mm3(dev_t[lat * n_lon + lon], field)
    far = window_sum(
        flags,
        weights,
        (
            (2, ((left, PTS), (own, PTS), (right, PTS))),
            (4 * parity, (None, (from_y, 2 * PTS), None)),
            (4 - 4 * parity, (None, (from_c, 2 * PTS), None)),
        ),
    )
    for leaf in range(4):
        rows = slice(leaf * RANK, (leaf + 1) * RANK)
        out[rows, :] = far[rows, :] + mm3(leaf_t[leaf], total)


def far_field(n_lat, n_lon, operands):
    specs = [scalars] + [whole] * 11
    specs[10] = pl.BlockSpec(memory_space=pl.ANY)
    return pl.pallas_call(
        functools.partial(far_kernel, n_lat, n_lon),
        in_specs=specs,
        out_specs=whole,
        out_shape=shape(QUAD, COLS),
        scratch_shapes=[VMEM((n_lat // 2, n_lon // 2, RANK, RANK), bf16)],
        compiler_params=params(),
        cost_estimate=pl.CostEstimate(
            flops=6_000_000_000, bytes_accessed=9_000_000, transcendentals=0
        ),
        name="far",
    )(*operands)


def down_kernel(
    flags, tpos, weights, left_y, right_y, c_ends, partial, basis, before, acc, *scratch
):
    acc[...] = before[...]
    parity = lat_parity()
    far = partial[...] + window_sum(
        flags,
        weights,
        (
            (4 * parity, ((left_y, PTS), None, (right_y, PTS))),
            (4 - 4 * parity, ((c_ends, 0), None, (c_ends, QUAD))),
        ),
    )
    for leaf in range(4):
        acc[leaf] += mm3(basis[leaf], far[leaf * RANK : (leaf + 1) * RANK, :], (0, 0))
    base = PTS + QUAD + 8 - 8 * parity
    slots = [(left_y[:PTS, :], left_y, base + 4), (right_y[:PTS, :], right_y, base)]
    pairs = [(s, 3 * parity - 1, 3 * s - 1, parity, s) for s in range(2)]
    near_blocks(flags, tpos, slots, pairs, acc, scratch)


def local(
    losses,
    positions,
    leaf_basis,
    near_flags,
    leaf_coupling,
    leaf_transfer,
    device_coupling,
    device_transfer,
    group_coupling,
):
    n_lat = lax.axis_size("lat")
    n_lon = lax.axis_size("lon")

    flat = losses.reshape(4, PTS, COLS)
    basis = jnp.swapaxes(leaf_basis, 2, 3).reshape(4, RANK, PTS)
    flags = near_flags.reshape(4, 9)
    weights = leaf_coupling.reshape(4, 36, RANK, RANK)
    transfer = leaf_transfer.reshape(4, RANK, RANK)

    to_right = [(i, (i + 1) % n_lon) for i in range(n_lon)]
    to_left = [(i, (i - 1) % n_lon) for i in range(n_lon)]
    in_chip = [(i, i ^ 1) for i in range(n_lat)]
    across = [(i, i + 1 if i % 2 else i - 1) for i in range(n_lat)]
    across = [(a, b) for a, b in across if 0 <= b < n_lat]

    a_right, a_left, b_right, b_left, to_y, to_c, tpos, dev = coefficients(
        flat, basis, transfer, positions.reshape(4, 2, PTS)
    )
    left = lax.ppermute(a_right, "lon", to_right)
    right = lax.ppermute(a_left, "lon", to_left)
    from_c = lax.ppermute(to_c, "lat", in_chip)
    left_b = lax.ppermute(b_right, "lon", to_right)
    right_b = lax.ppermute(b_left, "lon", to_left)
    from_y = lax.ppermute(to_y, "lat", across)

    pairs = [[2 * k, 2 * k + 1] for k in range(n_lon // 2)]
    classes = [list(range(j, n_lon, 2)) for j in range(2)]
    every = lax.all_gather(dev, "lon", axis_index_groups=pairs)
    every = lax.all_gather(every, "lon", axis_index_groups=classes)
    every = lax.all_gather(every, "lat")
    every = every.reshape(n_lat * n_lon, RANK, COLS)

    (acc,) = near(own_kernel, "own", 4, 16, (flags, tpos, flat, a_right), chained=False)
    (acc,) = near(lat_kernel, "lat", 4, 8, (flags, tpos, from_y, from_c, acc))
    left, right, acc = lax.optimization_barrier((left, right, acc))
    left_y = lax.ppermute(left, "lat", across)
    right_y = lax.ppermute(right, "lat", across)
    acc, to_c = near(
        lon_kernel, "lon", 2, 4, (flags, tpos, left, right, acc), more=[shape(2 * MSG, COLS)]
    )
    c_ends = lax.ppermute(to_c, "lat", in_chip)
    partial = far_field(
        n_lat,
        n_lon,
        (
            flags,
            weights,
            a_right,
            left,
            right,
            from_y,
            from_c,
            every,
            device_coupling.reshape(36, RANK, RANK),
            device_transfer.reshape(n_lat * n_lon, RANK, RANK),
            group_coupling,
            transfer,
        ),
    )
    left_c = lax.ppermute(left_b, "lat", in_chip)
    right_c = lax.ppermute(right_b, "lat", in_chip)
    (acc,) = near(
        down_kernel,
        "down",
        2,
        2,
        (flags, tpos, weights, left_y, right_y, c_ends, partial, basis, acc),
    )
    (acc,) = near(
        last_kernel,
        "last",
        4,
        6,
        (flags, tpos, left, right, left_b, right_b, c_ends, left_c, right_c, acc),
    )
    return acc.reshape(2, 2, PTS, COLS)


def solution(mesh):
    placed = (
        P("lat", "lon", None, None),
        P("lat", "lon", None, None),
        P("lat", "lon", None, None),
        P("lat", "lon", None),
        P("lat", "lon", None, None, None),
        P("lat", "lon", None, None),
        P("lat", "lon", None, None, None),
        P(),
        P(),
    )
    return jax.shard_map(
        local, mesh=mesh, in_specs=placed, out_specs=P("lat", "lon", None, None), check_vma=False
    )
```

```python
import functools

import jax
import jax.numpy as jnp
from jax import lax
from jax.experimental import pallas as pl
from jax.experimental.pallas import tpu as pltpu
from jax.sharding import PartitionSpec as P

PTS = 512
RANK = 64
COLS = 256
HALF = 256
QUAD = 4 * RANK
MSG = QUAD + 16

LN2 = 0.6931471805599453
UNIT = 1.7320508075688772 / 0.15 / LN2

f32 = jnp.float32
bf16 = jnp.bfloat16
VMEM = pltpu.VMEM
SMEM = pltpu.SMEM
whole = pl.BlockSpec(memory_space=VMEM)
scalars = pl.BlockSpec(memory_space=SMEM)


def split(x):
    hi = x.astype(bf16)
    return hi, (x - hi.astype(f32)).astype(bf16)


def mm(a, b, dims=(1, 0)):
    return lax.dot_general(
        a, b, (((dims[0],), (dims[1],)), ((), ())), preferred_element_type=f32
    )


def mm3(a, b, dims=(1, 0)):
    a_hi, a_lo = split(a)
    b_hi, b_lo = split(b)
    return mm(a_hi, b_hi, dims) + (mm(a_lo, b_hi, dims) + mm(a_hi, b_lo, dims))


def mm2(a, b):
    b_hi, b_lo = split(b)
    return mm(a, b_hi) + mm(a, b_lo)


def params(limit=64):
    return pltpu.CompilerParams(vmem_limit_bytes=limit * 1024 * 1024)


def shape(*dims):
    return jax.ShapeDtypeStruct(dims, f32)


def lat_parity():
    return lax.rem(lax.axis_index("lat"), 2)


def coef_kernel(
    loss, basis, transfer, pos, a_right, a_left, b_right, b_left, to_y, to_c, tpos, dev,
    values, bases, message, sems, load_sems,
):
    parity = lat_parity()
    loads = []
    for leaf in range(4):
        loads.append(
            (
                pltpu.make_async_copy(loss.at[leaf], values.at[leaf], load_sems.at[leaf]),
                pltpu.make_async_copy(basis.at[leaf], bases.at[leaf], load_sems.at[4 + leaf]),
            )
        )
        for copy in loads[-1]:
            copy.start()
    y_row, c_row = 2 * parity, 2 - 2 * parity
    first, second = slice(0, PTS), slice(PTS, 2 * PTS)
    copies = []
    for source, target in (
        (y_row + 1, a_right.at[first]),
        (y_row, a_left.at[first]),
        (c_row + 1, b_right),
        (c_row, b_left),
        (y_row, to_y.at[first]),
        (y_row + 1, to_y.at[second]),
        (c_row, to_c.at[first]),
        (c_row + 1, to_c.at[second]),
    ):
        copy = pltpu.make_async_copy(loss.at[source], target, sems.at[len(copies)])
        copy.start()
        copies.append(copy)
    for leaf in range(4):
        place = pos[leaf] * UNIT
        tpos[leaf] = jnp.concatenate([place, jnp.zeros((6, PTS), f32)], 0).T
        for coord in range(2):
            for half in range(2):
                at = QUAD + 4 * leaf + 2 * coord + half
                message[at : at + 1, :] = place[coord : coord + 1, half * HALF : (half + 1) * HALF]
    total = None
    for leaf in range(4):
        for copy in loads[leaf]:
            copy.wait()
        l_hi, l_lo = split(values[leaf])
        b_hi, b_lo = split(bases[leaf])
        coef = mm(b_hi, l_hi) + (mm(b_lo, l_hi) + mm(b_hi, l_lo))
        message[leaf * RANK : (leaf + 1) * RANK, :] = coef
        part = mm3(transfer[leaf], coef, (0, 0))
        total = part if leaf == 0 else total + part
    dev[...] = total
    for target in (
        a_right.at[PTS:], a_left.at[PTS:], to_y.at[2 * PTS :], to_c.at[2 * PTS :]
    ):
        copy = pltpu.make_async_copy(message, target, sems.at[len(copies)])
        copy.start()
        copies.append(copy)
    for copy in copies:
        copy.wait()


def coefficients(losses, basis, transfer, positions):
    hbm = pl.BlockSpec(memory_space=pl.ANY)
    return pl.pallas_call(
        coef_kernel,
        in_specs=[hbm, hbm, whole, whole],
        out_specs=[hbm] * 6 + [whole] * 2,
        out_shape=[
            shape(PTS + MSG, COLS),
            shape(PTS + MSG, COLS),
            shape(PTS, COLS),
            shape(PTS, COLS),
            shape(2 * PTS + MSG, COLS),
            shape(2 * PTS + MSG, COLS),
            shape(4, PTS, 8),
            shape(RANK, COLS),
        ],
        scratch_shapes=[
            VMEM((4, PTS, COLS), f32),
            VMEM((4, RANK, PTS), f32),
            VMEM((MSG, COLS), f32),
            pltpu.SemaphoreType.DMA((12,)),
            pltpu.SemaphoreType.DMA((8,)),
        ],
        compiler_params=params(),
        cost_estimate=COST,
        name="coefs",
    )(losses, basis, transfer, positions)


def near_scratch(n_slots, n_pairs):
    return [
        SMEM((n_pairs + 1, 8), jnp.int32),
        VMEM((n_slots, 8, PTS), f32),
        VMEM((n_slots, 2 * PTS, COLS), bf16),
        VMEM((PTS, 2 * PTS), bf16),
        VMEM((PTS, 2 * PTS), bf16),
    ]


def near_blocks(flags, tpos, slots, pairs, acc, scratch):
    table, spos, stack, kern_a, kern_b = scratch
    for slot, (values, places, base) in enumerate(slots):
        hi, lo = split(values)
        stack[slot, :PTS, :] = hi
        stack[slot, PTS:, :] = lo
        for coord in range(2):
            for half in range(2):
                spos[slot, coord : coord + 1, half * HALF : (half + 1) * HALF] = places[
                    pl.ds(base + 2 * coord + half, 1), :
                ]
    count = 0
    for slot, row, col, own_row, own_col in pairs:
        target = 2 * own_row + own_col
        table[count, 0] = slot
        table[count, 1] = target
        table[count, 2] = row - own_row
        table[count, 3] = col - own_col
        flag = flags[target, 3 * (row - own_row + 1) + col - own_col + 1]
        count = count + jnp.where(flag > 0, 1, 0)

    def evaluate(index, half, kern):
        slot, target = table[index, 0], table[index, 1]
        src_row = spos[slot, 0:1, :] + table[index, 2].astype(f32) * UNIT
        src_col = spos[slot, 1:2, :] + table[index, 3].astype(f32) * UNIT
        part = slice(half * HALF, (half + 1) * HALF)
        d_row = tpos[target, part, 0:1] - src_row
        d_col = tpos[target, part, 1:2] - src_col
        square = d_row * d_row + d_col * d_col
        dist = square * lax.rsqrt(jnp.maximum(square, 1e-30))
        decay = jnp.exp2(-dist)
        hi, lo = split(decay + decay * (dist * LN2))
        kern[part, :PTS] = hi
        kern[part, PTS:] = lo

    def apply(index, half, kern):
        slot, target = table[index, 0], table[index, 1]
        part = slice(half * HALF, (half + 1) * HALF)
        l_hi = stack[slot, :PTS, :]
        l_lo = stack[slot, PTS:, :]
        k_hi = kern[part, :PTS]
        k_lo = kern[part, PTS:]
        acc[target, part, :] += mm(k_hi, l_hi) + mm(k_lo, l_hi) + mm(k_hi, l_lo)

    def step(index, kern, other):
        following = jnp.minimum(index + 1, count - 1)
        for half in range(2):
            evaluate(following, half, other)
            apply(index, half, kern)

    @pl.when(count > 0)
    def _():
        for half in range(2):
            evaluate(0, half, kern_a)

    @pl.loop(0, (count + 1) // 2)
    def _(pair):
        step(2 * pair, kern_a, kern_b)

        @pl.when(2 * pair + 1 < count)
        def _():
            step(2 * pair + 1, kern_b, kern_a)


COST = pl.CostEstimate(flops=20_000_000_000, bytes_accessed=4_000_000, transcendentals=0)


ACC = shape(4, PTS, COLS)


def own_kernel(flags, tpos, loss, msg, acc, *scratch):
    slots = [(loss[leaf], msg, PTS + QUAD + 4 * leaf) for leaf in range(4)]
    pairs = [(s, s // 2, s % 2, t // 2, t % 2) for s in range(4) for t in range(4)]
    for leaf in range(4):
        acc[leaf] = 0.5 * loss[leaf]
    near_blocks(flags, tpos, slots, pairs, acc, scratch)


def lat_kernel(is_c, flags, tpos, source, before, acc, *scratch):
    acc[...] = before[...]
    parity = lat_parity()
    base = 2 * PTS + QUAD
    if is_c:
        place, row, own_row = 8 * parity, 2 - 3 * parity, 1 - parity
    else:
        place, row, own_row = 8 - 8 * parity, 3 * parity - 1, parity
    slots = [
        (source[col * PTS : (col + 1) * PTS, :], source, base + place + 4 * col)
        for col in range(2)
    ]
    pairs = [(col, row, col, own_row, own_col) for col in range(2) for own_col in range(2)]
    near_blocks(flags, tpos, slots, pairs, acc, scratch)


def lon_kernel(flags, tpos, left, right, before, acc, to_c, *scratch):
    acc[...] = before[...]
    parity = lat_parity()
    to_c[:QUAD, :] = left[PTS : PTS + QUAD, :]
    to_c[QUAD : 2 * QUAD, :] = right[PTS : PTS + QUAD, :]
    to_c[2 * QUAD : 2 * QUAD + 16, :] = left[PTS + QUAD :, :]
    to_c[2 * QUAD + 16 :, :] = right[PTS + QUAD :, :]
    base = PTS + QUAD + 8 * parity
    slots = [(left[:PTS, :], left, base + 4), (right[:PTS, :], right, base)]
    pairs = [(s, parity, 3 * s - 1, i, s) for s in range(2) for i in range(2)]
    near_blocks(flags, tpos, slots, pairs, acc, scratch)


def last_kernel(flags, tpos, a_left, a_right, left, right, before, acc, *scratch):
    acc[...] = before[...]
    parity = lat_parity()
    base = PTS + QUAD + 8 - 8 * parity
    slots = [(left[...], a_left, base + 4), (right[...], a_right, base)]
    pairs = [(s, 1 - parity, 3 * s - 1, i, s) for s in range(2) for i in range(2)]
    near_blocks(flags, tpos, slots, pairs, acc, scratch)


def corner_kernel(flags, tpos, c_ends, left_c, right_c, before, acc, *scratch):
    acc[...] = before[...]
    parity = lat_parity()
    ends = 2 * QUAD + 8 * parity
    slots = [(left_c[...], c_ends, ends + 4), (right_c[...], c_ends, ends + 16)]
    pairs = [(s, 2 - 3 * parity, 3 * s - 1, 1 - parity, s) for s in range(2)]
    near_blocks(flags, tpos, slots, pairs, acc, scratch)


def near(kernel, name, n_slots, n_pairs, operands, more=(), chained=True):
    return pl.pallas_call(
        kernel,
        in_specs=[scalars] + [whole] * (len(operands) - 1),
        out_specs=[whole] * (1 + len(more)),
        out_shape=[ACC, *more],
        scratch_shapes=near_scratch(n_slots, n_pairs),
        input_output_aliases={len(operands) - 1: 0} if chained else {},
        compiler_params=params(),
        cost_estimate=COST,
        name=name,
    )(*operands)


def window_sum(flags, weights, bands):
    total = None
    for base, cells in bands:
        for v in range(6):
            if cells[v // 2] is None:
                continue
            ref, offset = cells[v // 2]
            for a in range(2):
                start = offset + (2 * a + v % 2) * RANK
                hi, lo = split(ref[start : start + RANK, :])
                u = base + a
                w = 6 * u + v
                rows = []
                for leaf in range(4):
                    block = weights[leaf, w]
                    d_row = u - 2 - leaf // 2
                    d_col = v - 2 - leaf % 2
                    if abs(d_col) <= 1:
                        inside = (d_row >= -1) & (d_row <= 1)
                        flag = flags[leaf, 3 * jnp.clip(d_row + 1, 0, 2) + d_col + 1]
                        keep = 1 - jnp.where(inside, flag, 0)
                        block = (block.astype(f32) * keep.astype(f32)).astype(bf16)
                    rows.append(block)
                stacked = jnp.concatenate(rows, 0)
                part = mm(stacked, hi) + mm(stacked, lo)
                total = part if total is None else total + part
    return total


def far_kernel(
    n_lat, n_lon, flags, weights, own, left, right, from_y, from_c, every, dev_w, dev_t, group_w,
    leaf_t, out, group_row_w,
):
    lat = lax.axis_index("lat")
    lon = lax.axis_index("lon")
    parity = lax.rem(lat, 2)
    group_row, group_col = lat // 2, lon // 2
    n_gcol = n_lon // 2
    pltpu.sync_copy(group_w.at[group_row, group_col], group_row_w)
    total = jnp.zeros((RANK, COLS), f32)
    for other in range(n_lat):
        u = other + 2 - 2 * group_row
        for v in range(6):
            shift = 2 * group_col - 2 + v
            col = lax.rem(shift + n_lon, n_lon)
            drop = (jnp.abs(other - lat) <= 1) & (jnp.abs(shift - lon) <= 1)
            scale = jnp.where(drop, 0.0, 1.0)
            total = total + scale * mm2(dev_w[6 * u + v], every[other * n_lon + col])

    def group_step(step, field):
        gcol = lax.rem(group_col + step, n_gcol)
        for grow in range(n_lat // 2):
            coef = jnp.zeros((RANK, COLS), f32)
            for e in range(2):
                for f in range(2):
                    cell = (2 * grow + e) * n_lon + 2 * gcol + f
                    coef = coef + mm3(dev_t[cell], every[cell], (0, 0))
            field = field + mm2(group_row_w[grow, gcol], coef)
        return field

    field = lax.fori_loop(2, n_gcol - 1, group_step, jnp.zeros((RANK, COLS), f32))
    total = total + mm3(dev_t[lat * n_lon + lon], field)
    far = window_sum(
        flags,
        weights,
        (
            (2, ((left, PTS), (own, PTS), (right, PTS))),
            (4 * parity, (None, (from_y, 2 * PTS), None)),
            (4 - 4 * parity, (None, (from_c, 2 * PTS), None)),
        ),
    )
    for leaf in range(4):
        rows = slice(leaf * RANK, (leaf + 1) * RANK)
        out[rows, :] = far[rows, :] + mm3(leaf_t[leaf], total)


def far_field(n_lat, n_lon, operands):
    specs = [scalars] + [whole] * 11
    specs[10] = pl.BlockSpec(memory_space=pl.ANY)
    return pl.pallas_call(
        functools.partial(far_kernel, n_lat, n_lon),
        in_specs=specs,
        out_specs=whole,
        out_shape=shape(QUAD, COLS),
        scratch_shapes=[VMEM((n_lat // 2, n_lon // 2, RANK, RANK), bf16)],
        compiler_params=params(),
        cost_estimate=COST,
        name="far",
    )(*operands)


def down_kernel(
    flags, tpos, weights, left_y, right_y, c_ends, partial, basis, before, acc, *scratch
):
    acc[...] = before[...]
    parity = lat_parity()
    far = partial[...] + window_sum(
        flags,
        weights,
        (
            (4 * parity, ((left_y, PTS), None, (right_y, PTS))),
            (4 - 4 * parity, ((c_ends, 0), None, (c_ends, QUAD))),
        ),
    )
    for leaf in range(4):
        acc[leaf] += mm3(basis[leaf], far[leaf * RANK : (leaf + 1) * RANK, :], (0, 0))
    base = PTS + QUAD + 8 - 8 * parity
    slots = [(left_y[:PTS, :], left_y, base + 4), (right_y[:PTS, :], right_y, base)]
    pairs = [(s, 3 * parity - 1, 3 * s - 1, parity, s) for s in range(2)]
    near_blocks(flags, tpos, slots, pairs, acc, scratch)


def local(
    losses,
    positions,
    leaf_basis,
    near_flags,
    leaf_coupling,
    leaf_transfer,
    device_coupling,
    device_transfer,
    group_coupling,
):
    n_lat = lax.axis_size("lat")
    n_lon = lax.axis_size("lon")

    flat = losses.reshape(4, PTS, COLS)
    basis = jnp.swapaxes(leaf_basis, 2, 3).reshape(4, RANK, PTS)
    flags = near_flags.reshape(4, 9)
    weights = leaf_coupling.reshape(4, 36, RANK, RANK)
    transfer = leaf_transfer.reshape(4, RANK, RANK)

    to_right = [(i, (i + 1) % n_lon) for i in range(n_lon)]
    to_left = [(i, (i - 1) % n_lon) for i in range(n_lon)]
    in_chip = [(i, i ^ 1) for i in range(n_lat)]
    across = [(i, i + 1 if i % 2 else i - 1) for i in range(n_lat)]
    across = [(a, b) for a, b in across if 0 <= b < n_lat]

    a_right, a_left, b_right, b_left, to_y, to_c, tpos, dev = coefficients(
        flat, basis, transfer, positions.reshape(4, 2, PTS)
    )
    left = lax.ppermute(a_right, "lon", to_right)
    right = lax.ppermute(a_left, "lon", to_left)
    left_b = lax.ppermute(b_right, "lon", to_right)
    right_b = lax.ppermute(b_left, "lon", to_left)
    from_y = lax.ppermute(to_y, "lat", across)

    every = lax.all_gather(dev, "lon")

    (acc,) = near(own_kernel, "own", 4, 16, (flags, tpos, flat, a_right), chained=False)
    to_c, from_y, every, acc = lax.optimization_barrier((to_c, from_y, every, acc))
    from_c = lax.ppermute(to_c, "lat", in_chip)
    every = lax.all_gather(every, "lat").reshape(n_lat * n_lon, RANK, COLS)
    (acc,) = near(
        functools.partial(lat_kernel, False), "lat_y", 2, 4, (flags, tpos, from_y, acc)
    )
    (acc,) = near(
        functools.partial(lat_kernel, True), "lat_c", 2, 4, (flags, tpos, from_c, acc)
    )
    left, right, acc = lax.optimization_barrier((left, right, acc))
    left_y = lax.ppermute(left, "lat", across)
    right_y = lax.ppermute(right, "lat", across)
    acc, to_c = near(
        lon_kernel, "lon", 2, 4, (flags, tpos, left, right, acc), more=[shape(2 * MSG, COLS)]
    )
    every, acc = lax.optimization_barrier((every, acc))
    c_ends = lax.ppermute(to_c, "lat", in_chip)
    partial = far_field(
        n_lat,
        n_lon,
        (
            flags,
            weights,
            a_right,
            left,
            right,
            from_y,
            from_c,
            every,
            device_coupling.reshape(36, RANK, RANK),
            device_transfer.reshape(n_lat * n_lon, RANK, RANK),
            group_coupling,
            transfer,
        ),
    )
    left_y, right_y, partial = lax.optimization_barrier((left_y, right_y, partial))
    (acc,) = near(
        down_kernel,
        "down",
        2,
        2,
        (flags, tpos, weights, left_y, right_y, c_ends, partial, basis, acc),
    )
    left_b, right_b, acc = lax.optimization_barrier((left_b, right_b, acc))
    left_c = lax.ppermute(left_b, "lat", in_chip)
    right_c = lax.ppermute(right_b, "lat", in_chip)
    (acc,) = near(
        last_kernel, "last", 2, 4, (flags, tpos, left, right, left_b, right_b, acc)
    )
    left_c, right_c, acc = lax.optimization_barrier((left_c, right_c, acc))
    (acc,) = near(
        corner_kernel, "corner", 2, 2, (flags, tpos, c_ends, left_c, right_c, acc)
    )
    return acc.reshape(2, 2, PTS, COLS)


def solution(mesh):
    placed = (
        P("lat", "lon", None, None),
        P("lat", "lon", None, None),
        P("lat", "lon", None, None),
        P("lat", "lon", None),
        P("lat", "lon", None, None, None),
        P("lat", "lon", None, None),
        P("lat", "lon", None, None, None),
        P(),
        P(),
    )
    return jax.shard_map(
        local, mesh=mesh, in_specs=placed, out_specs=P("lat", "lon", None, None), check_vma=False
    )
```

```python
import functools

import jax
import jax.numpy as jnp
from jax import lax
from jax.experimental import pallas as pl
from jax.experimental.pallas import tpu as pltpu
from jax.sharding import PartitionSpec as P

PTS = 512
RANK = 64
COLS = 256
HALF = 256
QUAD = 4 * RANK
MSG = QUAD + 16

LN2 = 0.6931471805599453
UNIT = 1.7320508075688772 / 0.15 / LN2

f32 = jnp.float32
bf16 = jnp.bfloat16
VMEM = pltpu.VMEM
SMEM = pltpu.SMEM
whole = pl.BlockSpec(memory_space=VMEM)
scalars = pl.BlockSpec(memory_space=SMEM)


def split(x):
    hi = x.astype(bf16)
    return hi, (x - hi.astype(f32)).astype(bf16)


def mm(a, b, dims=(1, 0)):
    return lax.dot_general(
        a, b, (((dims[0],), (dims[1],)), ((), ())), preferred_element_type=f32
    )


def mm3(a, b, dims=(1, 0)):
    a_hi, a_lo = split(a)
    b_hi, b_lo = split(b)
    return mm(a_hi, b_hi, dims) + (mm(a_lo, b_hi, dims) + mm(a_hi, b_lo, dims))


def mm2(a, b):
    b_hi, b_lo = split(b)
    return mm(a, b_hi) + mm(a, b_lo)


def params(limit=64):
    return pltpu.CompilerParams(vmem_limit_bytes=limit * 1024 * 1024)


COST = pl.CostEstimate(flops=20_000_000_000, bytes_accessed=4_000_000, transcendentals=0)
LOW = pl.CostEstimate(flops=1_000, bytes_accessed=1_000, transcendentals=0)


def shape(*dims):
    return jax.ShapeDtypeStruct(dims, f32)


def lat_parity():
    return lax.rem(lax.axis_index("lat"), 2)


def coef_kernel(
    loss, basis, transfer, pos, a_right, a_left, b_right, b_left, to_y, to_c, place8, dev,
    values, bases, message, sems, load_sems,
):
    parity = lat_parity()
    loads = [
        (
            pltpu.make_async_copy(loss.at[leaf], values.at[leaf], load_sems.at[leaf]),
            pltpu.make_async_copy(basis.at[leaf], bases.at[leaf], load_sems.at[4 + leaf]),
        )
        for leaf in range(4)
    ]
    for pair in loads:
        for copy in pair:
            copy.start()
    for leaf in range(4):
        place = pos[leaf] * UNIT
        place8[leaf] = jnp.concatenate([place, jnp.zeros((6, PTS), f32)], 0)
        for coord in range(2):
            for half in range(2):
                at = QUAD + 4 * leaf + 2 * coord + half
                message[at : at + 1, :] = place[coord : coord + 1, half * HALF : (half + 1) * HALF]
    for pair in loads:
        for copy in pair:
            copy.wait()
    y_row, c_row = 2 * parity, 2 - 2 * parity
    first, second = slice(0, PTS), slice(PTS, 2 * PTS)
    copies = []
    for source, target in (
        (y_row + 1, a_right.at[first]),
        (y_row, a_left.at[first]),
        (c_row + 1, b_right),
        (c_row, b_left),
        (y_row, to_y.at[first]),
        (y_row + 1, to_y.at[second]),
        (c_row, to_c.at[first]),
        (c_row + 1, to_c.at[second]),
    ):
        copy = pltpu.make_async_copy(values.at[source], target, sems.at[len(copies)])
        copy.start()
        copies.append(copy)
    total = None
    for leaf in range(4):
        l_hi, l_lo = split(values[leaf])
        b_hi, b_lo = split(bases[leaf])
        coef = mm(b_hi, l_hi) + (mm(b_lo, l_hi) + mm(b_hi, l_lo))
        message[leaf * RANK : (leaf + 1) * RANK, :] = coef
        part = mm3(transfer[leaf], coef, (0, 0))
        total = part if leaf == 0 else total + part
    dev[...] = total
    for target in (
        a_right.at[PTS:], a_left.at[PTS:], to_y.at[2 * PTS :], to_c.at[2 * PTS :]
    ):
        copy = pltpu.make_async_copy(message, target, sems.at[len(copies)])
        copy.start()
        copies.append(copy)
    for copy in copies:
        copy.wait()


hbm = pl.BlockSpec(memory_space=pl.ANY)


def coefficients(losses, basis, transfer, positions):
    return pl.pallas_call(
        coef_kernel,
        in_specs=[hbm, hbm, whole, whole],
        out_specs=[hbm] * 6 + [whole] * 2,
        out_shape=[
            shape(PTS + MSG, COLS),
            shape(PTS + MSG, COLS),
            shape(PTS, COLS),
            shape(PTS, COLS),
            shape(2 * PTS + MSG, COLS),
            shape(2 * PTS + MSG, COLS),
            shape(4, 8, PTS),
            shape(RANK, COLS),
        ],
        scratch_shapes=[
            VMEM((4, PTS, COLS), f32),
            VMEM((4, RANK, PTS), f32),
            VMEM((MSG, COLS), f32),
            pltpu.SemaphoreType.DMA((12,)),
            pltpu.SemaphoreType.DMA((8,)),
        ],
        compiler_params=params(),
        cost_estimate=COST,
        name="coefs",
    )(losses, basis, transfer, positions)


def near_scratch(n_slots, n_pairs):
    return [
        SMEM((n_pairs + 1, 8), jnp.int32),
        VMEM((4, PTS, 8), f32),
        VMEM((n_slots, 8, PTS), f32),
        VMEM((n_slots, 2 * PTS, COLS), bf16),
        VMEM((PTS, 2 * PTS), bf16),
        VMEM((PTS, 2 * PTS), bf16),
        VMEM((4, PTS, COLS), f32),
        pltpu.SemaphoreType.DMA((8,)),
    ]


def near_blocks(flags, place8, slots, pairs, before, out, scratch, fill=None):
    table, tpos, spos, stack, kern_a, kern_b, acc, sems = scratch
    loads = []
    if before is not None:
        loads = [
            pltpu.make_async_copy(before.at[leaf], acc.at[leaf], sems.at[leaf])
            for leaf in range(4)
        ]
    for copy in loads:
        copy.start()
    for leaf in range(4):
        tpos[leaf] = place8[leaf].T
    for slot, (values, places, base) in enumerate(slots):
        hi, lo = split(values)
        stack[slot, :PTS, :] = hi
        stack[slot, PTS:, :] = lo
        for coord in range(2):
            for half in range(2):
                spos[slot, coord : coord + 1, half * HALF : (half + 1) * HALF] = places[
                    pl.ds(base + 2 * coord + half, 1), :
                ]
    count = 0
    for slot, row, col, own_row, own_col in pairs:
        target = 2 * own_row + own_col
        table[count, 0] = slot
        table[count, 1] = target
        table[count, 2] = row - own_row
        table[count, 3] = col - own_col
        flag = flags[target, 3 * (row - own_row + 1) + col - own_col + 1]
        count = count + jnp.where(flag > 0, 1, 0)

    def evaluate(index, half, kern):
        slot, target = table[index, 0], table[index, 1]
        src_row = spos[slot, 0:1, :] + table[index, 2].astype(f32) * UNIT
        src_col = spos[slot, 1:2, :] + table[index, 3].astype(f32) * UNIT
        part = slice(half * HALF, (half + 1) * HALF)
        d_row = tpos[target, part, 0:1] - src_row
        d_col = tpos[target, part, 1:2] - src_col
        square = d_row * d_row + d_col * d_col
        dist = square * lax.rsqrt(jnp.maximum(square, 1e-30))
        decay = jnp.exp2(-dist)
        hi, lo = split(decay + decay * (dist * LN2))
        kern[part, :PTS] = hi
        kern[part, PTS:] = lo

    def apply(index, half, kern):
        slot, target = table[index, 0], table[index, 1]
        part = slice(half * HALF, (half + 1) * HALF)
        l_hi = stack[slot, :PTS, :]
        l_lo = stack[slot, PTS:, :]
        k_hi = kern[part, :PTS]
        k_lo = kern[part, PTS:]
        acc[target, part, :] += mm(k_hi, l_hi) + mm(k_lo, l_hi) + mm(k_hi, l_lo)

    def step(index, kern, other):
        following = jnp.minimum(index + 1, count - 1)
        for half in range(2):
            evaluate(following, half, other)
            apply(index, half, kern)

    @pl.when(count > 0)
    def _():
        for half in range(2):
            evaluate(0, half, kern_a)

    for copy in loads:
        copy.wait()
    if fill is not None:
        fill(acc)

    @pl.loop(0, (count + 1) // 2)
    def _(pair):
        step(2 * pair, kern_a, kern_b)

        @pl.when(2 * pair + 1 < count)
        def _():
            step(2 * pair + 1, kern_b, kern_a)


    stores = [
        pltpu.make_async_copy(acc.at[leaf], out.at[leaf], sems.at[4 + leaf]) for leaf in range(4)
    ]
    for copy in stores:
        copy.start()
    for copy in stores:
        copy.wait()


ACC = shape(4, PTS, COLS)


def own_kernel(flags, place8, loss, msg, out, *scratch):
    slots = [(loss[leaf], msg, PTS + QUAD + 4 * leaf) for leaf in range(4)]
    pairs = [(s, s // 2, s % 2, t // 2, t % 2) for s in range(4) for t in range(4)]

    def fill(acc):
        for leaf in range(4):
            acc[leaf] = 0.5 * loss[leaf]

    near_blocks(flags, place8, slots, pairs, None, out, scratch, fill)


def lat_kernel(flags, place8, from_y, from_c, before, out, *scratch):
    parity = lat_parity()
    base = 2 * PTS + QUAD
    slots, pairs = [], []
    for ref, place, row, own_row in (
        (from_y, 8 - 8 * parity, 3 * parity - 1, parity),
        (from_c, 8 * parity, 2 - 3 * parity, 1 - parity),
    ):
        for col in range(2):
            for own_col in range(2):
                pairs.append((len(slots), row, col, own_row, own_col))
            slots.append((ref[col * PTS : (col + 1) * PTS, :], ref, base + place + 4 * col))
    near_blocks(flags, place8, slots, pairs, before, out, scratch)


def lon_kernel(flags, place8, left, right, before, out, *scratch):
    parity = lat_parity()
    base = PTS + QUAD + 8 * parity
    slots = [(left[:PTS, :], left, base + 4), (right[:PTS, :], right, base)]
    pairs = [(s, parity, 3 * s - 1, i, s) for s in range(2) for i in range(2)]
    near_blocks(flags, place8, slots, pairs, before, out, scratch)


def last_kernel(
    flags, place8, a_left, a_right, left, right, c_ends, left_c, right_c, before, out, *scratch
):
    parity = lat_parity()
    base = PTS + QUAD + 8 - 8 * parity
    ends = QUAD + 8 * parity
    slots = [
        (left[...], a_left, base + 4),
        (right[...], a_right, base),
        (left_c[...], c_ends, ends + 4),
        (right_c[...], c_ends, MSG + ends),
    ]
    pairs = [(s, 1 - parity, 3 * s - 1, i, s) for s in range(2) for i in range(2)]
    pairs += [(2 + s, 2 - 3 * parity, 3 * s - 1, 1 - parity, s) for s in range(2)]
    near_blocks(flags, place8, slots, pairs, before, out, scratch)


def near(kernel, name, n_slots, n_pairs, operands, chained=True, cost=None):
    return pl.pallas_call(
        kernel,
        in_specs=[scalars] + [whole] * (len(operands) - 2) + [hbm if chained else whole],
        out_specs=[hbm],
        out_shape=[ACC],
        scratch_shapes=near_scratch(n_slots, n_pairs),
        input_output_aliases={len(operands) - 1: 0} if chained else {},
        compiler_params=params(),
        cost_estimate=cost or COST,
        name=name,
    )(*operands)


def window_sum(flags, weights, bands):
    total = None
    for base, cells in bands:
        for v in range(6):
            if cells[v // 2] is None:
                continue
            ref, offset = cells[v // 2]
            for a in range(2):
                start = offset + (2 * a + v % 2) * RANK
                hi, lo = split(ref[start : start + RANK, :])
                u = base + a
                w = 6 * u + v
                rows = []
                for leaf in range(4):
                    block = weights[leaf, w]
                    d_row = u - 2 - leaf // 2
                    d_col = v - 2 - leaf % 2
                    if abs(d_col) <= 1:
                        inside = (d_row >= -1) & (d_row <= 1)
                        flag = flags[leaf, 3 * jnp.clip(d_row + 1, 0, 2) + d_col + 1]
                        keep = 1 - jnp.where(inside, flag, 0)
                        block = (block.astype(f32) * keep.astype(f32)).astype(bf16)
                    rows.append(block)
                stacked = jnp.concatenate(rows, 0)
                part = mm(stacked, hi) + mm(stacked, lo)
                total = part if total is None else total + part
    return total


def far_kernel(
    n_lat, n_lon, flags, weights, own, left, right, from_y, from_c, dev_a, dev_b, c_ends,
    dev_w, dev_t, group_w, leaf_t, out, group_row_w, sem,
):
    lat = lax.axis_index("lat")
    lon = lax.axis_index("lon")
    parity = lax.rem(lat, 2)
    side = lax.rem(lon, 2)
    group_row, group_col = lat // 2, lon // 2
    n_gcol = n_lon // 2
    copy = pltpu.make_async_copy(group_w.at[group_row, group_col], group_row_w, sem.at[0])
    copy.start()
    size = n_lon * RANK
    rows_of = ((dev_a, 0), (c_ends, 2 * MSG), (dev_b, 0), (c_ends, 2 * MSG + size))

    def device_coef(k, back, col_side):
        ref, offset = rows_of[k]
        which = jnp.where(side == col_side, 0, 1)
        start = pl.multiple_of(offset + (2 * back + which) * RANK, 8)
        return ref[pl.ds(start, RANK), :]

    total = jnp.zeros((RANK, COLS), f32)
    for k in range(n_lat):
        other = lat + k - 2 * (lat & k)
        u = other + 2 - 2 * group_row
        for v in range(6):
            shift = 2 * group_col - 2 + v
            drop = (jnp.abs(other - lat) <= 1) & (jnp.abs(shift - lon) <= 1)
            scale = jnp.where(drop, 0.0, 1.0)
            coef = device_coef(k, (1 - v // 2) % n_gcol, v % 2)
            total = total + scale * mm2(dev_w[6 * u + v], coef)
    copy.wait()

    def group_step(step, field):
        gcol = lax.rem(group_col + step, n_gcol)
        for pair in range(n_lat // 2):
            grow = group_row + pair - 2 * (group_row & pair)
            coef = jnp.zeros((RANK, COLS), f32)
            for e in range(2):
                k = 2 * pair + e
                other = lat + k - 2 * (lat & k)
                for f in range(2):
                    cell = other * n_lon + 2 * gcol + f
                    coef = coef + mm3(dev_t[cell], device_coef(k, n_gcol - step, f), (0, 0))
            field = field + mm2(group_row_w[grow, gcol], coef)
        return field

    field = lax.fori_loop(2, n_gcol - 1, group_step, jnp.zeros((RANK, COLS), f32))
    total = total + mm3(dev_t[lat * n_lon + lon], field)
    far = window_sum(
        flags,
        weights,
        (
            (2, ((left, PTS), (own, PTS), (right, PTS))),
            (4 * parity, (None, (from_y, 2 * PTS), None)),
            (4 - 4 * parity, ((c_ends, 0), (from_c, 2 * PTS), (c_ends, MSG))),
        ),
    )
    for leaf in range(4):
        rows = slice(leaf * RANK, (leaf + 1) * RANK)
        out[rows, :] = far[rows, :] + mm3(leaf_t[leaf], total)


def far_field(n_lat, n_lon, operands):
    specs = [scalars] + [whole] * 13
    specs[12] = hbm
    return pl.pallas_call(
        functools.partial(far_kernel, n_lat, n_lon),
        in_specs=specs,
        out_specs=whole,
        out_shape=shape(QUAD, COLS),
        scratch_shapes=[
            VMEM((n_lat // 2, n_lon // 2, RANK, RANK), bf16),
            pltpu.SemaphoreType.DMA((1,)),
        ],
        compiler_params=params(),
        cost_estimate=LOW,
        name="far",
    )(*operands)


def down_kernel(
    flags, place8, weights, left_y, right_y, partial, basis, before, out, *scratch
):
    parity = lat_parity()
    far = partial[...] + window_sum(
        flags, weights, ((4 * parity, ((left_y, PTS), None, (right_y, PTS))),)
    )
    acc = scratch[6]

    def fill(_):
        for leaf in range(4):
            acc[leaf] += mm3(basis[leaf], far[leaf * RANK : (leaf + 1) * RANK, :], (0, 0))

    base = PTS + QUAD + 8 - 8 * parity
    slots = [(left_y[:PTS, :], left_y, base + 4), (right_y[:PTS, :], right_y, base)]
    pairs = [(s, 3 * parity - 1, 3 * s - 1, parity, s) for s in range(2)]
    near_blocks(flags, place8, slots, pairs, before, out, scratch, fill)


def local(
    losses,
    positions,
    leaf_basis,
    near_flags,
    leaf_coupling,
    leaf_transfer,
    device_coupling,
    device_transfer,
    group_coupling,
):
    n_lat = lax.axis_size("lat")
    n_lon = lax.axis_size("lon")

    flat = losses.reshape(4, PTS, COLS)
    basis = jnp.swapaxes(leaf_basis, 2, 3).reshape(4, RANK, PTS)
    flags = near_flags.reshape(4, 9)
    weights = leaf_coupling.reshape(4, 36, RANK, RANK)
    transfer = leaf_transfer.reshape(4, RANK, RANK)

    to_right = [(i, (i + 1) % n_lon) for i in range(n_lon)]
    to_left = [(i, (i - 1) % n_lon) for i in range(n_lon)]
    in_chip = [(i, i ^ 1) for i in range(n_lat)]
    across = [(i, i + 1 if i % 2 else i - 1) for i in range(n_lat)]
    across = [(a, b) for a, b in across if 0 <= b < n_lat]

    across_two = [(i, i ^ 2) for i in range(n_lat)]
    partner = [(i, i ^ 1) for i in range(n_lon)]
    barrier = lax.optimization_barrier

    a_right, a_left, b_right, b_left, to_y, to_c, place8, dev = coefficients(
        flat, basis, transfer, positions.reshape(4, 2, PTS)
    )
    dev_pair = lax.ppermute(dev, "lon", partner)
    left = lax.ppermute(a_right, "lon", to_right)
    right = lax.ppermute(a_left, "lon", to_left)
    from_c = lax.ppermute(to_c, "lat", in_chip)
    from_y = lax.ppermute(to_y, "lat", across)

    dev_a = jnp.concatenate([dev, dev_pair], 0)
    step = 2
    moved = lax.ppermute(dev_a, "lon", [(i, (i + step) % n_lon) for i in range(n_lon)])
    moved, from_c, place8 = barrier((moved, from_c, place8))
    (acc,) = near(own_kernel, "own", 4, 16, (flags, place8, flat, a_right), chained=False)
    from_y, dev_a, acc = barrier((from_y, dev_a, acc))
    dev_a = jnp.concatenate([dev_a, moved], 0)
    while 2 * step < n_lon:
        step *= 2
        moved = lax.ppermute(dev_a, "lon", [(i, (i + step) % n_lon) for i in range(n_lon)])
        dev_a = jnp.concatenate([dev_a, moved], 0)
    (acc,) = near(lat_kernel, "lat", 4, 8, (flags, place8, from_y, from_c, acc))
    dev_a, acc = barrier((dev_a, acc))
    dev_b = lax.ppermute(dev_a, "lat", across_two)
    left, right, dev_b, b_right, b_left, acc = barrier(
        (left, right, dev_b, b_right, b_left, acc)
    )
    left_b = lax.ppermute(b_right, "lon", to_right)
    right_b = lax.ppermute(b_left, "lon", to_left)
    left_y = lax.ppermute(left, "lat", across)
    right_y = lax.ppermute(right, "lat", across)
    to_c = jnp.concatenate([left[PTS:], right[PTS:], dev_a, dev_b], 0)
    c_ends = lax.ppermute(to_c, "lat", in_chip)
    (acc,) = near(lon_kernel, "lon", 2, 4, (flags, place8, left, right, acc))
    c_ends, acc = barrier((c_ends, acc))
    partial = far_field(
        n_lat,
        n_lon,
        (
            flags,
            weights,
            a_right,
            left,
            right,
            from_y,
            from_c,
            dev_a,
            dev_b,
            c_ends,
            device_coupling.reshape(36, RANK, RANK),
            device_transfer.reshape(n_lat * n_lon, RANK, RANK),
            group_coupling,
            transfer,
        ),
    )
    left_y, right_y, partial = barrier((left_y, right_y, partial))
    (acc,) = near(
        down_kernel,
        "down",
        2,
        2,
        (flags, place8, weights, left_y, right_y, partial, basis, acc),
        cost=LOW,
    )
    left_b, right_b, acc = barrier((left_b, right_b, acc))
    left_c = lax.ppermute(left_b, "lat", in_chip)
    right_c = lax.ppermute(right_b, "lat", in_chip)
    (acc,) = near(
        last_kernel,
        "last",
        4,
        6,
        (flags, place8, left, right, left_b, right_b, c_ends, left_c, right_c, acc),
    )
    return acc.reshape(2, 2, PTS, COLS)


def solution(mesh):
    placed = (
        P("lat", "lon", None, None),
        P("lat", "lon", None, None),
        P("lat", "lon", None, None),
        P("lat", "lon", None),
        P("lat", "lon", None, None, None),
        P("lat", "lon", None, None),
        P("lat", "lon", None, None, None),
        P(),
        P(),
    )
    return jax.shard_map(
        local, mesh=mesh, in_specs=placed, out_specs=P("lat", "lon", None, None), check_vma=False
    )
```

```python
import functools

import jax
import jax.numpy as jnp
from jax import lax
from jax.experimental import pallas as pl
from jax.experimental.pallas import tpu as pltpu
from jax.sharding import PartitionSpec as P

PTS = 512
RANK = 64
COLS = 256
HALF = 256
QUAD = 4 * RANK
MSG = QUAD + 16

LN2 = 0.6931471805599453
UNIT = 1.7320508075688772 / 0.15 / LN2

f32 = jnp.float32
bf16 = jnp.bfloat16
VMEM = pltpu.VMEM
SMEM = pltpu.SMEM
whole = pl.BlockSpec(memory_space=VMEM)
scalars = pl.BlockSpec(memory_space=SMEM)


def split(x):
    hi = x.astype(bf16)
    return hi, (x - hi.astype(f32)).astype(bf16)


def mm(a, b, dims=(1, 0)):
    return lax.dot_general(
        a, b, (((dims[0],), (dims[1],)), ((), ())), preferred_element_type=f32
    )


def mm3(a, b, dims=(1, 0)):
    a_hi, a_lo = split(a)
    b_hi, b_lo = split(b)
    return mm(a_hi, b_hi, dims) + (mm(a_lo, b_hi, dims) + mm(a_hi, b_lo, dims))


def mm2(a, b):
    b_hi, b_lo = split(b)
    return mm(a, b_hi) + mm(a, b_lo)


def params(limit=64):
    return pltpu.CompilerParams(vmem_limit_bytes=limit * 1024 * 1024)


COST = pl.CostEstimate(flops=20_000_000_000, bytes_accessed=4_000_000, transcendentals=0)
LOW = pl.CostEstimate(flops=1_000, bytes_accessed=1_000, transcendentals=0)


def shape(*dims):
    return jax.ShapeDtypeStruct(dims, f32)


def lat_parity():
    return lax.rem(lax.axis_index("lat"), 2)


def coef_kernel(
    loss, basis, transfer, pos, a_right, a_left, b_right, b_left, to_y, to_c, place8, dev,
    values, bases, message, sems, load_sems,
):
    parity = lat_parity()
    loads = [
        (
            pltpu.make_async_copy(loss.at[leaf], values.at[leaf], load_sems.at[leaf]),
            pltpu.make_async_copy(basis.at[leaf], bases.at[leaf], load_sems.at[4 + leaf]),
        )
        for leaf in range(4)
    ]
    for pair in loads:
        for copy in pair:
            copy.start()
    for leaf in range(4):
        place = pos[leaf] * UNIT
        place8[leaf] = jnp.concatenate([place, jnp.zeros((6, PTS), f32)], 0)
        for coord in range(2):
            for half in range(2):
                at = QUAD + 4 * leaf + 2 * coord + half
                message[at : at + 1, :] = place[coord : coord + 1, half * HALF : (half + 1) * HALF]
    for pair in loads:
        for copy in pair:
            copy.wait()
    y_row, c_row = 2 * parity, 2 - 2 * parity
    first, second = slice(0, PTS), slice(PTS, 2 * PTS)
    copies = []
    for source, target in (
        (y_row + 1, a_right.at[first]),
        (y_row, a_left.at[first]),
        (c_row + 1, b_right),
        (c_row, b_left),
        (y_row, to_y.at[first]),
        (y_row + 1, to_y.at[second]),
        (c_row, to_c.at[first]),
        (c_row + 1, to_c.at[second]),
    ):
        copy = pltpu.make_async_copy(values.at[source], target, sems.at[len(copies)])
        copy.start()
        copies.append(copy)
    total = None
    for leaf in range(4):
        l_hi, l_lo = split(values[leaf])
        b_hi, b_lo = split(bases[leaf])
        coef = mm(b_hi, l_hi) + (mm(b_lo, l_hi) + mm(b_hi, l_lo))
        message[leaf * RANK : (leaf + 1) * RANK, :] = coef
        part = mm3(transfer[leaf], coef, (0, 0))
        total = part if leaf == 0 else total + part
    dev[...] = total
    for target in (
        a_right.at[PTS:], a_left.at[PTS:], to_y.at[2 * PTS :], to_c.at[2 * PTS :]
    ):
        copy = pltpu.make_async_copy(message, target, sems.at[len(copies)])
        copy.start()
        copies.append(copy)
    for copy in copies:
        copy.wait()


hbm = pl.BlockSpec(memory_space=pl.ANY)


def coefficients(losses, basis, transfer, positions):
    return pl.pallas_call(
        coef_kernel,
        in_specs=[hbm, hbm, whole, whole],
        out_specs=[hbm] * 6 + [whole] * 2,
        out_shape=[
            shape(PTS + MSG, COLS),
            shape(PTS + MSG, COLS),
            shape(PTS, COLS),
            shape(PTS, COLS),
            shape(2 * PTS + MSG, COLS),
            shape(2 * PTS + MSG, COLS),
            shape(4, 8, PTS),
            shape(RANK, COLS),
        ],
        scratch_shapes=[
            VMEM((4, PTS, COLS), f32),
            VMEM((4, RANK, PTS), f32),
            VMEM((MSG, COLS), f32),
            pltpu.SemaphoreType.DMA((12,)),
            pltpu.SemaphoreType.DMA((8,)),
        ],
        compiler_params=params(),
        cost_estimate=COST,
        name="coefs",
    )(losses, basis, transfer, positions)


def near_scratch(n_slots, n_pairs):
    return [
        SMEM((n_pairs + 1, 8), jnp.int32),
        VMEM((4, PTS, 8), f32),
        VMEM((n_slots, 8, PTS), f32),
        VMEM((n_slots, 2 * PTS, COLS), bf16),
        VMEM((PTS, 2 * PTS), bf16),
        VMEM((PTS, 2 * PTS), bf16),
        VMEM((4, PTS, COLS), f32),
        VMEM((n_slots, PTS, COLS), f32),
        VMEM((n_slots, 16, COLS), f32),
        pltpu.SemaphoreType.DMA((8 + 2 * n_slots,)),
    ]


def near_blocks(flags, place8, slots, pairs, before, out, scratch, fill=None):
    table, tpos, spos, stack, kern_a, kern_b, acc, stage, marks, sems = scratch
    arrivals = []
    for slot, (values, places, _) in enumerate(slots):
        pair = (
            pltpu.make_async_copy(values, stage.at[slot], sems.at[8 + 2 * slot]),
            pltpu.make_async_copy(places, marks.at[slot], sems.at[9 + 2 * slot]),
        )
        for copy in pair:
            copy.start()
        arrivals.append(pair)
    loads = []
    if before is not None:
        loads = [
            pltpu.make_async_copy(before.at[leaf], acc.at[leaf], sems.at[leaf])
            for leaf in range(4)
        ]
    for copy in loads:
        copy.start()
    for leaf in range(4):
        tpos[leaf] = place8[leaf].T
    for slot, (_, _, base) in enumerate(slots):
        for copy in arrivals[slot]:
            copy.wait()
        hi, lo = split(stage[slot])
        stack[slot, :PTS, :] = hi
        stack[slot, PTS:, :] = lo
        for coord in range(2):
            for half in range(2):
                spos[slot, coord : coord + 1, half * HALF : (half + 1) * HALF] = marks[
                    slot, pl.ds(base + 2 * coord + half, 1), :
                ]
    count = 0
    for slot, row, col, own_row, own_col in pairs:
        target = 2 * own_row + own_col
        table[count, 0] = slot
        table[count, 1] = target
        table[count, 2] = row - own_row
        table[count, 3] = col - own_col
        flag = flags[target, 3 * (row - own_row + 1) + col - own_col + 1]
        count = count + jnp.where(flag > 0, 1, 0)

    def evaluate(index, half, kern):
        slot, target = table[index, 0], table[index, 1]
        src_row = spos[slot, 0:1, :] + table[index, 2].astype(f32) * UNIT
        src_col = spos[slot, 1:2, :] + table[index, 3].astype(f32) * UNIT
        part = slice(half * HALF, (half + 1) * HALF)
        d_row = tpos[target, part, 0:1] - src_row
        d_col = tpos[target, part, 1:2] - src_col
        square = d_row * d_row + d_col * d_col
        dist = square * lax.rsqrt(jnp.maximum(square, 1e-30))
        decay = jnp.exp2(-dist)
        hi, lo = split(decay + decay * (dist * LN2))
        kern[part, :PTS] = hi
        kern[part, PTS:] = lo

    def apply(index, half, kern):
        slot, target = table[index, 0], table[index, 1]
        part = slice(half * HALF, (half + 1) * HALF)
        l_hi = stack[slot, :PTS, :]
        l_lo = stack[slot, PTS:, :]
        k_hi = kern[part, :PTS]
        k_lo = kern[part, PTS:]
        acc[target, part, :] += mm(k_hi, l_hi) + mm(k_lo, l_hi) + mm(k_hi, l_lo)

    def step(index, kern, other):
        following = jnp.minimum(index + 1, count - 1)
        for half in range(2):
            evaluate(following, half, other)
            apply(index, half, kern)

    @pl.when(count > 0)
    def _():
        for half in range(2):
            evaluate(0, half, kern_a)

    for copy in loads:
        copy.wait()
    if fill is not None:
        fill(acc, stage)

    @pl.loop(0, (count + 1) // 2)
    def _(pair):
        step(2 * pair, kern_a, kern_b)

        @pl.when(2 * pair + 1 < count)
        def _():
            step(2 * pair + 1, kern_b, kern_a)


    stores = [
        pltpu.make_async_copy(acc.at[leaf], out.at[leaf], sems.at[4 + leaf]) for leaf in range(4)
    ]
    for copy in stores:
        copy.start()
    for copy in stores:
        copy.wait()


ACC = shape(4, PTS, COLS)


def block(ref, start, rows):
    return ref.at[pl.ds(start, rows)]


def own_kernel(flags, place8, loss, msg, out, *scratch):
    slots = [(loss.at[leaf], block(msg, PTS + QUAD, 16), 4 * leaf) for leaf in range(4)]
    pairs = [(s, s // 2, s % 2, t // 2, t % 2) for s in range(4) for t in range(4)]

    def fill(acc, losses):
        for leaf in range(4):
            acc[leaf] = 0.5 * losses[leaf]

    near_blocks(flags, place8, slots, pairs, None, out, scratch, fill)


def lat_kernel(flags, place8, from_y, from_c, before, out, *scratch):
    parity = lat_parity()
    slots, pairs = [], []
    for ref, place, row, own_row in (
        (from_y, 8 - 8 * parity, 3 * parity - 1, parity),
        (from_c, 8 * parity, 2 - 3 * parity, 1 - parity),
    ):
        for col in range(2):
            for own_col in range(2):
                pairs.append((len(slots), row, col, own_row, own_col))
            slots.append(
                (block(ref, col * PTS, PTS), block(ref, 2 * PTS + QUAD, 16), place + 4 * col)
            )
    near_blocks(flags, place8, slots, pairs, before, out, scratch)


def lon_kernel(flags, place8, left, right, before, out, *scratch):
    parity = lat_parity()
    at = PTS + QUAD
    slots = [
        (block(left, 0, PTS), block(left, at, 16), 8 * parity + 4),
        (block(right, 0, PTS), block(right, at, 16), 8 * parity),
    ]
    pairs = [(s, parity, 3 * s - 1, i, s) for s in range(2) for i in range(2)]
    near_blocks(flags, place8, slots, pairs, before, out, scratch)


def last_kernel(
    flags, place8, a_left, a_right, left, right, c_ends, left_c, right_c, before, out, *scratch
):
    parity = lat_parity()
    at = PTS + QUAD
    own_place, far_place = 8 - 8 * parity, 8 * parity
    slots = [
        (left, block(a_left, at, 16), own_place + 4),
        (right, block(a_right, at, 16), own_place),
        (left_c, block(c_ends, at, 16), far_place + 4),
        (right_c, block(c_ends, PTS + MSG + at, 16), far_place),
    ]
    pairs = [(s, 1 - parity, 3 * s - 1, i, s) for s in range(2) for i in range(2)]
    pairs += [(2 + s, 2 - 3 * parity, 3 * s - 1, 1 - parity, s) for s in range(2)]
    near_blocks(flags, place8, slots, pairs, before, out, scratch)


def near(kernel, name, n_slots, n_pairs, operands, chained=True, cost=None, scratch=()):
    return pl.pallas_call(
        kernel,
        in_specs=[scalars, whole] + [hbm] * (len(operands) - 2),
        out_specs=[hbm],
        out_shape=[ACC],
        scratch_shapes=near_scratch(n_slots, n_pairs) + list(scratch),
        input_output_aliases={len(operands) - 1: 0} if chained else {},
        compiler_params=params(),
        cost_estimate=cost or COST,
        name=name,
    )(*operands)


def window_sum(flags, weights, bands, first=0):
    total = None
    for base, cells in bands:
        for v in range(6):
            if cells[v // 2] is None:
                continue
            ref, offset = cells[v // 2]
            for a in range(2):
                start = offset + (2 * a + v % 2) * RANK
                hi, lo = split(ref[start : start + RANK, :])
                u = base + a
                w = 6 * u + v
                rows = []
                for leaf in range(4):
                    part_w = weights[leaf, w - first]
                    d_row = u - 2 - leaf // 2
                    d_col = v - 2 - leaf % 2
                    if abs(d_col) <= 1:
                        inside = (d_row >= -1) & (d_row <= 1)
                        flag = flags[leaf, 3 * jnp.clip(d_row + 1, 0, 2) + d_col + 1]
                        keep = 1 - jnp.where(inside, flag, 0)
                        part_w = (part_w.astype(f32) * keep.astype(f32)).astype(bf16)
                    rows.append(part_w)
                stacked = jnp.concatenate(rows, 0)
                part = mm(stacked, hi) + mm(stacked, lo)
                total = part if total is None else total + part
    return total


def far_kernel(
    n_lat, n_lon, flags, weights, own, left, right, from_y, from_c, dev_a, dev_b, c_ends,
    dev_w, dev_t, group_w, leaf_t, out, weights_v, cells, rows_dev, dev_w_v, dev_t_v,
    group_row_w, leaf_t_v, sems,
):
    lat = lax.axis_index("lat")
    lon = lax.axis_index("lon")
    parity = lax.rem(lat, 2)
    side = lax.rem(lon, 2)
    group_row, group_col = lat // 2, lon // 2
    n_gcol = n_lon // 2
    size = n_lon * RANK
    ends = 2 * (PTS + MSG)
    copies = []
    for source, target in (
        (dev_w, dev_w_v),
        (dev_a, rows_dev.at[0]),
        (block(c_ends, ends, size), rows_dev.at[1]),
        (dev_b, rows_dev.at[2]),
        (block(c_ends, ends + size, size), rows_dev.at[3]),
        (group_w.at[group_row, group_col], group_row_w),
        (dev_t, dev_t_v),
        (leaf_t, leaf_t_v),
        (block(own, PTS, QUAD), cells.at[0]),
        (block(left, PTS, QUAD), cells.at[1]),
        (block(right, PTS, QUAD), cells.at[2]),
        (block(from_y, 2 * PTS, QUAD), cells.at[3]),
        (block(from_c, 2 * PTS, QUAD), cells.at[4]),
        (block(c_ends, PTS, QUAD), cells.at[5]),
        (block(c_ends, 2 * PTS + MSG, QUAD), cells.at[6]),
        (weights.at[0], weights_v.at[0]),
        (weights.at[1], weights_v.at[1]),
        (weights.at[2], weights_v.at[2]),
        (weights.at[3], weights_v.at[3]),
    ):
        copy = pltpu.make_async_copy(source, target, sems.at[len(copies)])
        copy.start()
        copies.append(copy)
    for copy in copies[:5]:
        copy.wait()

    def device_coef(k, back, col_side):
        which = jnp.where(side == col_side, 0, 1)
        start = pl.multiple_of((2 * back + which) * RANK, RANK)
        return rows_dev[k, pl.ds(start, RANK), :]

    total = jnp.zeros((RANK, COLS), f32)
    for k in range(n_lat):
        other = lat + k - 2 * (lat & k)
        u = other + 2 - 2 * group_row
        for v in range(6):
            shift = 2 * group_col - 2 + v
            drop = (jnp.abs(other - lat) <= 1) & (jnp.abs(shift - lon) <= 1)
            scale = jnp.where(drop, 0.0, 1.0)
            coef = device_coef(k, (1 - v // 2) % n_gcol, v % 2)
            total = total + scale * mm2(dev_w_v[6 * u + v], coef)
    for copy in copies[5:8]:
        copy.wait()

    def group_step(step, field):
        gcol = lax.rem(group_col + step, n_gcol)
        for pair in range(n_lat // 2):
            grow = group_row + pair - 2 * (group_row & pair)
            coef = jnp.zeros((RANK, COLS), f32)
            for e in range(2):
                k = 2 * pair + e
                other = lat + k - 2 * (lat & k)
                for f in range(2):
                    cell = other * n_lon + 2 * gcol + f
                    coef = coef + mm3(dev_t_v[cell], device_coef(k, n_gcol - step, f), (0, 0))
            field = field + mm2(group_row_w[grow, gcol], coef)
        return field

    field = lax.fori_loop(2, n_gcol - 1, group_step, jnp.zeros((RANK, COLS), f32))
    total = total + mm3(dev_t_v[lat * n_lon + lon], field)
    for copy in copies[8:]:
        copy.wait()
    far = window_sum(
        flags,
        weights_v,
        (
            (2, tuple((cells.at[i], 0) for i in (1, 0, 2))),
            (4 * parity, (None, (cells.at[3], 0), None)),
            (4 - 4 * parity, tuple((cells.at[i], 0) for i in (5, 4, 6))),
        ),
    )
    for leaf in range(4):
        rows = slice(leaf * RANK, (leaf + 1) * RANK)
        out[rows, :] = far[rows, :] + mm3(leaf_t_v[leaf], total)


def far_field(n_lat, n_lon, operands):
    return pl.pallas_call(
        functools.partial(far_kernel, n_lat, n_lon),
        in_specs=[scalars] + [hbm] * 13,
        out_specs=whole,
        out_shape=shape(QUAD, COLS),
        scratch_shapes=[
            VMEM((4, 36, RANK, RANK), bf16),
            VMEM((7, QUAD, COLS), f32),
            VMEM((n_lat, n_lon * RANK, COLS), f32),
            VMEM((36, RANK, RANK), bf16),
            VMEM((n_lat * n_lon, RANK, RANK), f32),
            VMEM((n_lat // 2, n_lon // 2, RANK, RANK), bf16),
            VMEM((4, RANK, RANK), f32),
            pltpu.SemaphoreType.DMA((19,)),
        ],
        compiler_params=params(),
        cost_estimate=LOW,
        name="far",
    )(*operands)


def down_kernel(
    flags, place8, weights, left_y, right_y, partial, basis, before, out, *scratch
):
    parity = lat_parity()
    near_refs, (weights_v, cells, basis_v, sems) = scratch[:-4], scratch[-4:]
    at = PTS + QUAD
    copies = []
    for source, target in (
        (block(left_y, PTS, QUAD), cells.at[0]),
        (block(right_y, PTS, QUAD), cells.at[1]),
        (partial, cells.at[2]),
        (weights.at[:, pl.ds(24 * parity, 12)], weights_v),
        (basis, basis_v),
    ):
        copy = pltpu.make_async_copy(source, target, sems.at[len(copies)])
        copy.start()
        copies.append(copy)

    def fill(acc, _):
        for copy in copies:
            copy.wait()
        band = (4 * parity, ((cells.at[0], 0), None, (cells.at[1], 0)))
        far = cells[2] + window_sum(flags, weights_v, (band,), 24 * parity)
        for leaf in range(4):
            acc[leaf] += mm3(basis_v[leaf], far[leaf * RANK : (leaf + 1) * RANK, :], (0, 0))

    base = 8 - 8 * parity
    slots = [
        (block(left_y, 0, PTS), block(left_y, at, 16), base + 4),
        (block(right_y, 0, PTS), block(right_y, at, 16), base),
    ]
    pairs = [(s, 3 * parity - 1, 3 * s - 1, parity, s) for s in range(2)]
    near_blocks(flags, place8, slots, pairs, before, out, near_refs, fill)


def local(
    losses,
    positions,
    leaf_basis,
    near_flags,
    leaf_coupling,
    leaf_transfer,
    device_coupling,
    device_transfer,
    group_coupling,
):
    n_lat = lax.axis_size("lat")
    n_lon = lax.axis_size("lon")

    flat = losses.reshape(4, PTS, COLS)
    basis = jnp.swapaxes(leaf_basis, 2, 3).reshape(4, RANK, PTS)
    flags = near_flags.reshape(4, 9)
    weights = leaf_coupling.reshape(4, 36, RANK, RANK)
    transfer = leaf_transfer.reshape(4, RANK, RANK)

    to_right = [(i, (i + 1) % n_lon) for i in range(n_lon)]
    to_left = [(i, (i - 1) % n_lon) for i in range(n_lon)]
    in_chip = [(i, i ^ 1) for i in range(n_lat)]
    across = [(i, i + 1 if i % 2 else i - 1) for i in range(n_lat)]
    across = [(a, b) for a, b in across if 0 <= b < n_lat]

    across_two = [(i, i ^ 2) for i in range(n_lat)]
    partner = [(i, i ^ 1) for i in range(n_lon)]
    barrier = lax.optimization_barrier

    a_right, a_left, b_right, b_left, to_y, to_c, place8, dev = coefficients(
        flat, basis, transfer, positions.reshape(4, 2, PTS)
    )
    dev_pair = lax.ppermute(dev, "lon", partner)
    from_c = lax.ppermute(to_c, "lat", in_chip)
    from_y = lax.ppermute(to_y, "lat", across)

    pair = jnp.concatenate([dev, dev_pair], 0)
    moved = [
        lax.ppermute(pair, "lon", [(i, (i + step) % n_lon) for i in range(n_lon)])
        for step in range(2, n_lon, 2)
    ]
    a_right, a_left, *moved = barrier((a_right, a_left, *moved))
    left = lax.ppermute(a_right, "lon", to_right)
    right = lax.ppermute(a_left, "lon", to_left)
    dev_a = jnp.concatenate([pair, *moved], 0)
    dev_a, from_c, place8 = barrier((dev_a, from_c, place8))
    dev_b = lax.ppermute(dev_a, "lat", across_two)
    (acc,) = near(own_kernel, "own", 4, 16, (flags, place8, flat, a_right), chained=False)
    from_y, acc = barrier((from_y, acc))
    (acc,) = near(lat_kernel, "lat", 4, 8, (flags, place8, from_y, from_c, acc))
    dev_b, acc = barrier((dev_b, acc))
    left, right, b_right, b_left, acc = barrier((left, right, b_right, b_left, acc))
    left_b = lax.ppermute(b_right, "lon", to_right)
    right_b = lax.ppermute(b_left, "lon", to_left)
    left_y = lax.ppermute(left, "lat", across)
    right_y = lax.ppermute(right, "lat", across)
    to_c = jnp.concatenate([left, right, dev_a, dev_b], 0)
    c_ends = lax.ppermute(to_c, "lat", in_chip)
    (acc,) = near(lon_kernel, "lon", 2, 4, (flags, place8, left, right, acc))
    c_ends, acc = barrier((c_ends, acc))
    partial = far_field(
        n_lat,
        n_lon,
        (
            flags,
            weights,
            a_right,
            left,
            right,
            from_y,
            from_c,
            dev_a,
            dev_b,
            c_ends,
            device_coupling.reshape(36, RANK, RANK),
            device_transfer.reshape(n_lat * n_lon, RANK, RANK),
            group_coupling,
            transfer,
        ),
    )
    left_y, right_y, partial = barrier((left_y, right_y, partial))
    (acc,) = near(
        down_kernel,
        "down",
        2,
        2,
        (flags, place8, weights, left_y, right_y, partial, basis, acc),
        cost=LOW,
        scratch=[
            VMEM((4, 12, RANK, RANK), bf16),
            VMEM((3, QUAD, COLS), f32),
            VMEM((4, RANK, PTS), f32),
            pltpu.SemaphoreType.DMA((5,)),
        ],
    )
    left_b, right_b, acc = barrier((left_b, right_b, acc))
    left_c = lax.ppermute(left_b, "lat", in_chip)
    right_c = lax.ppermute(right_b, "lat", in_chip)
    (acc,) = near(
        last_kernel,
        "last",
        4,
        6,
        (flags, place8, left, right, left_b, right_b, c_ends, left_c, right_c, acc),
    )
    return acc.reshape(2, 2, PTS, COLS)


def solution(mesh):
    placed = (
        P("lat", "lon", None, None),
        P("lat", "lon", None, None),
        P("lat", "lon", None, None),
        P("lat", "lon", None),
        P("lat", "lon", None, None, None),
        P("lat", "lon", None, None),
        P("lat", "lon", None, None, None),
        P(),
        P(),
    )
    return jax.shard_map(
        local, mesh=mesh, in_specs=placed, out_specs=P("lat", "lon", None, None), check_vma=False
    )
```

```python
import functools

import jax
import jax.numpy as jnp
from jax import lax
from jax.experimental import pallas as pl
from jax.experimental.pallas import tpu as pltpu
from jax.sharding import PartitionSpec as P

PTS = 512
RANK = 64
COLS = 256
HALF = 256
QUAD = 4 * RANK
MSG = QUAD + 16

LN2 = 0.6931471805599453
UNIT = 1.7320508075688772 / 0.15 / LN2

f32 = jnp.float32
bf16 = jnp.bfloat16
VMEM = pltpu.VMEM
SMEM = pltpu.SMEM
whole = pl.BlockSpec(memory_space=VMEM)
scalars = pl.BlockSpec(memory_space=SMEM)


def split(x):
    hi = x.astype(bf16)
    return hi, (x - hi.astype(f32)).astype(bf16)


def mm(a, b, dims=(1, 0)):
    return lax.dot_general(
        a, b, (((dims[0],), (dims[1],)), ((), ())), preferred_element_type=f32
    )


def mm3(a, b, dims=(1, 0)):
    a_hi, a_lo = split(a)
    b_hi, b_lo = split(b)
    return mm(a_hi, b_hi, dims) + (mm(a_lo, b_hi, dims) + mm(a_hi, b_lo, dims))


def mm2(a, b):
    b_hi, b_lo = split(b)
    return mm(a, b_hi) + mm(a, b_lo)


def params(limit=64):
    return pltpu.CompilerParams(vmem_limit_bytes=limit * 1024 * 1024)


COST = pl.CostEstimate(flops=20_000_000_000, bytes_accessed=4_000_000, transcendentals=0)
LOW = pl.CostEstimate(flops=1_000, bytes_accessed=1_000, transcendentals=0)


def shape(*dims):
    return jax.ShapeDtypeStruct(dims, f32)


def lat_parity():
    return lax.rem(lax.axis_index("lat"), 2)


def coef_kernel(
    loss, basis, transfer, pos, a_right, a_left, b_right, b_left, to_y, to_c, place8, dev,
    values, bases, message, sems, load_sems,
):
    parity = lat_parity()
    loads = [
        (
            pltpu.make_async_copy(loss.at[leaf], values.at[leaf], load_sems.at[leaf]),
            pltpu.make_async_copy(basis.at[leaf], bases.at[leaf], load_sems.at[4 + leaf]),
        )
        for leaf in range(4)
    ]
    for pair in loads:
        for copy in pair:
            copy.start()
    for leaf in range(4):
        place = pos[leaf] * UNIT
        place8[leaf] = jnp.concatenate([place, jnp.zeros((6, PTS), f32)], 0)
        for coord in range(2):
            for half in range(2):
                at = QUAD + 4 * leaf + 2 * coord + half
                message[at : at + 1, :] = place[coord : coord + 1, half * HALF : (half + 1) * HALF]
    for pair in loads:
        for copy in pair:
            copy.wait()
    y_row, c_row = 2 * parity, 2 - 2 * parity
    first, second = slice(0, PTS), slice(PTS, 2 * PTS)
    copies = []
    for source, target in (
        (y_row + 1, a_right.at[first]),
        (y_row, a_left.at[first]),
        (c_row + 1, b_right),
        (c_row, b_left),
        (y_row, to_y.at[first]),
        (y_row + 1, to_y.at[second]),
        (c_row, to_c.at[first]),
        (c_row + 1, to_c.at[second]),
    ):
        copy = pltpu.make_async_copy(values.at[source], target, sems.at[len(copies)])
        copy.start()
        copies.append(copy)
    total = None
    for leaf in range(4):
        l_hi, l_lo = split(values[leaf])
        b_hi, b_lo = split(bases[leaf])
        coef = mm(b_hi, l_hi) + (mm(b_lo, l_hi) + mm(b_hi, l_lo))
        message[leaf * RANK : (leaf + 1) * RANK, :] = coef
        part = mm3(transfer[leaf], coef, (0, 0))
        total = part if leaf == 0 else total + part
    dev[...] = total
    for target in (
        a_right.at[PTS:], a_left.at[PTS:], to_y.at[2 * PTS :], to_c.at[2 * PTS :]
    ):
        copy = pltpu.make_async_copy(message, target, sems.at[len(copies)])
        copy.start()
        copies.append(copy)
    for copy in copies:
        copy.wait()


hbm = pl.BlockSpec(memory_space=pl.ANY)


def coefficients(losses, basis, transfer, positions):
    return pl.pallas_call(
        coef_kernel,
        in_specs=[hbm, hbm, whole, whole],
        out_specs=[hbm] * 6 + [whole] * 2,
        out_shape=[
            shape(PTS + MSG, COLS),
            shape(PTS + MSG, COLS),
            shape(PTS, COLS),
            shape(PTS, COLS),
            shape(2 * PTS + MSG, COLS),
            shape(2 * PTS + MSG, COLS),
            shape(4, 8, PTS),
            shape(RANK, COLS),
        ],
        scratch_shapes=[
            VMEM((4, PTS, COLS), f32),
            VMEM((4, RANK, PTS), f32),
            VMEM((MSG, COLS), f32),
            pltpu.SemaphoreType.DMA((12,)),
            pltpu.SemaphoreType.DMA((8,)),
        ],
        compiler_params=params(),
        cost_estimate=COST,
        name="coefs",
    )(losses, basis, transfer, positions)


def near_scratch(n_slots, n_pairs):
    return [
        SMEM((n_pairs + 1, 8), jnp.int32),
        VMEM((4, PTS, 8), f32),
        VMEM((n_slots, 8, PTS), f32),
        VMEM((n_slots, 2 * PTS, COLS), bf16),
        VMEM((PTS, 2 * PTS), bf16),
        VMEM((PTS, 2 * PTS), bf16),
        VMEM((4, PTS, COLS), f32),
        VMEM((n_slots, PTS, COLS), f32),
        VMEM((n_slots, 16, COLS), f32),
        pltpu.SemaphoreType.DMA((8 + 2 * n_slots,)),
    ]


def near_blocks(flags, place8, slots, pairs, before, out, scratch, fill=None):
    table, tpos, spos, stack, kern_a, kern_b, acc, stage, marks, sems = scratch
    arrivals = []
    for slot, (values, places, _) in enumerate(slots):
        pair = (
            pltpu.make_async_copy(values, stage.at[slot], sems.at[8 + 2 * slot]),
            pltpu.make_async_copy(places, marks.at[slot], sems.at[9 + 2 * slot]),
        )
        for copy in pair:
            copy.start()
        arrivals.append(pair)
    loads = []
    if before is not None:
        loads = [
            pltpu.make_async_copy(before.at[leaf], acc.at[leaf], sems.at[leaf])
            for leaf in range(4)
        ]
    for copy in loads:
        copy.start()
    for leaf in range(4):
        tpos[leaf] = place8[leaf].T
    for slot, (_, _, base) in enumerate(slots):
        for copy in arrivals[slot]:
            copy.wait()
        hi, lo = split(stage[slot])
        stack[slot, :PTS, :] = hi
        stack[slot, PTS:, :] = lo
        for coord in range(2):
            for half in range(2):
                spos[slot, coord : coord + 1, half * HALF : (half + 1) * HALF] = marks[
                    slot, pl.ds(base + 2 * coord + half, 1), :
                ]
    count = 0
    for slot, row, col, own_row, own_col in pairs:
        target = 2 * own_row + own_col
        table[count, 0] = slot
        table[count, 1] = target
        table[count, 2] = row - own_row
        table[count, 3] = col - own_col
        flag = flags[target, 3 * (row - own_row + 1) + col - own_col + 1]
        count = count + jnp.where(flag > 0, 1, 0)

    def evaluate(index, half, kern):
        slot, target = table[index, 0], table[index, 1]
        src_row = spos[slot, 0:1, :] + table[index, 2].astype(f32) * UNIT
        src_col = spos[slot, 1:2, :] + table[index, 3].astype(f32) * UNIT
        part = slice(half * HALF, (half + 1) * HALF)
        d_row = tpos[target, part, 0:1] - src_row
        d_col = tpos[target, part, 1:2] - src_col
        square = d_row * d_row + d_col * d_col
        dist = square * lax.rsqrt(jnp.maximum(square, 1e-30))
        decay = jnp.exp2(-dist)
        hi, lo = split(decay + decay * (dist * LN2))
        kern[part, :PTS] = hi
        kern[part, PTS:] = lo

    def apply(index, half, kern):
        slot, target = table[index, 0], table[index, 1]
        part = slice(half * HALF, (half + 1) * HALF)
        l_hi = stack[slot, :PTS, :]
        l_lo = stack[slot, PTS:, :]
        k_hi = kern[part, :PTS]
        k_lo = kern[part, PTS:]
        acc[target, part, :] += mm(k_hi, l_hi) + mm(k_lo, l_hi) + mm(k_hi, l_lo)

    def step(index, kern, other):
        following = jnp.minimum(index + 1, count - 1)
        for half in range(2):
            evaluate(following, half, other)
            apply(index, half, kern)

    @pl.when(count > 0)
    def _():
        for half in range(2):
            evaluate(0, half, kern_a)

    for copy in loads:
        copy.wait()
    if fill is not None:
        fill(acc, stage)

    @pl.loop(0, (count + 1) // 2)
    def _(pair):
        step(2 * pair, kern_a, kern_b)

        @pl.when(2 * pair + 1 < count)
        def _():
            step(2 * pair + 1, kern_b, kern_a)


    stores = [
        pltpu.make_async_copy(acc.at[leaf], out.at[leaf], sems.at[4 + leaf]) for leaf in range(4)
    ]
    for copy in stores:
        copy.start()
    for copy in stores:
        copy.wait()


ACC = shape(4, PTS, COLS)


def block(ref, start, rows):
    return ref.at[pl.ds(start, rows)]


def own_kernel(flags, place8, loss, msg, out, *scratch):
    slots = [(loss.at[leaf], block(msg, PTS + QUAD, 16), 4 * leaf) for leaf in range(4)]
    pairs = [(s, s // 2, s % 2, t // 2, t % 2) for s in range(4) for t in range(4)]

    def fill(acc, losses):
        for leaf in range(4):
            acc[leaf] = 0.5 * losses[leaf]

    near_blocks(flags, place8, slots, pairs, None, out, scratch, fill)


def lat_kernel(flags, place8, from_y, from_c, before, out, *scratch):
    parity = lat_parity()
    slots, pairs = [], []
    for ref, place, row, own_row in (
        (from_y, 8 - 8 * parity, 3 * parity - 1, parity),
        (from_c, 8 * parity, 2 - 3 * parity, 1 - parity),
    ):
        for col in range(2):
            for own_col in range(2):
                pairs.append((len(slots), row, col, own_row, own_col))
            slots.append(
                (block(ref, col * PTS, PTS), block(ref, 2 * PTS + QUAD, 16), place + 4 * col)
            )
    near_blocks(flags, place8, slots, pairs, before, out, scratch)


def lon_kernel(flags, place8, left, right, before, out, *scratch):
    parity = lat_parity()
    at = PTS + QUAD
    slots = [
        (block(left, 0, PTS), block(left, at, 16), 8 * parity + 4),
        (block(right, 0, PTS), block(right, at, 16), 8 * parity),
    ]
    pairs = [(s, parity, 3 * s - 1, i, s) for s in range(2) for i in range(2)]
    near_blocks(flags, place8, slots, pairs, before, out, scratch)


def last_kernel(
    flags, place8, a_left, a_right, left, right, c_ends, left_c, right_c, before, out, *scratch
):
    parity = lat_parity()
    at = PTS + QUAD
    own_place, far_place = 8 - 8 * parity, 8 * parity
    slots = [
        (left, block(a_left, at, 16), own_place + 4),
        (right, block(a_right, at, 16), own_place),
        (left_c, block(c_ends, at, 16), far_place + 4),
        (right_c, block(c_ends, PTS + MSG + at, 16), far_place),
    ]
    pairs = [(s, 1 - parity, 3 * s - 1, i, s) for s in range(2) for i in range(2)]
    pairs += [(2 + s, 2 - 3 * parity, 3 * s - 1, 1 - parity, s) for s in range(2)]
    near_blocks(flags, place8, slots, pairs, before, out, scratch)


def near(kernel, name, n_slots, n_pairs, operands, chained=True, cost=None, scratch=()):
    return pl.pallas_call(
        kernel,
        in_specs=[scalars, whole] + [hbm] * (len(operands) - 2),
        out_specs=[hbm],
        out_shape=[ACC],
        scratch_shapes=near_scratch(n_slots, n_pairs) + list(scratch),
        input_output_aliases={len(operands) - 1: 0} if chained else {},
        compiler_params=params(),
        cost_estimate=cost or COST,
        name=name,
    )(*operands)


def window_sum(flags, weights, bands, first=0):
    total = None
    for base, cells in bands:
        for v in range(6):
            if cells[v // 2] is None:
                continue
            ref, offset = cells[v // 2]
            for a in range(2):
                start = offset + (2 * a + v % 2) * RANK
                hi, lo = split(ref[start : start + RANK, :])
                u = base + a
                w = 6 * u + v
                rows = []
                for leaf in range(4):
                    part_w = weights[leaf, w - first]
                    d_row = u - 2 - leaf // 2
                    d_col = v - 2 - leaf % 2
                    if abs(d_col) <= 1:
                        inside = (d_row >= -1) & (d_row <= 1)
                        flag = flags[leaf, 3 * jnp.clip(d_row + 1, 0, 2) + d_col + 1]
                        keep = 1 - jnp.where(inside, flag, 0)
                        part_w = (part_w.astype(f32) * keep.astype(f32)).astype(bf16)
                    rows.append(part_w)
                stacked = jnp.concatenate(rows, 0)
                part = mm(stacked, hi) + mm(stacked, lo)
                total = part if total is None else total + part
    return total


def far_kernel(
    n_lat, n_lon, flags, weights, own, left, right, from_y, from_c, devices, c_ends,
    dev_w, dev_t, group_w, leaf_t, out, weights_v, cells, rows_dev, dev_w_v, dev_t_v,
    group_row_w, leaf_t_v, sems,
):
    lat = lax.axis_index("lat")
    lon = lax.axis_index("lon")
    parity = lax.rem(lat, 2)
    side = lax.rem(lon, 2)
    group_row, group_col = lat // 2, lon // 2
    n_gcol = n_lon // 2
    size = 2 * n_lon * RANK
    copies = []
    for source, target in (
        (dev_w, dev_w_v),
        (devices, rows_dev.at[0]),
        (block(c_ends, 2 * (PTS + MSG), size), rows_dev.at[1]),
        (group_w.at[group_row, group_col], group_row_w),
        (dev_t, dev_t_v),
        (leaf_t, leaf_t_v),
        (block(own, PTS, QUAD), cells.at[0]),
        (block(left, PTS, QUAD), cells.at[1]),
        (block(right, PTS, QUAD), cells.at[2]),
        (block(from_y, 2 * PTS, QUAD), cells.at[3]),
        (block(from_c, 2 * PTS, QUAD), cells.at[4]),
        (block(c_ends, PTS, QUAD), cells.at[5]),
        (block(c_ends, 2 * PTS + MSG, QUAD), cells.at[6]),
        (weights.at[0], weights_v.at[0]),
        (weights.at[1], weights_v.at[1]),
        (weights.at[2], weights_v.at[2]),
        (weights.at[3], weights_v.at[3]),
    ):
        copy = pltpu.make_async_copy(source, target, sems.at[len(copies)])
        copy.start()
        copies.append(copy)
    for copy in copies[:3]:
        copy.wait()

    def device_coef(k, back, col_side):
        which = jnp.where(side == col_side, 0, 1)
        start = pl.multiple_of((4 * back + 2 * (k // 2) + which) * RANK, RANK)
        return rows_dev[k % 2, pl.ds(start, RANK), :]

    total = jnp.zeros((RANK, COLS), f32)
    for k in range(n_lat):
        other = lat + k - 2 * (lat & k)
        u = other + 2 - 2 * group_row
        for v in range(6):
            shift = 2 * group_col - 2 + v
            drop = (jnp.abs(other - lat) <= 1) & (jnp.abs(shift - lon) <= 1)
            scale = jnp.where(drop, 0.0, 1.0)
            coef = device_coef(k, (1 - v // 2) % n_gcol, v % 2)
            total = total + scale * mm2(dev_w_v[6 * u + v], coef)
    for copy in copies[3:6]:
        copy.wait()

    def group_step(step, field):
        gcol = lax.rem(group_col + step, n_gcol)
        for pair in range(n_lat // 2):
            grow = group_row + pair - 2 * (group_row & pair)
            coef = jnp.zeros((RANK, COLS), f32)
            for e in range(2):
                k = 2 * pair + e
                other = lat + k - 2 * (lat & k)
                for f in range(2):
                    cell = other * n_lon + 2 * gcol + f
                    coef = coef + mm3(dev_t_v[cell], device_coef(k, n_gcol - step, f), (0, 0))
            field = field + mm2(group_row_w[grow, gcol], coef)
        return field

    field = lax.fori_loop(2, n_gcol - 1, group_step, jnp.zeros((RANK, COLS), f32))
    total = total + mm3(dev_t_v[lat * n_lon + lon], field)
    for copy in copies[6:]:
        copy.wait()
    far = window_sum(
        flags,
        weights_v,
        (
            (2, tuple((cells.at[i], 0) for i in (1, 0, 2))),
            (4 * parity, (None, (cells.at[3], 0), None)),
            (4 - 4 * parity, tuple((cells.at[i], 0) for i in (5, 4, 6))),
        ),
    )
    for leaf in range(4):
        rows = slice(leaf * RANK, (leaf + 1) * RANK)
        out[rows, :] = far[rows, :] + mm3(leaf_t_v[leaf], total)


def far_field(n_lat, n_lon, operands):
    return pl.pallas_call(
        functools.partial(far_kernel, n_lat, n_lon),
        in_specs=[scalars] + [hbm] * 12,
        out_specs=whole,
        out_shape=shape(QUAD, COLS),
        scratch_shapes=[
            VMEM((4, 36, RANK, RANK), bf16),
            VMEM((7, QUAD, COLS), f32),
            VMEM((2, 2 * n_lon * RANK, COLS), f32),
            VMEM((36, RANK, RANK), bf16),
            VMEM((n_lat * n_lon, RANK, RANK), f32),
            VMEM((n_lat // 2, n_lon // 2, RANK, RANK), bf16),
            VMEM((4, RANK, RANK), f32),
            pltpu.SemaphoreType.DMA((17,)),
        ],
        compiler_params=params(),
        cost_estimate=LOW,
        name="far",
    )(*operands)


def down_kernel(
    flags, place8, weights, left_y, right_y, partial, basis, before, out, *scratch
):
    parity = lat_parity()
    near_refs, (weights_v, cells, basis_v, sems) = scratch[:-4], scratch[-4:]
    at = PTS + QUAD
    copies = []
    for source, target in (
        (block(left_y, PTS, QUAD), cells.at[0]),
        (block(right_y, PTS, QUAD), cells.at[1]),
        (partial, cells.at[2]),
        (weights.at[:, pl.ds(24 * parity, 12)], weights_v),
        (basis, basis_v),
    ):
        copy = pltpu.make_async_copy(source, target, sems.at[len(copies)])
        copy.start()
        copies.append(copy)

    def fill(acc, _):
        for copy in copies:
            copy.wait()
        band = (4 * parity, ((cells.at[0], 0), None, (cells.at[1], 0)))
        far = cells[2] + window_sum(flags, weights_v, (band,), 24 * parity)
        for leaf in range(4):
            acc[leaf] += mm3(basis_v[leaf], far[leaf * RANK : (leaf + 1) * RANK, :], (0, 0))

    base = 8 - 8 * parity
    slots = [
        (block(left_y, 0, PTS), block(left_y, at, 16), base + 4),
        (block(right_y, 0, PTS), block(right_y, at, 16), base),
    ]
    pairs = [(s, 3 * parity - 1, 3 * s - 1, parity, s) for s in range(2)]
    near_blocks(flags, place8, slots, pairs, before, out, near_refs, fill)


def local(
    losses,
    positions,
    leaf_basis,
    near_flags,
    leaf_coupling,
    leaf_transfer,
    device_coupling,
    device_transfer,
    group_coupling,
):
    n_lat = lax.axis_size("lat")
    n_lon = lax.axis_size("lon")

    flat = losses.reshape(4, PTS, COLS)
    basis = jnp.swapaxes(leaf_basis, 2, 3).reshape(4, RANK, PTS)
    flags = near_flags.reshape(4, 9)
    weights = leaf_coupling.reshape(4, 36, RANK, RANK)
    transfer = leaf_transfer.reshape(4, RANK, RANK)

    to_right = [(i, (i + 1) % n_lon) for i in range(n_lon)]
    to_left = [(i, (i - 1) % n_lon) for i in range(n_lon)]
    in_chip = [(i, i ^ 1) for i in range(n_lat)]
    across = [(i, i + 1 if i % 2 else i - 1) for i in range(n_lat)]
    across = [(a, b) for a, b in across if 0 <= b < n_lat]

    across_two = [(i, i ^ 2) for i in range(n_lat)]
    partner = [(i, i ^ 1) for i in range(n_lon)]
    barrier = lax.optimization_barrier

    a_right, a_left, b_right, b_left, to_y, to_c, place8, dev = coefficients(
        flat, basis, transfer, positions.reshape(4, 2, PTS)
    )
    dev_pair = lax.ppermute(dev, "lon", partner)
    from_c = lax.ppermute(to_c, "lat", in_chip)
    from_y = lax.ppermute(to_y, "lat", across)

    left = lax.ppermute(a_right, "lon", to_right)
    right = lax.ppermute(a_left, "lon", to_left)
    pair = jnp.concatenate([dev, dev_pair], 0)
    pair_two = lax.ppermute(pair, "lat", across_two)
    from_c, place8 = barrier((from_c, place8))
    (acc,) = near(own_kernel, "own", 4, 16, (flags, place8, flat, a_right), chained=False)
    from_y, pair_two, acc = barrier((from_y, pair_two, acc))
    quad = jnp.concatenate([pair, pair_two], 0)
    moved = [
        lax.ppermute(quad, "lon", [(i, (i + step) % n_lon) for i in range(n_lon)])
        for step in range(2, n_lon, 2)
    ]
    (acc,) = near(lat_kernel, "lat", 4, 8, (flags, place8, from_y, from_c, acc))
    devices = jnp.concatenate([quad, *moved], 0)
    left, right, b_right, b_left, devices, acc = barrier(
        (left, right, b_right, b_left, devices, acc)
    )
    left_b = lax.ppermute(b_right, "lon", to_right)
    right_b = lax.ppermute(b_left, "lon", to_left)
    left_y = lax.ppermute(left, "lat", across)
    right_y = lax.ppermute(right, "lat", across)
    to_c = jnp.concatenate([left, right, devices], 0)
    c_ends = lax.ppermute(to_c, "lat", in_chip)
    (acc,) = near(lon_kernel, "lon", 2, 4, (flags, place8, left, right, acc))
    c_ends, acc = barrier((c_ends, acc))
    partial = far_field(
        n_lat,
        n_lon,
        (
            flags,
            weights,
            a_right,
            left,
            right,
            from_y,
            from_c,
            devices,
            c_ends,
            device_coupling.reshape(36, RANK, RANK),
            device_transfer.reshape(n_lat * n_lon, RANK, RANK),
            group_coupling,
            transfer,
        ),
    )
    left_y, right_y, partial = barrier((left_y, right_y, partial))
    (acc,) = near(
        down_kernel,
        "down",
        2,
        2,
        (flags, place8, weights, left_y, right_y, partial, basis, acc),
        cost=LOW,
        scratch=[
            VMEM((4, 12, RANK, RANK), bf16),
            VMEM((3, QUAD, COLS), f32),
            VMEM((4, RANK, PTS), f32),
            pltpu.SemaphoreType.DMA((5,)),
        ],
    )
    left_b, right_b, acc = barrier((left_b, right_b, acc))
    left_c = lax.ppermute(left_b, "lat", in_chip)
    right_c = lax.ppermute(right_b, "lat", in_chip)
    (acc,) = near(
        last_kernel,
        "last",
        4,
        6,
        (flags, place8, left, right, left_b, right_b, c_ends, left_c, right_c, acc),
    )
    return acc.reshape(2, 2, PTS, COLS)


def solution(mesh):
    placed = (
        P("lat", "lon", None, None),
        P("lat", "lon", None, None),
        P("lat", "lon", None, None),
        P("lat", "lon", None),
        P("lat", "lon", None, None, None),
        P("lat", "lon", None, None),
        P("lat", "lon", None, None, None),
        P(),
        P(),
    )
    return jax.shard_map(
        local, mesh=mesh, in_specs=placed, out_specs=P("lat", "lon", None, None), check_vma=False
    )
```

```python
import functools

import jax
import jax.numpy as jnp
from jax import lax
from jax.experimental import pallas as pl
from jax.experimental.pallas import tpu as pltpu
from jax.sharding import PartitionSpec as P

PTS = 512
RANK = 64
COLS = 256
HALF = 256
QUAD = 4 * RANK
MSG = QUAD + 16

LN2 = 0.6931471805599453
UNIT = 1.7320508075688772 / 0.15 / LN2

f32 = jnp.float32
bf16 = jnp.bfloat16
VMEM = pltpu.VMEM
SMEM = pltpu.SMEM
whole = pl.BlockSpec(memory_space=VMEM)
scalars = pl.BlockSpec(memory_space=SMEM)


def split(x):
    hi = x.astype(bf16)
    return hi, (x - hi.astype(f32)).astype(bf16)


def mm(a, b, dims=(1, 0)):
    return lax.dot_general(
        a, b, (((dims[0],), (dims[1],)), ((), ())), preferred_element_type=f32
    )


def mm3(a, b, dims=(1, 0)):
    a_hi, a_lo = split(a)
    b_hi, b_lo = split(b)
    return mm(a_hi, b_hi, dims) + (mm(a_lo, b_hi, dims) + mm(a_hi, b_lo, dims))


def mm2(a, b):
    b_hi, b_lo = split(b)
    return mm(a, b_hi) + mm(a, b_lo)


def params(limit=64):
    return pltpu.CompilerParams(vmem_limit_bytes=limit * 1024 * 1024)


COST = pl.CostEstimate(flops=20_000_000_000, bytes_accessed=4_000_000, transcendentals=0)
LOW = pl.CostEstimate(flops=1_000, bytes_accessed=1_000, transcendentals=0)


def shape(*dims):
    return jax.ShapeDtypeStruct(dims, f32)


def lat_parity():
    return lax.rem(lax.axis_index("lat"), 2)


def coef_kernel(
    loss, basis, transfer, pos, a_right, a_left, b_right, b_left, to_y, to_c, place8, dev,
    values, bases, message, sems, load_sems,
):
    parity = lat_parity()
    loads = [
        (
            pltpu.make_async_copy(loss.at[leaf], values.at[leaf], load_sems.at[leaf]),
            pltpu.make_async_copy(basis.at[leaf], bases.at[leaf], load_sems.at[4 + leaf]),
        )
        for leaf in range(4)
    ]
    for pair in loads:
        for copy in pair:
            copy.start()
    for leaf in range(4):
        place = pos[leaf] * UNIT
        place8[leaf] = jnp.concatenate([place, jnp.zeros((6, PTS), f32)], 0)
        for coord in range(2):
            for half in range(2):
                at = QUAD + 4 * leaf + 2 * coord + half
                message[at : at + 1, :] = place[coord : coord + 1, half * HALF : (half + 1) * HALF]
    for pair in loads:
        for copy in pair:
            copy.wait()
    y_row, c_row = 2 * parity, 2 - 2 * parity
    first, second = slice(0, PTS), slice(PTS, 2 * PTS)
    copies = []
    for source, target in (
        (y_row + 1, a_right.at[first]),
        (y_row, a_left.at[first]),
        (c_row + 1, b_right),
        (c_row, b_left),
        (y_row, to_y.at[first]),
        (y_row + 1, to_y.at[second]),
        (c_row, to_c.at[first]),
        (c_row + 1, to_c.at[second]),
    ):
        copy = pltpu.make_async_copy(values.at[source], target, sems.at[len(copies)])
        copy.start()
        copies.append(copy)
    total = None
    for leaf in range(4):
        l_hi, l_lo = split(values[leaf])
        b_hi, b_lo = split(bases[leaf])
        coef = mm(b_hi, l_hi) + (mm(b_lo, l_hi) + mm(b_hi, l_lo))
        message[leaf * RANK : (leaf + 1) * RANK, :] = coef
        part = mm3(transfer[leaf], coef, (0, 0))
        total = part if leaf == 0 else total + part
    dev[...] = total
    for target in (
        a_right.at[PTS:], a_left.at[PTS:], to_y.at[2 * PTS :], to_c.at[2 * PTS :]
    ):
        copy = pltpu.make_async_copy(message, target, sems.at[len(copies)])
        copy.start()
        copies.append(copy)
    for copy in copies:
        copy.wait()


hbm = pl.BlockSpec(memory_space=pl.ANY)


def coefficients(losses, basis, transfer, positions):
    return pl.pallas_call(
        coef_kernel,
        in_specs=[hbm, hbm, whole, whole],
        out_specs=[hbm] * 6 + [whole] * 2,
        out_shape=[
            shape(PTS + MSG, COLS),
            shape(PTS + MSG, COLS),
            shape(PTS, COLS),
            shape(PTS, COLS),
            shape(2 * PTS + MSG, COLS),
            shape(2 * PTS + MSG, COLS),
            shape(4, 8, PTS),
            shape(RANK, COLS),
        ],
        scratch_shapes=[
            VMEM((4, PTS, COLS), f32),
            VMEM((4, RANK, PTS), f32),
            VMEM((MSG, COLS), f32),
            pltpu.SemaphoreType.DMA((12,)),
            pltpu.SemaphoreType.DMA((8,)),
        ],
        compiler_params=params(),
        cost_estimate=COST,
        name="coefs",
    )(losses, basis, transfer, positions)


def near_scratch(n_slots, n_pairs):
    return [
        SMEM((n_pairs + 1, 8), jnp.int32),
        VMEM((4, PTS, 8), f32),
        VMEM((n_slots, 8, PTS), f32),
        VMEM((n_slots, 2 * PTS, COLS), bf16),
        VMEM((PTS, 2 * PTS), bf16),
        VMEM((PTS, 2 * PTS), bf16),
        VMEM((4, PTS, COLS), f32),
        VMEM((n_slots, PTS, COLS), f32),
        VMEM((n_slots, 16, COLS), f32),
        pltpu.SemaphoreType.DMA((8 + 2 * n_slots,)),
    ]


def near_blocks(flags, place8, slots, pairs, before, out, scratch, fill=None):
    table, tpos, spos, stack, kern_a, kern_b, acc, stage, marks, sems = scratch
    arrivals = []
    for slot, (values, places, _) in enumerate(slots):
        pair = (
            pltpu.make_async_copy(values, stage.at[slot], sems.at[8 + 2 * slot]),
            pltpu.make_async_copy(places, marks.at[slot], sems.at[9 + 2 * slot]),
        )
        for copy in pair:
            copy.start()
        arrivals.append(pair)
    loads = []
    if before is not None:
        loads = [
            pltpu.make_async_copy(before.at[leaf], acc.at[leaf], sems.at[leaf])
            for leaf in range(4)
        ]
    for copy in loads:
        copy.start()
    for leaf in range(4):
        tpos[leaf] = place8[leaf].T
    for slot, (_, _, base) in enumerate(slots):
        for copy in arrivals[slot]:
            copy.wait()
        hi, lo = split(stage[slot])
        stack[slot, :PTS, :] = hi
        stack[slot, PTS:, :] = lo
        for coord in range(2):
            for half in range(2):
                spos[slot, coord : coord + 1, half * HALF : (half + 1) * HALF] = marks[
                    slot, pl.ds(base + 2 * coord + half, 1), :
                ]
    count = 0
    for slot, row, col, own_row, own_col in pairs:
        target = 2 * own_row + own_col
        table[count, 0] = slot
        table[count, 1] = target
        table[count, 2] = row - own_row
        table[count, 3] = col - own_col
        flag = flags[target, 3 * (row - own_row + 1) + col - own_col + 1]
        count = count + jnp.where(flag > 0, 1, 0)

    def evaluate(index, half, kern):
        slot, target = table[index, 0], table[index, 1]
        src_row = spos[slot, 0:1, :] + table[index, 2].astype(f32) * UNIT
        src_col = spos[slot, 1:2, :] + table[index, 3].astype(f32) * UNIT
        part = slice(half * HALF, (half + 1) * HALF)
        d_row = tpos[target, part, 0:1] - src_row
        d_col = tpos[target, part, 1:2] - src_col
        square = d_row * d_row + d_col * d_col
        dist = square * lax.rsqrt(jnp.maximum(square, 1e-30))
        decay = jnp.exp2(-dist)
        hi, lo = split(decay + decay * (dist * LN2))
        kern[part, :PTS] = hi
        kern[part, PTS:] = lo

    def apply(index, half, kern):
        slot, target = table[index, 0], table[index, 1]
        part = slice(half * HALF, (half + 1) * HALF)
        l_hi = stack[slot, :PTS, :]
        l_lo = stack[slot, PTS:, :]
        k_hi = kern[part, :PTS]
        k_lo = kern[part, PTS:]
        acc[target, part, :] += mm(k_hi, l_hi) + mm(k_lo, l_hi) + mm(k_hi, l_lo)

    def step(index, kern, other):
        following = jnp.minimum(index + 1, count - 1)
        for half in range(2):
            evaluate(following, half, other)
            apply(index, half, kern)

    @pl.when(count > 0)
    def _():
        for half in range(2):
            evaluate(0, half, kern_a)

    for copy in loads:
        copy.wait()
    if fill is not None:
        fill(acc, stage)

    @pl.loop(0, (count + 1) // 2)
    def _(pair):
        step(2 * pair, kern_a, kern_b)

        @pl.when(2 * pair + 1 < count)
        def _():
            step(2 * pair + 1, kern_b, kern_a)


    stores = [
        pltpu.make_async_copy(acc.at[leaf], out.at[leaf], sems.at[4 + leaf]) for leaf in range(4)
    ]
    for copy in stores:
        copy.start()
    for copy in stores:
        copy.wait()


ACC = shape(4, PTS, COLS)


def block(ref, start, rows):
    return ref.at[pl.ds(start, rows)]


def own_kernel(flags, place8, loss, msg, out, *scratch):
    slots = [(loss.at[leaf], block(msg, PTS + QUAD, 16), 4 * leaf) for leaf in range(4)]
    pairs = [(s, s // 2, s % 2, t // 2, t % 2) for s in range(4) for t in range(4)]

    def fill(acc, losses):
        for leaf in range(4):
            acc[leaf] = 0.5 * losses[leaf]

    near_blocks(flags, place8, slots, pairs, None, out, scratch, fill)


def lat_kernel(flags, place8, from_y, from_c, before, out, *scratch):
    parity = lat_parity()
    slots, pairs = [], []
    for ref, place, row, own_row in (
        (from_y, 8 - 8 * parity, 3 * parity - 1, parity),
        (from_c, 8 * parity, 2 - 3 * parity, 1 - parity),
    ):
        for col in range(2):
            for own_col in range(2):
                pairs.append((len(slots), row, col, own_row, own_col))
            slots.append(
                (block(ref, col * PTS, PTS), block(ref, 2 * PTS + QUAD, 16), place + 4 * col)
            )
    near_blocks(flags, place8, slots, pairs, before, out, scratch)


def lon_kernel(flags, place8, left, right, before, out, *scratch):
    parity = lat_parity()
    at = PTS + QUAD
    slots = [
        (block(left, 0, PTS), block(left, at, 16), 8 * parity + 4),
        (block(right, 0, PTS), block(right, at, 16), 8 * parity),
    ]
    pairs = [(s, parity, 3 * s - 1, i, s) for s in range(2) for i in range(2)]
    near_blocks(flags, place8, slots, pairs, before, out, scratch)


def last_kernel(
    flags, place8, a_left, a_right, left, right, c_ends, left_c, right_c, before, out, *scratch
):
    parity = lat_parity()
    at = PTS + QUAD
    own_place, far_place = 8 - 8 * parity, 8 * parity
    slots = [
        (left, block(a_left, at, 16), own_place + 4),
        (right, block(a_right, at, 16), own_place),
        (left_c, block(c_ends, QUAD, 16), far_place + 4),
        (right_c, block(c_ends, MSG + QUAD, 16), far_place),
    ]
    pairs = [(s, 1 - parity, 3 * s - 1, i, s) for s in range(2) for i in range(2)]
    pairs += [(2 + s, 2 - 3 * parity, 3 * s - 1, 1 - parity, s) for s in range(2)]
    near_blocks(flags, place8, slots, pairs, before, out, scratch)


def near(kernel, name, n_slots, n_pairs, operands, chained=True, cost=None, scratch=()):
    return pl.pallas_call(
        kernel,
        in_specs=[scalars, whole] + [hbm] * (len(operands) - 2),
        out_specs=[hbm],
        out_shape=[ACC],
        scratch_shapes=near_scratch(n_slots, n_pairs) + list(scratch),
        input_output_aliases={len(operands) - 1: 0} if chained else {},
        compiler_params=params(),
        cost_estimate=cost or COST,
        name=name,
    )(*operands)


def window_sum(flags, weights, bands, first=0):
    total = None
    for base, cells in bands:
        for v in range(6):
            if cells[v // 2] is None:
                continue
            ref, offset = cells[v // 2]
            for a in range(2):
                start = offset + (2 * a + v % 2) * RANK
                hi, lo = split(ref[start : start + RANK, :])
                u = base + a
                w = 6 * u + v
                rows = []
                for leaf in range(4):
                    part_w = weights[leaf, w - first]
                    d_row = u - 2 - leaf // 2
                    d_col = v - 2 - leaf % 2
                    if abs(d_col) <= 1:
                        inside = (d_row >= -1) & (d_row <= 1)
                        flag = flags[leaf, 3 * jnp.clip(d_row + 1, 0, 2) + d_col + 1]
                        keep = 1 - jnp.where(inside, flag, 0)
                        part_w = (part_w.astype(f32) * keep.astype(f32)).astype(bf16)
                    rows.append(part_w)
                stacked = jnp.concatenate(rows, 0)
                part = mm(stacked, hi) + mm(stacked, lo)
                total = part if total is None else total + part
    return total


def far_kernel(
    n_lat, n_lon, flags, weights, own, left, right, from_y, from_c, devices, c_ends,
    dev_w, dev_t, group_w, leaf_t, out, weights_v, cells, rows_dev, dev_w_v, dev_t_v,
    group_row_w, leaf_t_v, sems,
):
    lat = lax.axis_index("lat")
    lon = lax.axis_index("lon")
    parity = lax.rem(lat, 2)
    side = lax.rem(lon, 2)
    group_row, group_col = lat // 2, lon // 2
    n_gcol = n_lon // 2
    size = 2 * n_lon * RANK
    copies = []
    for source, target in (
        (dev_w, dev_w_v),
        (block(devices, 2 * MSG, size), rows_dev.at[0]),
        (block(c_ends, 2 * MSG, size), rows_dev.at[1]),
        (group_w.at[group_row, group_col], group_row_w),
        (dev_t, dev_t_v),
        (leaf_t, leaf_t_v),
        (block(own, PTS, QUAD), cells.at[0]),
        (block(left, PTS, QUAD), cells.at[1]),
        (block(right, PTS, QUAD), cells.at[2]),
        (block(from_y, 2 * PTS, QUAD), cells.at[3]),
        (block(from_c, 2 * PTS, QUAD), cells.at[4]),
        (block(c_ends, 0, QUAD), cells.at[5]),
        (block(c_ends, MSG, QUAD), cells.at[6]),
        (weights.at[0], weights_v.at[0]),
        (weights.at[1], weights_v.at[1]),
        (weights.at[2], weights_v.at[2]),
        (weights.at[3], weights_v.at[3]),
    ):
        copy = pltpu.make_async_copy(source, target, sems.at[len(copies)])
        copy.start()
        copies.append(copy)
    for copy in copies[:3]:
        copy.wait()

    def device_coef(k, back, col_side):
        which = jnp.where(side == col_side, 0, 1)
        start = pl.multiple_of((4 * back + 2 * (k // 2) + which) * RANK, RANK)
        return rows_dev[k % 2, pl.ds(start, RANK), :]

    total = jnp.zeros((RANK, COLS), f32)
    for k in range(n_lat):
        other = lat + k - 2 * (lat & k)
        u = other + 2 - 2 * group_row
        for v in range(6):
            shift = 2 * group_col - 2 + v
            drop = (jnp.abs(other - lat) <= 1) & (jnp.abs(shift - lon) <= 1)
            scale = jnp.where(drop, 0.0, 1.0)
            coef = device_coef(k, (1 - v // 2) % n_gcol, v % 2)
            total = total + scale * mm2(dev_w_v[6 * u + v], coef)
    for copy in copies[3:6]:
        copy.wait()

    def group_step(step, field):
        gcol = lax.rem(group_col + step, n_gcol)
        for pair in range(n_lat // 2):
            grow = group_row + pair - 2 * (group_row & pair)
            coef = jnp.zeros((RANK, COLS), f32)
            for e in range(2):
                k = 2 * pair + e
                other = lat + k - 2 * (lat & k)
                for f in range(2):
                    cell = other * n_lon + 2 * gcol + f
                    coef = coef + mm3(dev_t_v[cell], device_coef(k, n_gcol - step, f), (0, 0))
            field = field + mm2(group_row_w[grow, gcol], coef)
        return field

    field = lax.fori_loop(2, n_gcol - 1, group_step, jnp.zeros((RANK, COLS), f32))
    total = total + mm3(dev_t_v[lat * n_lon + lon], field)
    for copy in copies[6:]:
        copy.wait()
    far = window_sum(
        flags,
        weights_v,
        (
            (2, tuple((cells.at[i], 0) for i in (1, 0, 2))),
            (4 * parity, (None, (cells.at[3], 0), None)),
            (4 - 4 * parity, tuple((cells.at[i], 0) for i in (5, 4, 6))),
        ),
    )
    for leaf in range(4):
        rows = slice(leaf * RANK, (leaf + 1) * RANK)
        out[rows, :] = far[rows, :] + mm3(leaf_t_v[leaf], total)


def far_field(n_lat, n_lon, operands):
    return pl.pallas_call(
        functools.partial(far_kernel, n_lat, n_lon),
        in_specs=[scalars] + [hbm] * 12,
        out_specs=whole,
        out_shape=shape(QUAD, COLS),
        scratch_shapes=[
            VMEM((4, 36, RANK, RANK), bf16),
            VMEM((7, QUAD, COLS), f32),
            VMEM((2, 2 * n_lon * RANK, COLS), f32),
            VMEM((36, RANK, RANK), bf16),
            VMEM((n_lat * n_lon, RANK, RANK), f32),
            VMEM((n_lat // 2, n_lon // 2, RANK, RANK), bf16),
            VMEM((4, RANK, RANK), f32),
            pltpu.SemaphoreType.DMA((17,)),
        ],
        compiler_params=params(),
        cost_estimate=LOW,
        name="far",
    )(*operands)


def pack_kernel(*refs):
    parts, (out, sems) = refs[:-2], refs[-2:]
    copies = []
    row = 0
    for index, part in enumerate(parts):
        source = block(part, PTS, MSG) if index < 2 else part
        size = source.shape[0]
        copies.append(pltpu.make_async_copy(source, block(out, row, size), sems.at[index]))
        copies[-1].start()
        row += size
    for copy in copies:
        copy.wait()


def pack(left, right, devices):
    parts = [left, right, *devices]
    rows = 2 * MSG + sum(part.shape[0] for part in devices)
    return pl.pallas_call(
        pack_kernel,
        in_specs=[hbm] * len(parts),
        out_specs=whole,
        out_shape=shape(rows, COLS),
        scratch_shapes=[pltpu.SemaphoreType.DMA((len(parts),))],
        compiler_params=params(),
        cost_estimate=LOW,
        name="pack",
    )(*parts)


def down_kernel(
    flags, place8, weights, left_y, right_y, partial, basis, before, out, *scratch
):
    parity = lat_parity()
    near_refs, (weights_v, cells, basis_v, sems) = scratch[:-4], scratch[-4:]
    at = PTS + QUAD
    copies = []
    for source, target in (
        (block(left_y, PTS, QUAD), cells.at[0]),
        (block(right_y, PTS, QUAD), cells.at[1]),
        (partial, cells.at[2]),
        (weights.at[:, pl.ds(24 * parity, 12)], weights_v),
        (basis, basis_v),
    ):
        copy = pltpu.make_async_copy(source, target, sems.at[len(copies)])
        copy.start()
        copies.append(copy)

    def fill(acc, _):
        for copy in copies:
            copy.wait()
        band = (4 * parity, ((cells.at[0], 0), None, (cells.at[1], 0)))
        far = cells[2] + window_sum(flags, weights_v, (band,), 24 * parity)
        for leaf in range(4):
            acc[leaf] += mm3(basis_v[leaf], far[leaf * RANK : (leaf + 1) * RANK, :], (0, 0))

    base = 8 - 8 * parity
    slots = [
        (block(left_y, 0, PTS), block(left_y, at, 16), base + 4),
        (block(right_y, 0, PTS), block(right_y, at, 16), base),
    ]
    pairs = [(s, 3 * parity - 1, 3 * s - 1, parity, s) for s in range(2)]
    near_blocks(flags, place8, slots, pairs, before, out, near_refs, fill)


def local(
    losses,
    positions,
    leaf_basis,
    near_flags,
    leaf_coupling,
    leaf_transfer,
    device_coupling,
    device_transfer,
    group_coupling,
):
    n_lat = lax.axis_size("lat")
    n_lon = lax.axis_size("lon")

    flat = losses.reshape(4, PTS, COLS)
    basis = jnp.swapaxes(leaf_basis, 2, 3).reshape(4, RANK, PTS)
    flags = near_flags.reshape(4, 9)
    weights = leaf_coupling.reshape(4, 36, RANK, RANK)
    transfer = leaf_transfer.reshape(4, RANK, RANK)

    to_right = [(i, (i + 1) % n_lon) for i in range(n_lon)]
    to_left = [(i, (i - 1) % n_lon) for i in range(n_lon)]
    in_chip = [(i, i ^ 1) for i in range(n_lat)]
    across = [(i, i + 1 if i % 2 else i - 1) for i in range(n_lat)]
    across = [(a, b) for a, b in across if 0 <= b < n_lat]

    across_two = [(i, i ^ 2) for i in range(n_lat)]
    partner = [(i, i ^ 1) for i in range(n_lon)]
    barrier = lax.optimization_barrier

    a_right, a_left, b_right, b_left, to_y, to_c, place8, dev = coefficients(
        flat, basis, transfer, positions.reshape(4, 2, PTS)
    )
    dev_pair = lax.ppermute(dev, "lon", partner)
    from_c = lax.ppermute(to_c, "lat", in_chip)
    dev_pair, to_y = barrier((dev_pair, to_y))
    from_y = lax.ppermute(to_y, "lat", across)

    left = lax.ppermute(a_right, "lon", to_right)
    right = lax.ppermute(a_left, "lon", to_left)
    pair = jnp.concatenate([dev, dev_pair], 0)
    pair_two = lax.ppermute(pair, "lat", across_two)
    from_c, place8 = barrier((from_c, place8))
    (acc,) = near(own_kernel, "own", 4, 16, (flags, place8, flat, a_right), chained=False)
    from_y, pair_two, acc = barrier((from_y, pair_two, acc))
    quad = jnp.concatenate([pair, pair_two], 0)
    moved = [
        lax.ppermute(quad, "lon", [(i, (i + step) % n_lon) for i in range(n_lon)])
        for step in range(2, n_lon, 2)
    ]
    (acc,) = near(lat_kernel, "lat", 4, 8, (flags, place8, from_y, from_c, acc))
    left, right, b_right, b_left, quad, acc, *moved = barrier(
        (left, right, b_right, b_left, quad, acc, *moved)
    )
    left_b = lax.ppermute(b_right, "lon", to_right)
    right_b = lax.ppermute(b_left, "lon", to_left)
    left_y = lax.ppermute(left, "lat", across)
    right_y = lax.ppermute(right, "lat", across)
    to_c = pack(left, right, (quad, *moved))
    c_ends = lax.ppermute(to_c, "lat", in_chip)
    (acc,) = near(lon_kernel, "lon", 2, 4, (flags, place8, left, right, acc))
    c_ends, acc = barrier((c_ends, acc))
    partial = far_field(
        n_lat,
        n_lon,
        (
            flags,
            weights,
            a_right,
            left,
            right,
            from_y,
            from_c,
            to_c,
            c_ends,
            device_coupling.reshape(36, RANK, RANK),
            device_transfer.reshape(n_lat * n_lon, RANK, RANK),
            group_coupling,
            transfer,
        ),
    )
    left_y, right_y, partial = barrier((left_y, right_y, partial))
    (acc,) = near(
        down_kernel,
        "down",
        2,
        2,
        (flags, place8, weights, left_y, right_y, partial, basis, acc),
        cost=LOW,
        scratch=[
            VMEM((4, 12, RANK, RANK), bf16),
            VMEM((3, QUAD, COLS), f32),
            VMEM((4, RANK, PTS), f32),
            pltpu.SemaphoreType.DMA((5,)),
        ],
    )
    left_b, right_b, acc = barrier((left_b, right_b, acc))
    left_c = lax.ppermute(left_b, "lat", in_chip)
    right_c = lax.ppermute(right_b, "lat", in_chip)
    (acc,) = near(
        last_kernel,
        "last",
        4,
        6,
        (flags, place8, left, right, left_b, right_b, c_ends, left_c, right_c, acc),
    )
    return acc.reshape(2, 2, PTS, COLS)


def solution(mesh):
    placed = (
        P("lat", "lon", None, None),
        P("lat", "lon", None, None),
        P("lat", "lon", None, None),
        P("lat", "lon", None),
        P("lat", "lon", None, None, None),
        P("lat", "lon", None, None),
        P("lat", "lon", None, None, None),
        P(),
        P(),
    )
    return jax.shard_map(
        local, mesh=mesh, in_specs=placed, out_specs=P("lat", "lon", None, None), check_vma=False
    )
```

```python
import functools

import jax
import jax.numpy as jnp
from jax import lax
from jax.experimental import pallas as pl
from jax.experimental.pallas import tpu as pltpu
from jax.sharding import PartitionSpec as P

PTS = 512
RANK = 64
COLS = 256
HALF = 256
QUAD = 4 * RANK
MSG = QUAD + 16

LN2 = 0.6931471805599453
UNIT = 1.7320508075688772 / 0.15 / LN2

f32 = jnp.float32
bf16 = jnp.bfloat16
VMEM = pltpu.VMEM
SMEM = pltpu.SMEM
whole = pl.BlockSpec(memory_space=VMEM)
scalars = pl.BlockSpec(memory_space=SMEM)


def split(x):
    hi = x.astype(bf16)
    return hi, (x - hi.astype(f32)).astype(bf16)


def mm(a, b, dims=(1, 0)):
    return lax.dot_general(
        a, b, (((dims[0],), (dims[1],)), ((), ())), preferred_element_type=f32
    )


def mm3(a, b, dims=(1, 0)):
    a_hi, a_lo = split(a)
    b_hi, b_lo = split(b)
    return mm(a_hi, b_hi, dims) + (mm(a_lo, b_hi, dims) + mm(a_hi, b_lo, dims))


def mm2(a, b):
    b_hi, b_lo = split(b)
    return mm(a, b_hi) + mm(a, b_lo)


def params(limit=64):
    return pltpu.CompilerParams(vmem_limit_bytes=limit * 1024 * 1024)


COST = pl.CostEstimate(flops=20_000_000_000, bytes_accessed=4_000_000, transcendentals=0)
LOW = pl.CostEstimate(flops=1_000, bytes_accessed=1_000, transcendentals=0)


def shape(*dims):
    return jax.ShapeDtypeStruct(dims, f32)


def lat_parity():
    return lax.rem(lax.axis_index("lat"), 2)


def coef_kernel(
    loss, basis, transfer, pos, a_right, a_left, b_right, b_left, to_y, to_c, place8, dev,
    values, bases, message, sems, load_sems,
):
    parity = lat_parity()
    loads = [
        (
            pltpu.make_async_copy(loss.at[leaf], values.at[leaf], load_sems.at[leaf]),
            pltpu.make_async_copy(basis.at[leaf], bases.at[leaf], load_sems.at[4 + leaf]),
        )
        for leaf in range(4)
    ]
    for pair in loads:
        for copy in pair:
            copy.start()
    for leaf in range(4):
        place = pos[leaf] * UNIT
        place8[leaf] = jnp.concatenate([place, jnp.zeros((6, PTS), f32)], 0)
        for coord in range(2):
            for half in range(2):
                at = QUAD + 4 * leaf + 2 * coord + half
                message[at : at + 1, :] = place[coord : coord + 1, half * HALF : (half + 1) * HALF]
    for pair in loads:
        for copy in pair:
            copy.wait()
    y_row, c_row = 2 * parity, 2 - 2 * parity
    first, second = slice(0, PTS), slice(PTS, 2 * PTS)
    copies = []
    for source, target in (
        (y_row + 1, a_right.at[first]),
        (y_row, a_left.at[first]),
        (c_row + 1, b_right),
        (c_row, b_left),
        (y_row, to_y.at[first]),
        (y_row + 1, to_y.at[second]),
        (c_row, to_c.at[first]),
        (c_row + 1, to_c.at[second]),
    ):
        copy = pltpu.make_async_copy(values.at[source], target, sems.at[len(copies)])
        copy.start()
        copies.append(copy)
    total = None
    for leaf in range(4):
        l_hi, l_lo = split(values[leaf])
        b_hi, b_lo = split(bases[leaf])
        coef = mm(b_hi, l_hi) + (mm(b_lo, l_hi) + mm(b_hi, l_lo))
        message[leaf * RANK : (leaf + 1) * RANK, :] = coef
        part = mm3(transfer[leaf], coef, (0, 0))
        total = part if leaf == 0 else total + part
    dev[...] = total
    for target in (
        a_right.at[PTS:], a_left.at[PTS:], to_y.at[2 * PTS :], to_c.at[2 * PTS :]
    ):
        copy = pltpu.make_async_copy(message, target, sems.at[len(copies)])
        copy.start()
        copies.append(copy)
    for copy in copies:
        copy.wait()


hbm = pl.BlockSpec(memory_space=pl.ANY)


def coefficients(losses, basis, transfer, positions):
    return pl.pallas_call(
        coef_kernel,
        in_specs=[hbm, hbm, whole, whole],
        out_specs=[hbm] * 6 + [whole] * 2,
        out_shape=[
            shape(PTS + MSG, COLS),
            shape(PTS + MSG, COLS),
            shape(PTS, COLS),
            shape(PTS, COLS),
            shape(2 * PTS + MSG, COLS),
            shape(2 * PTS + MSG, COLS),
            shape(4, 8, PTS),
            shape(RANK, COLS),
        ],
        scratch_shapes=[
            VMEM((4, PTS, COLS), f32),
            VMEM((4, RANK, PTS), f32),
            VMEM((MSG, COLS), f32),
            pltpu.SemaphoreType.DMA((12,)),
            pltpu.SemaphoreType.DMA((8,)),
        ],
        compiler_params=params(),
        cost_estimate=COST,
        name="coefs",
    )(losses, basis, transfer, positions)


def near_scratch(n_slots, n_pairs):
    return [
        SMEM((n_pairs + 1, 8), jnp.int32),
        VMEM((4, PTS, 8), f32),
        VMEM((n_slots, 8, PTS), f32),
        VMEM((n_slots, 2 * PTS, COLS), bf16),
        VMEM((PTS, 2 * PTS), bf16),
        VMEM((PTS, 2 * PTS), bf16),
        VMEM((4, PTS, COLS), f32),
        VMEM((n_slots, PTS, COLS), f32),
        VMEM((n_slots, 16, COLS), f32),
        pltpu.SemaphoreType.DMA((8 + 2 * n_slots,)),
    ]


def near_blocks(flags, place8, slots, pairs, before, out, scratch, fill=None):
    table, tpos, spos, stack, kern_a, kern_b, acc, stage, marks, sems = scratch
    arrivals = []
    for slot, (values, places, _) in enumerate(slots):
        pair = (
            pltpu.make_async_copy(values, stage.at[slot], sems.at[8 + 2 * slot]),
            pltpu.make_async_copy(places, marks.at[slot], sems.at[9 + 2 * slot]),
        )
        for copy in pair:
            copy.start()
        arrivals.append(pair)
    loads = []
    if before is not None:
        loads = [
            pltpu.make_async_copy(before.at[leaf], acc.at[leaf], sems.at[leaf])
            for leaf in range(4)
        ]
    for copy in loads:
        copy.start()
    for leaf in range(4):
        tpos[leaf] = place8[leaf].T
    for slot, (_, _, base) in enumerate(slots):
        for copy in arrivals[slot]:
            copy.wait()
        hi, lo = split(stage[slot])
        stack[slot, :PTS, :] = hi
        stack[slot, PTS:, :] = lo
        for coord in range(2):
            for half in range(2):
                spos[slot, coord : coord + 1, half * HALF : (half + 1) * HALF] = marks[
                    slot, pl.ds(base + 2 * coord + half, 1), :
                ]
    count = 0
    for slot, row, col, own_row, own_col in pairs:
        target = 2 * own_row + own_col
        table[count, 0] = slot
        table[count, 1] = target
        table[count, 2] = row - own_row
        table[count, 3] = col - own_col
        flag = flags[target, 3 * (row - own_row + 1) + col - own_col + 1]
        count = count + jnp.where(flag > 0, 1, 0)

    def evaluate(index, half, kern):
        slot, target = table[index, 0], table[index, 1]
        src_row = spos[slot, 0:1, :] + table[index, 2].astype(f32) * UNIT
        src_col = spos[slot, 1:2, :] + table[index, 3].astype(f32) * UNIT
        part = slice(half * HALF, (half + 1) * HALF)
        d_row = tpos[target, part, 0:1] - src_row
        d_col = tpos[target, part, 1:2] - src_col
        square = d_row * d_row + d_col * d_col
        dist = square * lax.rsqrt(jnp.maximum(square, 1e-30))
        decay = jnp.exp2(-dist)
        hi, lo = split(decay + decay * (dist * LN2))
        kern[part, :PTS] = hi
        kern[part, PTS:] = lo

    def apply(index, half, kern):
        slot, target = table[index, 0], table[index, 1]
        part = slice(half * HALF, (half + 1) * HALF)
        l_hi = stack[slot, :PTS, :]
        l_lo = stack[slot, PTS:, :]
        k_hi = kern[part, :PTS]
        k_lo = kern[part, PTS:]
        acc[target, part, :] += mm(k_hi, l_hi) + mm(k_lo, l_hi) + mm(k_hi, l_lo)

    def step(index, kern, other):
        following = jnp.minimum(index + 1, count - 1)
        for half in range(2):
            evaluate(following, half, other)
            apply(index, half, kern)

    @pl.when(count > 0)
    def _():
        for half in range(2):
            evaluate(0, half, kern_a)

    for copy in loads:
        copy.wait()
    if fill is not None:
        fill(acc, stage)

    @pl.loop(0, (count + 1) // 2)
    def _(pair):
        step(2 * pair, kern_a, kern_b)

        @pl.when(2 * pair + 1 < count)
        def _():
            step(2 * pair + 1, kern_b, kern_a)


    stores = [
        pltpu.make_async_copy(acc.at[leaf], out.at[leaf], sems.at[4 + leaf]) for leaf in range(4)
    ]
    for copy in stores:
        copy.start()
    for copy in stores:
        copy.wait()


ACC = shape(4, PTS, COLS)


def block(ref, start, rows):
    return ref.at[pl.ds(start, rows)]


def own_kernel(flags, place8, loss, msg, out, *scratch):
    slots = [(loss.at[leaf], block(msg, PTS + QUAD, 16), 4 * leaf) for leaf in range(4)]
    pairs = [(s, s // 2, s % 2, t // 2, t % 2) for s in range(4) for t in range(4)]

    def fill(acc, losses):
        for leaf in range(4):
            acc[leaf] = 0.5 * losses[leaf]

    near_blocks(flags, place8, slots, pairs, None, out, scratch, fill)


def lat_kernel(flags, place8, from_y, from_c, before, out, *scratch):
    parity = lat_parity()
    slots, pairs = [], []
    for ref, place, row, own_row in (
        (from_y, 8 - 8 * parity, 3 * parity - 1, parity),
        (from_c, 8 * parity, 2 - 3 * parity, 1 - parity),
    ):
        for col in range(2):
            for own_col in range(2):
                pairs.append((len(slots), row, col, own_row, own_col))
            slots.append(
                (block(ref, col * PTS, PTS), block(ref, 2 * PTS + QUAD, 16), place + 4 * col)
            )
    near_blocks(flags, place8, slots, pairs, before, out, scratch)


def lon_kernel(flags, place8, left, right, before, out, *scratch):
    parity = lat_parity()
    at = PTS + QUAD
    slots = [
        (block(left, 0, PTS), block(left, at, 16), 8 * parity + 4),
        (block(right, 0, PTS), block(right, at, 16), 8 * parity),
    ]
    pairs = [(s, parity, 3 * s - 1, i, s) for s in range(2) for i in range(2)]
    near_blocks(flags, place8, slots, pairs, before, out, scratch)


def last_kernel(
    flags, place8, a_left, a_right, left, right, c_ends, left_c, right_c, before, out, *scratch
):
    parity = lat_parity()
    at = PTS + QUAD
    own_place, far_place = 8 - 8 * parity, 8 * parity
    slots = [
        (left, block(a_left, at, 16), own_place + 4),
        (right, block(a_right, at, 16), own_place),
        (left_c, block(c_ends, QUAD, 16), far_place + 4),
        (right_c, block(c_ends, MSG + QUAD, 16), far_place),
    ]
    pairs = [(s, 1 - parity, 3 * s - 1, i, s) for s in range(2) for i in range(2)]
    pairs += [(2 + s, 2 - 3 * parity, 3 * s - 1, 1 - parity, s) for s in range(2)]
    near_blocks(flags, place8, slots, pairs, before, out, scratch)


def near(kernel, name, n_slots, n_pairs, operands, chained=True, cost=None, scratch=()):
    return pl.pallas_call(
        kernel,
        in_specs=[scalars, whole] + [hbm] * (len(operands) - 2),
        out_specs=[hbm],
        out_shape=[ACC],
        scratch_shapes=near_scratch(n_slots, n_pairs) + list(scratch),
        input_output_aliases={len(operands) - 1: 0} if chained else {},
        compiler_params=params(),
        cost_estimate=cost or COST,
        name=name,
    )(*operands)


def window_sum(flags, weights, bands, first=0):
    total = None
    for base, cells in bands:
        for v in range(6):
            if cells[v // 2] is None:
                continue
            ref, offset = cells[v // 2]
            for a in range(2):
                start = offset + (2 * a + v % 2) * RANK
                hi, lo = split(ref[start : start + RANK, :])
                u = base + a
                w = 6 * u + v
                rows = []
                for leaf in range(4):
                    part_w = weights[leaf, w - first]
                    d_row = u - 2 - leaf // 2
                    d_col = v - 2 - leaf % 2
                    if abs(d_col) <= 1:
                        inside = (d_row >= -1) & (d_row <= 1)
                        flag = flags[leaf, 3 * jnp.clip(d_row + 1, 0, 2) + d_col + 1]
                        keep = 1 - jnp.where(inside, flag, 0)
                        part_w = (part_w.astype(f32) * keep.astype(f32)).astype(bf16)
                    rows.append(part_w)
                stacked = jnp.concatenate(rows, 0)
                part = mm(stacked, hi) + mm(stacked, lo)
                total = part if total is None else total + part
    return total


def far_kernel(
    n_lat, n_lon, flags, weights, own, left, right, from_y, from_c, devices, c_ends,
    dev_w, dev_t, group_w, leaf_t, out, weights_v, cells, rows_dev, dev_w_v, dev_t_v,
    group_row_w, leaf_t_v, sems,
):
    lat = lax.axis_index("lat")
    lon = lax.axis_index("lon")
    parity = lax.rem(lat, 2)
    side = lax.rem(lon, 2)
    group_row, group_col = lat // 2, lon // 2
    n_gcol = n_lon // 2
    size = 2 * n_lon * RANK
    copies = []
    for source, target in (
        (dev_w, dev_w_v),
        (block(devices, 2 * MSG, size), rows_dev.at[0]),
        (block(c_ends, 2 * MSG, size), rows_dev.at[1]),
        (group_w.at[group_row, group_col], group_row_w),
        (dev_t, dev_t_v),
        (leaf_t, leaf_t_v),
        (block(own, PTS, QUAD), cells.at[0]),
        (block(left, PTS, QUAD), cells.at[1]),
        (block(right, PTS, QUAD), cells.at[2]),
        (block(from_y, 2 * PTS, QUAD), cells.at[3]),
        (block(from_c, 2 * PTS, QUAD), cells.at[4]),
        (block(c_ends, 0, QUAD), cells.at[5]),
        (block(c_ends, MSG, QUAD), cells.at[6]),
        (weights.at[0], weights_v.at[0]),
        (weights.at[1], weights_v.at[1]),
        (weights.at[2], weights_v.at[2]),
        (weights.at[3], weights_v.at[3]),
    ):
        copy = pltpu.make_async_copy(source, target, sems.at[len(copies)])
        copy.start()
        copies.append(copy)
    for copy in copies[:3]:
        copy.wait()

    def device_coef(k, back, col_side):
        which = jnp.where(side == col_side, 0, 1)
        start = pl.multiple_of((4 * back + 2 * (k // 2) + which) * RANK, RANK)
        return rows_dev[k % 2, pl.ds(start, RANK), :]

    total = jnp.zeros((RANK, COLS), f32)
    for k in range(n_lat):
        other = lat + k - 2 * (lat & k)
        u = other + 2 - 2 * group_row
        for v in range(6):
            shift = 2 * group_col - 2 + v
            drop = (jnp.abs(other - lat) <= 1) & (jnp.abs(shift - lon) <= 1)
            scale = jnp.where(drop, 0.0, 1.0)
            coef = device_coef(k, (1 - v // 2) % n_gcol, v % 2)
            total = total + scale * mm2(dev_w_v[6 * u + v], coef)
    for copy in copies[3:6]:
        copy.wait()

    def group_step(step, field):
        gcol = lax.rem(group_col + step, n_gcol)
        for pair in range(n_lat // 2):
            grow = group_row + pair - 2 * (group_row & pair)
            coef = jnp.zeros((RANK, COLS), f32)
            for e in range(2):
                k = 2 * pair + e
                other = lat + k - 2 * (lat & k)
                for f in range(2):
                    cell = other * n_lon + 2 * gcol + f
                    coef = coef + mm3(dev_t_v[cell], device_coef(k, n_gcol - step, f), (0, 0))
            field = field + mm2(group_row_w[grow, gcol], coef)
        return field

    field = lax.fori_loop(2, n_gcol - 1, group_step, jnp.zeros((RANK, COLS), f32))
    total = total + mm3(dev_t_v[lat * n_lon + lon], field)
    for copy in copies[6:]:
        copy.wait()
    far = window_sum(
        flags,
        weights_v,
        (
            (2, tuple((cells.at[i], 0) for i in (1, 0, 2))),
            (4 * parity, (None, (cells.at[3], 0), None)),
            (4 - 4 * parity, tuple((cells.at[i], 0) for i in (5, 4, 6))),
        ),
    )
    for leaf in range(4):
        rows = slice(leaf * RANK, (leaf + 1) * RANK)
        out[rows, :] = far[rows, :] + mm3(leaf_t_v[leaf], total)


def far_field(n_lat, n_lon, operands):
    return pl.pallas_call(
        functools.partial(far_kernel, n_lat, n_lon),
        in_specs=[scalars] + [hbm] * 12,
        out_specs=whole,
        out_shape=shape(QUAD, COLS),
        scratch_shapes=[
            VMEM((4, 36, RANK, RANK), bf16),
            VMEM((7, QUAD, COLS), f32),
            VMEM((2, 2 * n_lon * RANK, COLS), f32),
            VMEM((36, RANK, RANK), bf16),
            VMEM((n_lat * n_lon, RANK, RANK), f32),
            VMEM((n_lat // 2, n_lon // 2, RANK, RANK), bf16),
            VMEM((4, RANK, RANK), f32),
            pltpu.SemaphoreType.DMA((17,)),
        ],
        compiler_params=params(),
        cost_estimate=LOW,
        name="far",
    )(*operands)


def pack_kernel(*refs):
    parts, (out, sems) = refs[:-2], refs[-2:]
    copies = []
    row = 0
    for index, part in enumerate(parts):
        source = block(part, PTS, MSG) if index < 2 else part
        size = source.shape[0]
        copies.append(pltpu.make_async_copy(source, block(out, row, size), sems.at[index]))
        copies[-1].start()
        row += size
    for copy in copies:
        copy.wait()


def pack(left, right, devices):
    parts = [left, right, *devices]
    rows = 2 * MSG + sum(part.shape[0] for part in devices)
    return pl.pallas_call(
        pack_kernel,
        in_specs=[hbm] * len(parts),
        out_specs=whole,
        out_shape=shape(rows, COLS),
        scratch_shapes=[pltpu.SemaphoreType.DMA((len(parts),))],
        compiler_params=params(),
        cost_estimate=LOW,
        name="pack",
    )(*parts)


def down_kernel(
    flags, place8, weights, left_y, right_y, partial, basis, before, out, *scratch
):
    parity = lat_parity()
    near_refs, (weights_v, cells, basis_v, sems) = scratch[:-4], scratch[-4:]
    at = PTS + QUAD
    copies = []
    for source, target in (
        (block(left_y, PTS, QUAD), cells.at[0]),
        (block(right_y, PTS, QUAD), cells.at[1]),
        (partial, cells.at[2]),
        (weights.at[:, pl.ds(24 * parity, 12)], weights_v),
        (basis, basis_v),
    ):
        copy = pltpu.make_async_copy(source, target, sems.at[len(copies)])
        copy.start()
        copies.append(copy)

    def fill(acc, _):
        for copy in copies:
            copy.wait()
        band = (4 * parity, ((cells.at[0], 0), None, (cells.at[1], 0)))
        far = cells[2] + window_sum(flags, weights_v, (band,), 24 * parity)
        for leaf in range(4):
            acc[leaf] += mm3(basis_v[leaf], far[leaf * RANK : (leaf + 1) * RANK, :], (0, 0))

    base = 8 - 8 * parity
    slots = [
        (block(left_y, 0, PTS), block(left_y, at, 16), base + 4),
        (block(right_y, 0, PTS), block(right_y, at, 16), base),
    ]
    pairs = [(s, 3 * parity - 1, 3 * s - 1, parity, s) for s in range(2)]
    near_blocks(flags, place8, slots, pairs, before, out, near_refs, fill)


def local(
    losses,
    positions,
    leaf_basis,
    near_flags,
    leaf_coupling,
    leaf_transfer,
    device_coupling,
    device_transfer,
    group_coupling,
):
    n_lat = lax.axis_size("lat")
    n_lon = lax.axis_size("lon")

    flat = losses.reshape(4, PTS, COLS)
    basis = jnp.swapaxes(leaf_basis, 2, 3).reshape(4, RANK, PTS)
    flags = near_flags.reshape(4, 9)
    weights = leaf_coupling.reshape(4, 36, RANK, RANK)
    transfer = leaf_transfer.reshape(4, RANK, RANK)

    to_right = [(i, (i + 1) % n_lon) for i in range(n_lon)]
    to_left = [(i, (i - 1) % n_lon) for i in range(n_lon)]
    in_chip = [(i, i ^ 1) for i in range(n_lat)]
    across = [(i, i + 1 if i % 2 else i - 1) for i in range(n_lat)]
    across = [(a, b) for a, b in across if 0 <= b < n_lat]

    across_two = [(i, i ^ 2) for i in range(n_lat)]
    partner = [(i, i ^ 1) for i in range(n_lon)]
    barrier = lax.optimization_barrier

    a_right, a_left, b_right, b_left, to_y, to_c, place8, dev = coefficients(
        flat, basis, transfer, positions.reshape(4, 2, PTS)
    )
    dev_pair = lax.ppermute(dev, "lon", partner)
    from_c = lax.ppermute(to_c, "lat", in_chip)
    dev_pair, to_y = barrier((dev_pair, to_y))
    from_y = lax.ppermute(to_y, "lat", across)

    left = lax.ppermute(a_right, "lon", to_right)
    right = lax.ppermute(a_left, "lon", to_left)
    pair = jnp.concatenate([dev, dev_pair], 0)
    pair_two = lax.ppermute(pair, "lat", across_two)
    quad = jnp.concatenate([pair, pair_two], 0)

    def rotate(step):
        return lax.ppermute(quad, "lon", [(i, (i + step) % n_lon) for i in range(n_lon)])

    first, last = rotate(2), rotate(n_lon - 2)
    from_c, quad, place8 = barrier((from_c, quad, place8))
    (acc,) = near(own_kernel, "own", 4, 16, (flags, place8, flat, a_right), chained=False)
    from_y, first, last, quad, acc = barrier((from_y, first, last, quad, acc))
    moved = [first, *(rotate(step) for step in range(4, n_lon - 2, 2)), last]
    (acc,) = near(lat_kernel, "lat", 4, 8, (flags, place8, from_y, from_c, acc))
    left, right, b_right, b_left, acc = barrier((left, right, b_right, b_left, acc))
    left_b = lax.ppermute(b_right, "lon", to_right)
    right_b = lax.ppermute(b_left, "lon", to_left)
    left_y = lax.ppermute(left, "lat", across)
    right_y = lax.ppermute(right, "lat", across)
    to_c = pack(left, right, (quad, *moved))
    c_ends = lax.ppermute(to_c, "lat", in_chip)
    (acc,) = near(lon_kernel, "lon", 2, 4, (flags, place8, left, right, acc))
    c_ends, acc = barrier((c_ends, acc))
    partial = far_field(
        n_lat,
        n_lon,
        (
            flags,
            weights,
            a_right,
            left,
            right,
            from_y,
            from_c,
            to_c,
            c_ends,
            device_coupling.reshape(36, RANK, RANK),
            device_transfer.reshape(n_lat * n_lon, RANK, RANK),
            group_coupling,
            transfer,
        ),
    )
    left_y, right_y, partial = barrier((left_y, right_y, partial))
    (acc,) = near(
        down_kernel,
        "down",
        2,
        2,
        (flags, place8, weights, left_y, right_y, partial, basis, acc),
        cost=LOW,
        scratch=[
            VMEM((4, 12, RANK, RANK), bf16),
            VMEM((3, QUAD, COLS), f32),
            VMEM((4, RANK, PTS), f32),
            pltpu.SemaphoreType.DMA((5,)),
        ],
    )
    left_b, right_b, acc = barrier((left_b, right_b, acc))
    left_c = lax.ppermute(left_b, "lat", in_chip)
    right_c = lax.ppermute(right_b, "lat", in_chip)
    (acc,) = near(
        last_kernel,
        "last",
        4,
        6,
        (flags, place8, left, right, left_b, right_b, c_ends, left_c, right_c, acc),
    )
    return acc.reshape(2, 2, PTS, COLS)


def solution(mesh):
    placed = (
        P("lat", "lon", None, None),
        P("lat", "lon", None, None),
        P("lat", "lon", None, None),
        P("lat", "lon", None),
        P("lat", "lon", None, None, None),
        P("lat", "lon", None, None),
        P("lat", "lon", None, None, None),
        P(),
        P(),
    )
    return jax.shard_map(
        local, mesh=mesh, in_specs=placed, out_specs=P("lat", "lon", None, None), check_vma=False
    )
```

```python
import functools

import jax
import jax.numpy as jnp
from jax import lax
from jax.experimental import pallas as pl
from jax.experimental.pallas import tpu as pltpu
from jax.sharding import PartitionSpec as P

PTS = 512
RANK = 64
COLS = 256
HALF = 256
QUAD = 4 * RANK
MSG = QUAD + 16

LN2 = 0.6931471805599453
UNIT = 1.7320508075688772 / 0.15 / LN2

f32 = jnp.float32
bf16 = jnp.bfloat16
VMEM = pltpu.VMEM
SMEM = pltpu.SMEM
whole = pl.BlockSpec(memory_space=VMEM)
scalars = pl.BlockSpec(memory_space=SMEM)


def split(x):
    hi = x.astype(bf16)
    return hi, (x - hi.astype(f32)).astype(bf16)


def mm(a, b, dims=(1, 0)):
    return lax.dot_general(
        a, b, (((dims[0],), (dims[1],)), ((), ())), preferred_element_type=f32
    )


def mm3(a, b, dims=(1, 0)):
    a_hi, a_lo = split(a)
    b_hi, b_lo = split(b)
    return mm(a_hi, b_hi, dims) + (mm(a_lo, b_hi, dims) + mm(a_hi, b_lo, dims))


def mm2(a, b):
    b_hi, b_lo = split(b)
    return mm(a, b_hi) + mm(a, b_lo)


def params(limit=64):
    return pltpu.CompilerParams(vmem_limit_bytes=limit * 1024 * 1024)


COST = pl.CostEstimate(flops=20_000_000_000, bytes_accessed=4_000_000, transcendentals=0)
LOW = pl.CostEstimate(flops=1_000, bytes_accessed=1_000, transcendentals=0)


def shape(*dims):
    return jax.ShapeDtypeStruct(dims, f32)


def lat_parity():
    return lax.rem(lax.axis_index("lat"), 2)


def coef_kernel(
    loss, basis, transfer, pos, a_right, a_left, b_right, b_left, to_y, to_c, place8, dev,
    values, bases, message, sems, load_sems,
):
    parity = lat_parity()
    loads = [
        (
            pltpu.make_async_copy(loss.at[leaf], values.at[leaf], load_sems.at[leaf]),
            pltpu.make_async_copy(basis.at[leaf], bases.at[leaf], load_sems.at[4 + leaf]),
        )
        for leaf in range(4)
    ]
    for pair in loads:
        for copy in pair:
            copy.start()
    for leaf in range(4):
        place = pos[leaf] * UNIT
        place8[leaf] = jnp.concatenate([place, jnp.zeros((6, PTS), f32)], 0)
        for coord in range(2):
            for half in range(2):
                at = QUAD + 4 * leaf + 2 * coord + half
                message[at : at + 1, :] = place[coord : coord + 1, half * HALF : (half + 1) * HALF]
    for pair in loads:
        for copy in pair:
            copy.wait()
    y_row, c_row = 2 * parity, 2 - 2 * parity
    first, second = slice(0, PTS), slice(PTS, 2 * PTS)
    copies = []
    for source, target in (
        (y_row + 1, a_right.at[first]),
        (y_row, a_left.at[first]),
        (c_row + 1, b_right),
        (c_row, b_left),
        (y_row, to_y.at[first]),
        (y_row + 1, to_y.at[second]),
        (c_row, to_c.at[first]),
        (c_row + 1, to_c.at[second]),
    ):
        copy = pltpu.make_async_copy(values.at[source], target, sems.at[len(copies)])
        copy.start()
        copies.append(copy)
    total = None
    for leaf in range(4):
        l_hi, l_lo = split(values[leaf])
        b_hi, b_lo = split(bases[leaf])
        coef = mm(b_hi, l_hi) + (mm(b_lo, l_hi) + mm(b_hi, l_lo))
        message[leaf * RANK : (leaf + 1) * RANK, :] = coef
        part = mm3(transfer[leaf], coef, (0, 0))
        total = part if leaf == 0 else total + part
    dev[...] = total
    for target in (
        a_right.at[PTS:], a_left.at[PTS:], to_y.at[2 * PTS :], to_c.at[2 * PTS :]
    ):
        copy = pltpu.make_async_copy(message, target, sems.at[len(copies)])
        copy.start()
        copies.append(copy)
    for copy in copies:
        copy.wait()


hbm = pl.BlockSpec(memory_space=pl.ANY)


def coefficients(losses, basis, transfer, positions):
    return pl.pallas_call(
        coef_kernel,
        in_specs=[hbm, hbm, whole, whole],
        out_specs=[hbm] * 6 + [whole] * 2,
        out_shape=[
            shape(PTS + MSG, COLS),
            shape(PTS + MSG, COLS),
            shape(PTS, COLS),
            shape(PTS, COLS),
            shape(2 * PTS + MSG, COLS),
            shape(2 * PTS + MSG, COLS),
            shape(4, 8, PTS),
            shape(RANK, COLS),
        ],
        scratch_shapes=[
            VMEM((4, PTS, COLS), f32),
            VMEM((4, RANK, PTS), f32),
            VMEM((MSG, COLS), f32),
            pltpu.SemaphoreType.DMA((12,)),
            pltpu.SemaphoreType.DMA((8,)),
        ],
        compiler_params=params(),
        cost_estimate=COST,
        name="coefs",
    )(losses, basis, transfer, positions)


def near_scratch(n_slots, n_pairs):
    return [
        SMEM((n_pairs + 1, 8), jnp.int32),
        VMEM((4, PTS, 8), f32),
        VMEM((n_slots, 8, PTS), f32),
        VMEM((n_slots, 2 * PTS, COLS), bf16),
        VMEM((PTS, 2 * PTS), bf16),
        VMEM((PTS, 2 * PTS), bf16),
        VMEM((4, PTS, COLS), f32),
        VMEM((n_slots, PTS, COLS), f32),
        VMEM((n_slots, 16, COLS), f32),
        pltpu.SemaphoreType.DMA((8 + 2 * n_slots,)),
    ]


def near_blocks(flags, place8, slots, pairs, before, out, scratch, fill=None):
    table, tpos, spos, stack, kern_a, kern_b, acc, stage, marks, sems = scratch
    arrivals = []
    for slot, (values, places, _) in enumerate(slots):
        pair = (
            pltpu.make_async_copy(values, stage.at[slot], sems.at[8 + 2 * slot]),
            pltpu.make_async_copy(places, marks.at[slot], sems.at[9 + 2 * slot]),
        )
        for copy in pair:
            copy.start()
        arrivals.append(pair)
    loads = []
    if before is not None:
        loads = [
            pltpu.make_async_copy(before.at[leaf], acc.at[leaf], sems.at[leaf])
            for leaf in range(4)
        ]
    for copy in loads:
        copy.start()
    for leaf in range(4):
        tpos[leaf] = place8[leaf].T
    for slot, (_, _, base) in enumerate(slots):
        for copy in arrivals[slot]:
            copy.wait()
        hi, lo = split(stage[slot])
        stack[slot, :PTS, :] = hi
        stack[slot, PTS:, :] = lo
        for coord in range(2):
            for half in range(2):
                spos[slot, coord : coord + 1, half * HALF : (half + 1) * HALF] = marks[
                    slot, pl.ds(base + 2 * coord + half, 1), :
                ]
    count = 0
    for slot, row, col, own_row, own_col in pairs:
        target = 2 * own_row + own_col
        table[count, 0] = slot
        table[count, 1] = target
        table[count, 2] = row - own_row
        table[count, 3] = col - own_col
        flag = flags[target, 3 * (row - own_row + 1) + col - own_col + 1]
        count = count + jnp.where(flag > 0, 1, 0)

    def evaluate(index, half, kern):
        slot, target = table[index, 0], table[index, 1]
        src_row = spos[slot, 0:1, :] + table[index, 2].astype(f32) * UNIT
        src_col = spos[slot, 1:2, :] + table[index, 3].astype(f32) * UNIT
        part = slice(half * HALF, (half + 1) * HALF)
        d_row = tpos[target, part, 0:1] - src_row
        d_col = tpos[target, part, 1:2] - src_col
        square = d_row * d_row + d_col * d_col
        dist = square * lax.rsqrt(jnp.maximum(square, 1e-30))
        decay = jnp.exp2(-dist)
        hi, lo = split(decay + decay * (dist * LN2))
        kern[part, :PTS] = hi
        kern[part, PTS:] = lo

    def apply(index, half, kern):
        slot, target = table[index, 0], table[index, 1]
        part = slice(half * HALF, (half + 1) * HALF)
        l_hi = stack[slot, :PTS, :]
        l_lo = stack[slot, PTS:, :]
        k_hi = kern[part, :PTS]
        k_lo = kern[part, PTS:]
        acc[target, part, :] += mm(k_hi, l_hi) + mm(k_lo, l_hi) + mm(k_hi, l_lo)

    def step(index, kern, other):
        following = jnp.minimum(index + 1, count - 1)
        for half in range(2):
            evaluate(following, half, other)
            apply(index, half, kern)

    @pl.when(count > 0)
    def _():
        for half in range(2):
            evaluate(0, half, kern_a)

    for copy in loads:
        copy.wait()
    if fill is not None:
        fill(acc, stage)

    @pl.loop(0, (count + 1) // 2)
    def _(pair):
        step(2 * pair, kern_a, kern_b)

        @pl.when(2 * pair + 1 < count)
        def _():
            step(2 * pair + 1, kern_b, kern_a)


    stores = [
        pltpu.make_async_copy(acc.at[leaf], out.at[leaf], sems.at[4 + leaf]) for leaf in range(4)
    ]
    for copy in stores:
        copy.start()
    for copy in stores:
        copy.wait()


ACC = shape(4, PTS, COLS)


def block(ref, start, rows):
    return ref.at[pl.ds(start, rows)]


def own_kernel(flags, place8, loss, msg, out, *scratch):
    slots = [(loss.at[leaf], block(msg, PTS + QUAD, 16), 4 * leaf) for leaf in range(4)]
    pairs = [(s, s // 2, s % 2, t // 2, t % 2) for s in range(4) for t in range(4)]

    def fill(acc, losses):
        for leaf in range(4):
            acc[leaf] = 0.5 * losses[leaf]

    near_blocks(flags, place8, slots, pairs, None, out, scratch, fill)


def lat_kernel(flags, place8, from_y, from_c, before, out, *scratch):
    parity = lat_parity()
    slots, pairs = [], []
    for ref, place, row, own_row in (
        (from_y, 8 - 8 * parity, 3 * parity - 1, parity),
        (from_c, 8 * parity, 2 - 3 * parity, 1 - parity),
    ):
        for col in range(2):
            for own_col in range(2):
                pairs.append((len(slots), row, col, own_row, own_col))
            slots.append(
                (block(ref, col * PTS, PTS), block(ref, 2 * PTS + QUAD, 16), place + 4 * col)
            )
    near_blocks(flags, place8, slots, pairs, before, out, scratch)


def lon_kernel(flags, place8, left, right, before, out, *scratch):
    parity = lat_parity()
    at = PTS + QUAD
    slots = [
        (block(left, 0, PTS), block(left, at, 16), 8 * parity + 4),
        (block(right, 0, PTS), block(right, at, 16), 8 * parity),
    ]
    pairs = [(s, parity, 3 * s - 1, i, s) for s in range(2) for i in range(2)]
    near_blocks(flags, place8, slots, pairs, before, out, scratch)


def last_kernel(
    flags, place8, a_left, a_right, left, right, c_ends, left_c, right_c, before, out, *scratch
):
    parity = lat_parity()
    at = PTS + QUAD
    own_place, far_place = 8 - 8 * parity, 8 * parity
    slots = [
        (left, block(a_left, at, 16), own_place + 4),
        (right, block(a_right, at, 16), own_place),
        (left_c, block(c_ends, QUAD, 16), far_place + 4),
        (right_c, block(c_ends, MSG + QUAD, 16), far_place),
    ]
    pairs = [(s, 1 - parity, 3 * s - 1, i, s) for s in range(2) for i in range(2)]
    pairs += [(2 + s, 2 - 3 * parity, 3 * s - 1, 1 - parity, s) for s in range(2)]
    near_blocks(flags, place8, slots, pairs, before, out, scratch)


def near(kernel, name, n_slots, n_pairs, operands, chained=True, cost=None, scratch=()):
    return pl.pallas_call(
        kernel,
        in_specs=[scalars, whole] + [hbm] * (len(operands) - 2),
        out_specs=[hbm],
        out_shape=[ACC],
        scratch_shapes=near_scratch(n_slots, n_pairs) + list(scratch),
        input_output_aliases={len(operands) - 1: 0} if chained else {},
        compiler_params=params(),
        cost_estimate=cost or COST,
        name=name,
    )(*operands)


def window_sum(flags, weights, bands, first=0):
    total = None
    for base, cells in bands:
        for v in range(6):
            if cells[v // 2] is None:
                continue
            ref, offset = cells[v // 2]
            for a in range(2):
                start = offset + (2 * a + v % 2) * RANK
                hi, lo = split(ref[start : start + RANK, :])
                u = base + a
                w = 6 * u + v
                rows = []
                for leaf in range(4):
                    part_w = weights[leaf, w - first]
                    d_row = u - 2 - leaf // 2
                    d_col = v - 2 - leaf % 2
                    if abs(d_col) <= 1:
                        inside = (d_row >= -1) & (d_row <= 1)
                        flag = flags[leaf, 3 * jnp.clip(d_row + 1, 0, 2) + d_col + 1]
                        keep = 1 - jnp.where(inside, flag, 0)
                        part_w = (part_w.astype(f32) * keep.astype(f32)).astype(bf16)
                    rows.append(part_w)
                stacked = jnp.concatenate(rows, 0)
                part = mm(stacked, hi) + mm(stacked, lo)
                total = part if total is None else total + part
    return total


def far_kernel(
    n_lat, n_lon, flags, weights, own, left, right, from_y, from_c, devices, c_ends,
    dev_w, dev_t, group_w, leaf_t, out, weights_v, cells, rows_dev, dev_w_v, dev_t_v,
    group_row_w, leaf_t_v, sems,
):
    lat = lax.axis_index("lat")
    lon = lax.axis_index("lon")
    parity = lax.rem(lat, 2)
    side = lax.rem(lon, 2)
    group_row, group_col = lat // 2, lon // 2
    n_gcol = n_lon // 2
    size = 2 * n_lon * RANK
    copies = []
    for source, target in (
        (dev_w, dev_w_v),
        (block(devices, 2 * MSG, size), rows_dev.at[0]),
        (block(c_ends, 2 * MSG, size), rows_dev.at[1]),
        (group_w.at[group_row, group_col], group_row_w),
        (dev_t, dev_t_v),
        (leaf_t, leaf_t_v),
        (block(own, PTS, QUAD), cells.at[0]),
        (block(left, PTS, QUAD), cells.at[1]),
        (block(right, PTS, QUAD), cells.at[2]),
        (block(from_y, 2 * PTS, QUAD), cells.at[3]),
        (block(from_c, 2 * PTS, QUAD), cells.at[4]),
        (block(c_ends, 0, QUAD), cells.at[5]),
        (block(c_ends, MSG, QUAD), cells.at[6]),
        (weights.at[0], weights_v.at[0]),
        (weights.at[1], weights_v.at[1]),
        (weights.at[2], weights_v.at[2]),
        (weights.at[3], weights_v.at[3]),
    ):
        copy = pltpu.make_async_copy(source, target, sems.at[len(copies)])
        copy.start()
        copies.append(copy)
    for copy in copies[:3]:
        copy.wait()

    def device_coef(k, back, col_side):
        which = jnp.where(side == col_side, 0, 1)
        start = pl.multiple_of((4 * back + 2 * (k // 2) + which) * RANK, RANK)
        return rows_dev[k % 2, pl.ds(start, RANK), :]

    total = jnp.zeros((RANK, COLS), f32)
    for k in range(n_lat):
        other = lat + k - 2 * (lat & k)
        u = other + 2 - 2 * group_row
        for v in range(6):
            shift = 2 * group_col - 2 + v
            drop = (jnp.abs(other - lat) <= 1) & (jnp.abs(shift - lon) <= 1)
            scale = jnp.where(drop, 0.0, 1.0)
            coef = device_coef(k, (1 - v // 2) % n_gcol, v % 2)
            total = total + scale * mm2(dev_w_v[6 * u + v], coef)
    for copy in copies[3:6]:
        copy.wait()

    def group_step(step, field):
        gcol = lax.rem(group_col + step, n_gcol)
        for pair in range(n_lat // 2):
            grow = group_row + pair - 2 * (group_row & pair)
            coef = jnp.zeros((RANK, COLS), f32)
            for e in range(2):
                k = 2 * pair + e
                other = lat + k - 2 * (lat & k)
                for f in range(2):
                    cell = other * n_lon + 2 * gcol + f
                    coef = coef + mm3(dev_t_v[cell], device_coef(k, n_gcol - step, f), (0, 0))
            field = field + mm2(group_row_w[grow, gcol], coef)
        return field

    field = lax.fori_loop(2, n_gcol - 1, group_step, jnp.zeros((RANK, COLS), f32))
    total = total + mm3(dev_t_v[lat * n_lon + lon], field)
    for copy in copies[6:]:
        copy.wait()
    far = window_sum(
        flags,
        weights_v,
        (
            (2, tuple((cells.at[i], 0) for i in (1, 0, 2))),
            (4 * parity, (None, (cells.at[3], 0), None)),
            (4 - 4 * parity, tuple((cells.at[i], 0) for i in (5, 4, 6))),
        ),
    )
    for leaf in range(4):
        rows = slice(leaf * RANK, (leaf + 1) * RANK)
        out[rows, :] = far[rows, :] + mm3(leaf_t_v[leaf], total)


def far_field(n_lat, n_lon, operands):
    return pl.pallas_call(
        functools.partial(far_kernel, n_lat, n_lon),
        in_specs=[scalars] + [hbm] * 12,
        out_specs=whole,
        out_shape=shape(QUAD, COLS),
        scratch_shapes=[
            VMEM((4, 36, RANK, RANK), bf16),
            VMEM((7, QUAD, COLS), f32),
            VMEM((2, 2 * n_lon * RANK, COLS), f32),
            VMEM((36, RANK, RANK), bf16),
            VMEM((n_lat * n_lon, RANK, RANK), f32),
            VMEM((n_lat // 2, n_lon // 2, RANK, RANK), bf16),
            VMEM((4, RANK, RANK), f32),
            pltpu.SemaphoreType.DMA((17,)),
        ],
        compiler_params=params(),
        cost_estimate=LOW,
        name="far",
    )(*operands)


def pack_kernel(*refs):
    parts, (out, sems) = refs[:-2], refs[-2:]
    copies = []
    row = 0
    for index, part in enumerate(parts):
        source = block(part, PTS, MSG) if index < 2 else part
        size = source.shape[0]
        copies.append(pltpu.make_async_copy(source, block(out, row, size), sems.at[index]))
        copies[-1].start()
        row += size
    for copy in copies:
        copy.wait()


def pack(left, right, devices):
    parts = [left, right, *devices]
    rows = 2 * MSG + sum(part.shape[0] for part in devices)
    return pl.pallas_call(
        pack_kernel,
        in_specs=[hbm] * len(parts),
        out_specs=whole,
        out_shape=shape(rows, COLS),
        scratch_shapes=[pltpu.SemaphoreType.DMA((len(parts),))],
        compiler_params=params(),
        cost_estimate=LOW,
        name="pack",
    )(*parts)


def down_kernel(
    flags, place8, weights, left_y, right_y, partial, basis, before, out, *scratch
):
    parity = lat_parity()
    near_refs, (weights_v, cells, basis_v, sems) = scratch[:-4], scratch[-4:]
    at = PTS + QUAD
    copies = []
    for source, target in (
        (block(left_y, PTS, QUAD), cells.at[0]),
        (block(right_y, PTS, QUAD), cells.at[1]),
        (partial, cells.at[2]),
        (weights.at[:, pl.ds(24 * parity, 12)], weights_v),
        (basis, basis_v),
    ):
        copy = pltpu.make_async_copy(source, target, sems.at[len(copies)])
        copy.start()
        copies.append(copy)

    def fill(acc, _):
        for copy in copies:
            copy.wait()
        band = (4 * parity, ((cells.at[0], 0), None, (cells.at[1], 0)))
        far = cells[2] + window_sum(flags, weights_v, (band,), 24 * parity)
        for leaf in range(4):
            acc[leaf] += mm3(basis_v[leaf], far[leaf * RANK : (leaf + 1) * RANK, :], (0, 0))

    base = 8 - 8 * parity
    slots = [
        (block(left_y, 0, PTS), block(left_y, at, 16), base + 4),
        (block(right_y, 0, PTS), block(right_y, at, 16), base),
    ]
    pairs = [(s, 3 * parity - 1, 3 * s - 1, parity, s) for s in range(2)]
    near_blocks(flags, place8, slots, pairs, before, out, near_refs, fill)


def local(
    losses,
    positions,
    leaf_basis,
    near_flags,
    leaf_coupling,
    leaf_transfer,
    device_coupling,
    device_transfer,
    group_coupling,
):
    n_lat = lax.axis_size("lat")
    n_lon = lax.axis_size("lon")

    flat = losses.reshape(4, PTS, COLS)
    basis = jnp.swapaxes(leaf_basis, 2, 3).reshape(4, RANK, PTS)
    flags = near_flags.reshape(4, 9)
    weights = leaf_coupling.reshape(4, 36, RANK, RANK)
    transfer = leaf_transfer.reshape(4, RANK, RANK)

    to_right = [(i, (i + 1) % n_lon) for i in range(n_lon)]
    to_left = [(i, (i - 1) % n_lon) for i in range(n_lon)]
    in_chip = [(i, i ^ 1) for i in range(n_lat)]
    across = [(i, i + 1 if i % 2 else i - 1) for i in range(n_lat)]
    across = [(a, b) for a, b in across if 0 <= b < n_lat]

    across_two = [(i, i ^ 2) for i in range(n_lat)]
    partner = [(i, i ^ 1) for i in range(n_lon)]
    barrier = lax.optimization_barrier

    a_right, a_left, b_right, b_left, to_y, to_c, place8, dev = coefficients(
        flat, basis, transfer, positions.reshape(4, 2, PTS)
    )
    dev_pair = lax.ppermute(dev, "lon", partner)
    from_c = lax.ppermute(to_c, "lat", in_chip)
    dev_pair, to_y = barrier((dev_pair, to_y))
    from_y = lax.ppermute(to_y, "lat", across)

    left = lax.ppermute(a_right, "lon", to_right)
    right = lax.ppermute(a_left, "lon", to_left)
    pair = jnp.concatenate([dev, dev_pair], 0)
    pair_two = lax.ppermute(pair, "lat", across_two)
    quad = jnp.concatenate([pair, pair_two], 0)

    def rotate(step):
        return lax.ppermute(quad, "lon", [(i, (i + step) % n_lon) for i in range(n_lon)])

    first, last = rotate(2), rotate(n_lon - 2)
    from_c, quad, place8 = barrier((from_c, quad, place8))
    (acc,) = near(own_kernel, "own", 4, 16, (flags, place8, flat, a_right), chained=False)
    from_y, quad, acc = barrier((from_y, quad, acc))
    moved = [first, *(rotate(step) for step in range(4, n_lon - 2, 2)), last]
    (acc,) = near(lat_kernel, "lat", 4, 8, (flags, place8, from_y, from_c, acc), cost=LOW)
    left, right, b_right, b_left, acc = barrier((left, right, b_right, b_left, acc))
    left_b = lax.ppermute(b_right, "lon", to_right)
    right_b = lax.ppermute(b_left, "lon", to_left)
    left_y = lax.ppermute(left, "lat", across)
    right_y = lax.ppermute(right, "lat", across)
    to_c = pack(left, right, (quad, *moved))
    c_ends = lax.ppermute(to_c, "lat", in_chip)
    (acc,) = near(lon_kernel, "lon", 2, 4, (flags, place8, left, right, acc))
    c_ends, acc = barrier((c_ends, acc))
    partial = far_field(
        n_lat,
        n_lon,
        (
            flags,
            weights,
            a_right,
            left,
            right,
            from_y,
            from_c,
            to_c,
            c_ends,
            device_coupling.reshape(36, RANK, RANK),
            device_transfer.reshape(n_lat * n_lon, RANK, RANK),
            group_coupling,
            transfer,
        ),
    )
    left_b, right_b, left_y, right_y, partial = barrier(
        (left_b, right_b, left_y, right_y, partial)
    )
    left_c = lax.ppermute(left_b, "lat", in_chip)
    right_c = lax.ppermute(right_b, "lat", in_chip)
    (acc,) = near(
        down_kernel,
        "down",
        2,
        2,
        (flags, place8, weights, left_y, right_y, partial, basis, acc),
        cost=LOW,
        scratch=[
            VMEM((4, 12, RANK, RANK), bf16),
            VMEM((3, QUAD, COLS), f32),
            VMEM((4, RANK, PTS), f32),
            pltpu.SemaphoreType.DMA((5,)),
        ],
    )
    left_c, right_c, acc = barrier((left_c, right_c, acc))
    (acc,) = near(
        last_kernel,
        "last",
        4,
        6,
        (flags, place8, left, right, left_b, right_b, c_ends, left_c, right_c, acc),
    )
    return acc.reshape(2, 2, PTS, COLS)


def solution(mesh):
    placed = (
        P("lat", "lon", None, None),
        P("lat", "lon", None, None),
        P("lat", "lon", None, None),
        P("lat", "lon", None),
        P("lat", "lon", None, None, None),
        P("lat", "lon", None, None),
        P("lat", "lon", None, None, None),
        P(),
        P(),
    )
    return jax.shard_map(
        local, mesh=mesh, in_specs=placed, out_specs=P("lat", "lon", None, None), check_vma=False
    )
```

```python
import functools

import jax
import jax.numpy as jnp
from jax import lax
from jax.experimental import pallas as pl
from jax.experimental.pallas import tpu as pltpu
from jax.sharding import PartitionSpec as P

PTS = 512
RANK = 64
COLS = 256
HALF = 256
QUAD = 4 * RANK
MSG = QUAD + 16

LN2 = 0.6931471805599453
UNIT = 1.7320508075688772 / 0.15 / LN2

f32 = jnp.float32
bf16 = jnp.bfloat16
VMEM = pltpu.VMEM
SMEM = pltpu.SMEM
whole = pl.BlockSpec(memory_space=VMEM)
scalars = pl.BlockSpec(memory_space=SMEM)


def split(x):
    hi = x.astype(bf16)
    return hi, (x - hi.astype(f32)).astype(bf16)


def mm(a, b, dims=(1, 0)):
    return lax.dot_general(
        a, b, (((dims[0],), (dims[1],)), ((), ())), preferred_element_type=f32
    )


def mm3(a, b, dims=(1, 0)):
    a_hi, a_lo = split(a)
    b_hi, b_lo = split(b)
    return mm(a_hi, b_hi, dims) + (mm(a_lo, b_hi, dims) + mm(a_hi, b_lo, dims))


def mm2(a, b):
    b_hi, b_lo = split(b)
    return mm(a, b_hi) + mm(a, b_lo)


def params(limit=64):
    return pltpu.CompilerParams(vmem_limit_bytes=limit * 1024 * 1024)


COST = pl.CostEstimate(flops=20_000_000_000, bytes_accessed=4_000_000, transcendentals=0)
LOW = pl.CostEstimate(flops=1_000, bytes_accessed=1_000, transcendentals=0)


def shape(*dims):
    return jax.ShapeDtypeStruct(dims, f32)


def lat_parity():
    return lax.rem(lax.axis_index("lat"), 2)


def coef_kernel(
    loss, basis, transfer, pos, a_right, a_left, b_right, b_left, to_y, to_c, place8, dev,
    values, bases, message, sems, load_sems,
):
    parity = lat_parity()
    loads = [
        (
            pltpu.make_async_copy(loss.at[leaf], values.at[leaf], load_sems.at[leaf]),
            pltpu.make_async_copy(basis.at[leaf], bases.at[leaf], load_sems.at[4 + leaf]),
        )
        for leaf in range(4)
    ]
    for pair in loads:
        for copy in pair:
            copy.start()
    for leaf in range(4):
        place = pos[leaf] * UNIT
        place8[leaf] = jnp.concatenate([place, jnp.zeros((6, PTS), f32)], 0)
        for coord in range(2):
            for half in range(2):
                at = QUAD + 4 * leaf + 2 * coord + half
                message[at : at + 1, :] = place[coord : coord + 1, half * HALF : (half + 1) * HALF]
    for pair in loads:
        for copy in pair:
            copy.wait()
    y_row, c_row = 2 * parity, 2 - 2 * parity
    first, second = slice(0, PTS), slice(PTS, 2 * PTS)
    copies = []
    for source, target in (
        (y_row + 1, a_right.at[first]),
        (y_row, a_left.at[first]),
        (c_row + 1, b_right),
        (c_row, b_left),
        (y_row, to_y.at[first]),
        (y_row + 1, to_y.at[second]),
        (c_row, to_c.at[first]),
        (c_row + 1, to_c.at[second]),
    ):
        copy = pltpu.make_async_copy(values.at[source], target, sems.at[len(copies)])
        copy.start()
        copies.append(copy)
    total = None
    for leaf in range(4):
        l_hi, l_lo = split(values[leaf])
        b_hi, b_lo = split(bases[leaf])
        coef = mm(b_hi, l_hi) + (mm(b_lo, l_hi) + mm(b_hi, l_lo))
        message[leaf * RANK : (leaf + 1) * RANK, :] = coef
        part = mm3(transfer[leaf], coef, (0, 0))
        total = part if leaf == 0 else total + part
    dev[...] = total
    for target in (
        a_right.at[PTS:], a_left.at[PTS:], to_y.at[2 * PTS :], to_c.at[2 * PTS :]
    ):
        copy = pltpu.make_async_copy(message, target, sems.at[len(copies)])
        copy.start()
        copies.append(copy)
    for copy in copies:
        copy.wait()


hbm = pl.BlockSpec(memory_space=pl.ANY)


def coefficients(losses, basis, transfer, positions):
    return pl.pallas_call(
        coef_kernel,
        in_specs=[hbm, hbm, whole, whole],
        out_specs=[hbm] * 6 + [whole] * 2,
        out_shape=[
            shape(PTS + MSG, COLS),
            shape(PTS + MSG, COLS),
            shape(PTS, COLS),
            shape(PTS, COLS),
            shape(2 * PTS + MSG, COLS),
            shape(2 * PTS + MSG, COLS),
            shape(4, 8, PTS),
            shape(RANK, COLS),
        ],
        scratch_shapes=[
            VMEM((4, PTS, COLS), f32),
            VMEM((4, RANK, PTS), f32),
            VMEM((MSG, COLS), f32),
            pltpu.SemaphoreType.DMA((12,)),
            pltpu.SemaphoreType.DMA((8,)),
        ],
        compiler_params=params(),
        cost_estimate=COST,
        name="coefs",
    )(losses, basis, transfer, positions)


def near_scratch(n_slots, n_pairs):
    return [
        SMEM((n_pairs + 1, 8), jnp.int32),
        VMEM((4, PTS, 8), f32),
        VMEM((n_slots, 8, PTS), f32),
        VMEM((n_slots, 2 * PTS, COLS), bf16),
        VMEM((PTS, 2 * PTS), bf16),
        VMEM((PTS, 2 * PTS), bf16),
        VMEM((4, PTS, COLS), f32),
        VMEM((n_slots, PTS, COLS), f32),
        VMEM((n_slots, 16, COLS), f32),
        pltpu.SemaphoreType.DMA((8 + 2 * n_slots,)),
    ]


def near_blocks(flags, place8, slots, pairs, before, out, scratch, fill=None):
    table, tpos, spos, stack, kern_a, kern_b, acc, stage, marks, sems = scratch
    arrivals = []
    for slot, (values, places, _) in enumerate(slots):
        pair = (
            pltpu.make_async_copy(values, stage.at[slot], sems.at[8 + 2 * slot]),
            pltpu.make_async_copy(places, marks.at[slot], sems.at[9 + 2 * slot]),
        )
        for copy in pair:
            copy.start()
        arrivals.append(pair)
    loads = []
    if before is not None:
        loads = [
            pltpu.make_async_copy(before.at[leaf], acc.at[leaf], sems.at[leaf])
            for leaf in range(4)
        ]
    for copy in loads:
        copy.start()
    for leaf in range(4):
        tpos[leaf] = place8[leaf].T
    for slot, (_, _, base) in enumerate(slots):
        for copy in arrivals[slot]:
            copy.wait()
        hi, lo = split(stage[slot])
        stack[slot, :PTS, :] = hi
        stack[slot, PTS:, :] = lo
        for coord in range(2):
            for half in range(2):
                spos[slot, coord : coord + 1, half * HALF : (half + 1) * HALF] = marks[
                    slot, pl.ds(base + 2 * coord + half, 1), :
                ]
    count = 0
    for slot, row, col, own_row, own_col in pairs:
        target = 2 * own_row + own_col
        table[count, 0] = slot
        table[count, 1] = target
        table[count, 2] = row - own_row
        table[count, 3] = col - own_col
        flag = flags[target, 3 * (row - own_row + 1) + col - own_col + 1]
        count = count + jnp.where(flag > 0, 1, 0)

    def evaluate(index, half, kern):
        slot, target = table[index, 0], table[index, 1]
        src_row = spos[slot, 0:1, :] + table[index, 2].astype(f32) * UNIT
        src_col = spos[slot, 1:2, :] + table[index, 3].astype(f32) * UNIT
        part = slice(half * HALF, (half + 1) * HALF)
        d_row = tpos[target, part, 0:1] - src_row
        d_col = tpos[target, part, 1:2] - src_col
        square = d_row * d_row + d_col * d_col
        dist = square * lax.rsqrt(jnp.maximum(square, 1e-30))
        decay = jnp.exp2(-dist)
        hi, lo = split(decay + decay * (dist * LN2))
        kern[part, :PTS] = hi
        kern[part, PTS:] = lo

    def apply(index, half, kern):
        slot, target = table[index, 0], table[index, 1]
        part = slice(half * HALF, (half + 1) * HALF)
        l_hi = stack[slot, :PTS, :]
        l_lo = stack[slot, PTS:, :]
        k_hi = kern[part, :PTS]
        k_lo = kern[part, PTS:]
        acc[target, part, :] += mm(k_hi, l_hi) + mm(k_lo, l_hi) + mm(k_hi, l_lo)

    def step(index, kern, other):
        following = jnp.minimum(index + 1, count - 1)
        for half in range(2):
            evaluate(following, half, other)
            apply(index, half, kern)

    @pl.when(count > 0)
    def _():
        for half in range(2):
            evaluate(0, half, kern_a)

    for copy in loads:
        copy.wait()
    if fill is not None:
        fill(acc, stage)

    @pl.loop(0, (count + 1) // 2)
    def _(pair):
        step(2 * pair, kern_a, kern_b)

        @pl.when(2 * pair + 1 < count)
        def _():
            step(2 * pair + 1, kern_b, kern_a)


    stores = [
        pltpu.make_async_copy(acc.at[leaf], out.at[leaf], sems.at[4 + leaf]) for leaf in range(4)
    ]
    for copy in stores:
        copy.start()
    for copy in stores:
        copy.wait()


ACC = shape(4, PTS, COLS)


def block(ref, start, rows):
    return ref.at[pl.ds(start, rows)]


def own_kernel(flags, place8, loss, msg, out, *scratch):
    slots = [(loss.at[leaf], block(msg, PTS + QUAD, 16), 4 * leaf) for leaf in range(4)]
    pairs = [(s, s // 2, s % 2, t // 2, t % 2) for s in range(4) for t in range(4)]

    def fill(acc, losses):
        for leaf in range(4):
            acc[leaf] = 0.5 * losses[leaf]

    near_blocks(flags, place8, slots, pairs, None, out, scratch, fill)


def lat_kernel(flags, place8, from_y, from_c, before, out, *scratch):
    parity = lat_parity()
    slots, pairs = [], []
    for ref, place, row, own_row in (
        (from_y, 8 - 8 * parity, 3 * parity - 1, parity),
        (from_c, 8 * parity, 2 - 3 * parity, 1 - parity),
    ):
        for col in range(2):
            for own_col in range(2):
                pairs.append((len(slots), row, col, own_row, own_col))
            slots.append(
                (block(ref, col * PTS, PTS), block(ref, 2 * PTS + QUAD, 16), place + 4 * col)
            )
    near_blocks(flags, place8, slots, pairs, before, out, scratch)


def lon_kernel(flags, place8, left, right, before, out, *scratch):
    parity = lat_parity()
    at = PTS + QUAD
    slots = [
        (block(left, 0, PTS), block(left, at, 16), 8 * parity + 4),
        (block(right, 0, PTS), block(right, at, 16), 8 * parity),
    ]
    pairs = [(s, parity, 3 * s - 1, i, s) for s in range(2) for i in range(2)]
    near_blocks(flags, place8, slots, pairs, before, out, scratch)


def last_kernel(
    flags, place8, a_left, a_right, left, right, c_ends, left_c, right_c, before, out, *scratch
):
    parity = lat_parity()
    at = PTS + QUAD
    own_place, far_place = 8 - 8 * parity, 8 * parity
    slots = [
        (left, block(a_left, at, 16), own_place + 4),
        (right, block(a_right, at, 16), own_place),
        (left_c, block(c_ends, QUAD, 16), far_place + 4),
        (right_c, block(c_ends, MSG + QUAD, 16), far_place),
    ]
    pairs = [(s, 1 - parity, 3 * s - 1, i, s) for s in range(2) for i in range(2)]
    pairs += [(2 + s, 2 - 3 * parity, 3 * s - 1, 1 - parity, s) for s in range(2)]
    near_blocks(flags, place8, slots, pairs, before, out, scratch)


def near(kernel, name, n_slots, n_pairs, operands, chained=True, cost=None, scratch=()):
    return pl.pallas_call(
        kernel,
        in_specs=[scalars, whole] + [hbm] * (len(operands) - 2),
        out_specs=[hbm],
        out_shape=[ACC],
        scratch_shapes=near_scratch(n_slots, n_pairs) + list(scratch),
        input_output_aliases={len(operands) - 1: 0} if chained else {},
        compiler_params=params(),
        cost_estimate=cost or COST,
        name=name,
    )(*operands)


def window_sum(flags, weights, bands, first=0):
    total = None
    for base, cells in bands:
        for v in range(6):
            if cells[v // 2] is None:
                continue
            ref, offset = cells[v // 2]
            for a in range(2):
                start = offset + (2 * a + v % 2) * RANK
                hi, lo = split(ref[start : start + RANK, :])
                u = base + a
                w = 6 * u + v
                rows = []
                for leaf in range(4):
                    part_w = weights[leaf, w - first]
                    d_row = u - 2 - leaf // 2
                    d_col = v - 2 - leaf % 2
                    if abs(d_col) <= 1:
                        inside = (d_row >= -1) & (d_row <= 1)
                        flag = flags[leaf, 3 * jnp.clip(d_row + 1, 0, 2) + d_col + 1]
                        keep = 1 - jnp.where(inside, flag, 0)
                        part_w = (part_w.astype(f32) * keep.astype(f32)).astype(bf16)
                    rows.append(part_w)
                stacked = jnp.concatenate(rows, 0)
                part = mm(stacked, hi) + mm(stacked, lo)
                total = part if total is None else total + part
    return total


def far_kernel(
    n_lat, n_lon, flags, weights, own, left, right, from_y, from_c, devices, c_ends,
    dev_w, dev_t, group_w, leaf_t, out, weights_v, cells, rows_dev, dev_w_v, dev_t_v,
    group_row_w, leaf_t_v, sems,
):
    lat = lax.axis_index("lat")
    lon = lax.axis_index("lon")
    parity = lax.rem(lat, 2)
    side = lax.rem(lon, 2)
    group_row, group_col = lat // 2, lon // 2
    n_gcol = n_lon // 2
    size = 2 * n_lon * RANK
    copies = []
    for source, target in (
        (dev_w, dev_w_v),
        (block(devices, 2 * MSG, size), rows_dev.at[0]),
        (block(c_ends, 2 * MSG, size), rows_dev.at[1]),
        (group_w.at[group_row, group_col], group_row_w),
        (dev_t, dev_t_v),
        (leaf_t, leaf_t_v),
        (block(own, PTS, QUAD), cells.at[0]),
        (block(left, PTS, QUAD), cells.at[1]),
        (block(right, PTS, QUAD), cells.at[2]),
        (block(from_y, 2 * PTS, QUAD), cells.at[3]),
        (block(from_c, 2 * PTS, QUAD), cells.at[4]),
        (block(c_ends, 0, QUAD), cells.at[5]),
        (block(c_ends, MSG, QUAD), cells.at[6]),
        (weights.at[0], weights_v.at[0]),
        (weights.at[1], weights_v.at[1]),
        (weights.at[2], weights_v.at[2]),
        (weights.at[3], weights_v.at[3]),
    ):
        copy = pltpu.make_async_copy(source, target, sems.at[len(copies)])
        copy.start()
        copies.append(copy)
    for copy in copies[:3]:
        copy.wait()

    def device_coef(k, back, col_side):
        which = jnp.where(side == col_side, 0, 1)
        start = pl.multiple_of((4 * back + 2 * (k // 2) + which) * RANK, RANK)
        return rows_dev[k % 2, pl.ds(start, RANK), :]

    total = jnp.zeros((RANK, COLS), f32)
    for k in range(n_lat):
        other = lat + k - 2 * (lat & k)
        u = other + 2 - 2 * group_row
        for v in range(6):
            shift = 2 * group_col - 2 + v
            drop = (jnp.abs(other - lat) <= 1) & (jnp.abs(shift - lon) <= 1)
            scale = jnp.where(drop, 0.0, 1.0)
            coef = device_coef(k, (1 - v // 2) % n_gcol, v % 2)
            total = total + scale * mm2(dev_w_v[6 * u + v], coef)
    for copy in copies[3:6]:
        copy.wait()

    def group_step(step, field):
        gcol = lax.rem(group_col + step, n_gcol)
        for pair in range(n_lat // 2):
            grow = group_row + pair - 2 * (group_row & pair)
            coef = jnp.zeros((RANK, COLS), f32)
            for e in range(2):
                k = 2 * pair + e
                other = lat + k - 2 * (lat & k)
                for f in range(2):
                    cell = other * n_lon + 2 * gcol + f
                    coef = coef + mm3(dev_t_v[cell], device_coef(k, n_gcol - step, f), (0, 0))
            field = field + mm2(group_row_w[grow, gcol], coef)
        return field

    field = lax.fori_loop(2, n_gcol - 1, group_step, jnp.zeros((RANK, COLS), f32))
    total = total + mm3(dev_t_v[lat * n_lon + lon], field)
    for copy in copies[6:]:
        copy.wait()
    far = window_sum(
        flags,
        weights_v,
        (
            (2, tuple((cells.at[i], 0) for i in (1, 0, 2))),
            (4 * parity, (None, (cells.at[3], 0), None)),
            (4 - 4 * parity, tuple((cells.at[i], 0) for i in (5, 4, 6))),
        ),
    )
    for leaf in range(4):
        rows = slice(leaf * RANK, (leaf + 1) * RANK)
        out[rows, :] = far[rows, :] + mm3(leaf_t_v[leaf], total)


def far_field(n_lat, n_lon, operands):
    return pl.pallas_call(
        functools.partial(far_kernel, n_lat, n_lon),
        in_specs=[scalars] + [hbm] * 12,
        out_specs=whole,
        out_shape=shape(QUAD, COLS),
        scratch_shapes=[
            VMEM((4, 36, RANK, RANK), bf16),
            VMEM((7, QUAD, COLS), f32),
            VMEM((2, 2 * n_lon * RANK, COLS), f32),
            VMEM((36, RANK, RANK), bf16),
            VMEM((n_lat * n_lon, RANK, RANK), f32),
            VMEM((n_lat // 2, n_lon // 2, RANK, RANK), bf16),
            VMEM((4, RANK, RANK), f32),
            pltpu.SemaphoreType.DMA((17,)),
        ],
        compiler_params=params(),
        cost_estimate=LOW,
        name="far",
    )(*operands)


def pack_kernel(*refs):
    parts, (out, sems) = refs[:-2], refs[-2:]
    copies = []
    row = 0
    for index, part in enumerate(parts):
        source = block(part, PTS, MSG) if index < 2 else part
        size = source.shape[0]
        copies.append(pltpu.make_async_copy(source, block(out, row, size), sems.at[index]))
        copies[-1].start()
        row += size
    for copy in copies:
        copy.wait()


def pack(left, right, devices):
    parts = [left, right, *devices]
    rows = 2 * MSG + sum(part.shape[0] for part in devices)
    return pl.pallas_call(
        pack_kernel,
        in_specs=[hbm] * len(parts),
        out_specs=whole,
        out_shape=shape(rows, COLS),
        scratch_shapes=[pltpu.SemaphoreType.DMA((len(parts),))],
        compiler_params=params(),
        cost_estimate=LOW,
        name="pack",
    )(*parts)


def down_kernel(
    flags, place8, weights, left_y, right_y, partial, basis, before, out, *scratch
):
    parity = lat_parity()
    near_refs, (weights_v, cells, basis_v, sems) = scratch[:-4], scratch[-4:]
    at = PTS + QUAD
    copies = []
    for source, target in (
        (block(left_y, PTS, QUAD), cells.at[0]),
        (block(right_y, PTS, QUAD), cells.at[1]),
        (partial, cells.at[2]),
        (weights.at[:, pl.ds(24 * parity, 12)], weights_v),
        (basis, basis_v),
    ):
        copy = pltpu.make_async_copy(source, target, sems.at[len(copies)])
        copy.start()
        copies.append(copy)

    def fill(acc, _):
        for copy in copies:
            copy.wait()
        band = (4 * parity, ((cells.at[0], 0), None, (cells.at[1], 0)))
        far = cells[2] + window_sum(flags, weights_v, (band,), 24 * parity)
        for leaf in range(4):
            acc[leaf] += mm3(basis_v[leaf], far[leaf * RANK : (leaf + 1) * RANK, :], (0, 0))

    base = 8 - 8 * parity
    slots = [
        (block(left_y, 0, PTS), block(left_y, at, 16), base + 4),
        (block(right_y, 0, PTS), block(right_y, at, 16), base),
    ]
    pairs = [(s, 3 * parity - 1, 3 * s - 1, parity, s) for s in range(2)]
    near_blocks(flags, place8, slots, pairs, before, out, near_refs, fill)


def local(
    losses,
    positions,
    leaf_basis,
    near_flags,
    leaf_coupling,
    leaf_transfer,
    device_coupling,
    device_transfer,
    group_coupling,
):
    n_lat = lax.axis_size("lat")
    n_lon = lax.axis_size("lon")

    flat = losses.reshape(4, PTS, COLS)
    basis = jnp.swapaxes(leaf_basis, 2, 3).reshape(4, RANK, PTS)
    flags = near_flags.reshape(4, 9)
    weights = leaf_coupling.reshape(4, 36, RANK, RANK)
    transfer = leaf_transfer.reshape(4, RANK, RANK)

    to_right = [(i, (i + 1) % n_lon) for i in range(n_lon)]
    to_left = [(i, (i - 1) % n_lon) for i in range(n_lon)]
    in_chip = [(i, i ^ 1) for i in range(n_lat)]
    across = [(i, i + 1 if i % 2 else i - 1) for i in range(n_lat)]
    across = [(a, b) for a, b in across if 0 <= b < n_lat]

    across_two = [(i, i ^ 2) for i in range(n_lat)]
    partner = [(i, i ^ 1) for i in range(n_lon)]
    barrier = lax.optimization_barrier

    a_right, a_left, b_right, b_left, to_y, to_c, place8, dev = coefficients(
        flat, basis, transfer, positions.reshape(4, 2, PTS)
    )
    dev_pair = lax.ppermute(dev, "lon", partner)
    from_c = lax.ppermute(to_c, "lat", in_chip)
    dev_pair, to_y = barrier((dev_pair, to_y))
    from_y = lax.ppermute(to_y, "lat", across)

    left = lax.ppermute(a_right, "lon", to_right)
    right = lax.ppermute(a_left, "lon", to_left)
    pair = jnp.concatenate([dev, dev_pair], 0)
    pair_two = lax.ppermute(pair, "lat", across_two)
    quad = jnp.concatenate([pair, pair_two], 0)

    def rotate(step):
        return lax.ppermute(quad, "lon", [(i, (i + step) % n_lon) for i in range(n_lon)])

    first, last = rotate(2), rotate(n_lon - 2)
    from_c, quad, place8 = barrier((from_c, quad, place8))
    (acc,) = near(own_kernel, "own", 4, 16, (flags, place8, flat, a_right), chained=False)
    from_y, quad, acc = barrier((from_y, quad, acc))
    moved = [first, *(rotate(step) for step in range(4, n_lon - 2, 2)), last]
    (acc,) = near(lat_kernel, "lat", 4, 8, (flags, place8, from_y, from_c, acc), cost=LOW)
    left, right, b_right, b_left, acc = barrier((left, right, b_right, b_left, acc))
    left_b = lax.ppermute(b_right, "lon", to_right)
    right_b = lax.ppermute(b_left, "lon", to_left)
    left_y = lax.ppermute(left, "lat", across)
    right_y = lax.ppermute(right, "lat", across)
    to_c = pack(left, right, (quad, *moved))
    c_ends = lax.ppermute(to_c, "lat", in_chip)
    (acc,) = near(lon_kernel, "lon", 2, 4, (flags, place8, left, right, acc))
    c_ends, acc = barrier((c_ends, acc))
    partial = far_field(
        n_lat,
        n_lon,
        (
            flags,
            weights,
            a_right,
            left,
            right,
            from_y,
            from_c,
            to_c,
            c_ends,
            device_coupling.reshape(36, RANK, RANK),
            device_transfer.reshape(n_lat * n_lon, RANK, RANK),
            group_coupling,
            transfer,
        ),
    )
    left_y, right_y, partial = barrier((left_y, right_y, partial))
    (acc,) = near(
        down_kernel,
        "down",
        2,
        2,
        (flags, place8, weights, left_y, right_y, partial, basis, acc),
        cost=LOW,
        scratch=[
            VMEM((4, 12, RANK, RANK), bf16),
            VMEM((3, QUAD, COLS), f32),
            VMEM((4, RANK, PTS), f32),
            pltpu.SemaphoreType.DMA((5,)),
        ],
    )
    left_b, right_b, acc = barrier((left_b, right_b, acc))
    left_c = lax.ppermute(left_b, "lat", in_chip)
    right_c = lax.ppermute(right_b, "lat", in_chip)
    (acc,) = near(
        last_kernel,
        "last",
        4,
        6,
        (flags, place8, left, right, left_b, right_b, c_ends, left_c, right_c, acc),
    )
    return acc.reshape(2, 2, PTS, COLS)


def solution(mesh):
    placed = (
        P("lat", "lon", None, None),
        P("lat", "lon", None, None),
        P("lat", "lon", None, None),
        P("lat", "lon", None),
        P("lat", "lon", None, None, None),
        P("lat", "lon", None, None),
        P("lat", "lon", None, None, None),
        P(),
        P(),
    )
    return jax.shard_map(
        local, mesh=mesh, in_specs=placed, out_specs=P("lat", "lon", None, None), check_vma=False
    )
```

```python
import functools

import jax
import jax.numpy as jnp
from jax import lax
from jax.experimental import pallas as pl
from jax.experimental.pallas import tpu as pltpu
from jax.sharding import PartitionSpec as P

PTS = 512
RANK = 64
COLS = 256
HALF = 256
QUAD = 4 * RANK
MSG = QUAD + 16

LN2 = 0.6931471805599453
UNIT = 1.7320508075688772 / 0.15 / LN2

f32 = jnp.float32
bf16 = jnp.bfloat16
VMEM = pltpu.VMEM
SMEM = pltpu.SMEM
whole = pl.BlockSpec(memory_space=VMEM)
scalars = pl.BlockSpec(memory_space=SMEM)


def split(x):
    hi = x.astype(bf16)
    return hi, (x - hi.astype(f32)).astype(bf16)


def mm(a, b, dims=(1, 0)):
    return lax.dot_general(
        a, b, (((dims[0],), (dims[1],)), ((), ())), preferred_element_type=f32
    )


def mm3(a, b, dims=(1, 0)):
    a_hi, a_lo = split(a)
    b_hi, b_lo = split(b)
    return mm(a_hi, b_hi, dims) + (mm(a_lo, b_hi, dims) + mm(a_hi, b_lo, dims))


def mm2(a, b):
    b_hi, b_lo = split(b)
    return mm(a, b_hi) + mm(a, b_lo)


def params(limit=64):
    return pltpu.CompilerParams(vmem_limit_bytes=limit * 1024 * 1024)


COST = pl.CostEstimate(flops=20_000_000_000, bytes_accessed=4_000_000, transcendentals=0)
LOW = pl.CostEstimate(flops=1_000, bytes_accessed=1_000, transcendentals=0)


def shape(*dims):
    return jax.ShapeDtypeStruct(dims, f32)


def lat_parity():
    return lax.rem(lax.axis_index("lat"), 2)


def coef_kernel(
    loss, basis, transfer, pos, a_right, a_left, b_right, b_left, to_y, to_c, place8, dev,
    values, bases, message, sems, load_sems,
):
    parity = lat_parity()
    loads = [
        (
            pltpu.make_async_copy(loss.at[leaf], values.at[leaf], load_sems.at[leaf]),
            pltpu.make_async_copy(basis.at[leaf], bases.at[leaf], load_sems.at[4 + leaf]),
        )
        for leaf in range(4)
    ]
    for pair in loads:
        for copy in pair:
            copy.start()
    for leaf in range(4):
        place = pos[leaf] * UNIT
        place8[leaf] = jnp.concatenate([place, jnp.zeros((6, PTS), f32)], 0)
        for coord in range(2):
            for half in range(2):
                at = QUAD + 4 * leaf + 2 * coord + half
                message[at : at + 1, :] = place[coord : coord + 1, half * HALF : (half + 1) * HALF]
    for pair in loads:
        for copy in pair:
            copy.wait()
    y_row, c_row = 2 * parity, 2 - 2 * parity
    first, second = slice(0, PTS), slice(PTS, 2 * PTS)
    copies = []
    for source, target in (
        (y_row + 1, a_right.at[first]),
        (y_row, a_left.at[first]),
        (c_row + 1, b_right),
        (c_row, b_left),
        (y_row, to_y.at[first]),
        (y_row + 1, to_y.at[second]),
        (c_row, to_c.at[first]),
        (c_row + 1, to_c.at[second]),
    ):
        copy = pltpu.make_async_copy(values.at[source], target, sems.at[len(copies)])
        copy.start()
        copies.append(copy)
    total = None
    for leaf in range(4):
        l_hi, l_lo = split(values[leaf])
        b_hi, b_lo = split(bases[leaf])
        coef = mm(b_hi, l_hi) + (mm(b_lo, l_hi) + mm(b_hi, l_lo))
        message[leaf * RANK : (leaf + 1) * RANK, :] = coef
        part = mm3(transfer[leaf], coef, (0, 0))
        total = part if leaf == 0 else total + part
    dev[...] = total
    for target in (
        a_right.at[PTS:], a_left.at[PTS:], to_y.at[2 * PTS :], to_c.at[2 * PTS :]
    ):
        copy = pltpu.make_async_copy(message, target, sems.at[len(copies)])
        copy.start()
        copies.append(copy)
    for copy in copies:
        copy.wait()


hbm = pl.BlockSpec(memory_space=pl.ANY)


def coefficients(losses, basis, transfer, positions):
    return pl.pallas_call(
        coef_kernel,
        in_specs=[hbm, hbm, whole, whole],
        out_specs=[hbm] * 6 + [whole] * 2,
        out_shape=[
            shape(PTS + MSG, COLS),
            shape(PTS + MSG, COLS),
            shape(PTS, COLS),
            shape(PTS, COLS),
            shape(2 * PTS + MSG, COLS),
            shape(2 * PTS + MSG, COLS),
            shape(4, 8, PTS),
            shape(RANK, COLS),
        ],
        scratch_shapes=[
            VMEM((4, PTS, COLS), f32),
            VMEM((4, RANK, PTS), f32),
            VMEM((MSG, COLS), f32),
            pltpu.SemaphoreType.DMA((12,)),
            pltpu.SemaphoreType.DMA((8,)),
        ],
        compiler_params=params(),
        cost_estimate=COST,
        name="coefs",
    )(losses, basis, transfer, positions)


def near_scratch(n_slots, n_pairs):
    return [
        SMEM((n_pairs + 1, 8), jnp.int32),
        VMEM((4, PTS, 8), f32),
        VMEM((n_slots, 8, PTS), f32),
        VMEM((n_slots, 2 * PTS, COLS), bf16),
        VMEM((PTS, 2 * PTS), bf16),
        VMEM((PTS, 2 * PTS), bf16),
        VMEM((4, PTS, COLS), f32),
        VMEM((n_slots, PTS, COLS), f32),
        VMEM((n_slots, 16, COLS), f32),
        pltpu.SemaphoreType.DMA((8 + 2 * n_slots,)),
    ]


def near_blocks(flags, place8, slots, pairs, before, out, scratch, fill=None):
    table, tpos, spos, stack, kern_a, kern_b, acc, stage, marks, sems = scratch
    arrivals = []
    for slot, (values, places, _) in enumerate(slots):
        pair = (
            pltpu.make_async_copy(values, stage.at[slot], sems.at[8 + 2 * slot]),
            pltpu.make_async_copy(places, marks.at[slot], sems.at[9 + 2 * slot]),
        )
        for copy in pair:
            copy.start()
        arrivals.append(pair)
    loads = []
    if before is not None:
        loads = [
            pltpu.make_async_copy(before.at[leaf], acc.at[leaf], sems.at[leaf])
            for leaf in range(4)
        ]
    for copy in loads:
        copy.start()
    for leaf in range(4):
        tpos[leaf] = place8[leaf].T
    for slot, (_, _, base) in enumerate(slots):
        for copy in arrivals[slot]:
            copy.wait()
        hi, lo = split(stage[slot])
        stack[slot, :PTS, :] = hi
        stack[slot, PTS:, :] = lo
        for coord in range(2):
            for half in range(2):
                spos[slot, coord : coord + 1, half * HALF : (half + 1) * HALF] = marks[
                    slot, pl.ds(base + 2 * coord + half, 1), :
                ]
    count = 0
    for slot, row, col, own_row, own_col in pairs:
        target = 2 * own_row + own_col
        table[count, 0] = slot
        table[count, 1] = target
        table[count, 2] = row - own_row
        table[count, 3] = col - own_col
        flag = flags[target, 3 * (row - own_row + 1) + col - own_col + 1]
        count = count + jnp.where(flag > 0, 1, 0)

    def evaluate(index, half, kern):
        slot, target = table[index, 0], table[index, 1]
        src_row = spos[slot, 0:1, :] + table[index, 2].astype(f32) * UNIT
        src_col = spos[slot, 1:2, :] + table[index, 3].astype(f32) * UNIT
        part = slice(half * HALF, (half + 1) * HALF)
        d_row = tpos[target, part, 0:1] - src_row
        d_col = tpos[target, part, 1:2] - src_col
        square = d_row * d_row + d_col * d_col
        dist = square * lax.rsqrt(jnp.maximum(square, 1e-30))
        decay = jnp.exp2(-dist)
        hi, lo = split(decay + decay * (dist * LN2))
        kern[part, :PTS] = hi
        kern[part, PTS:] = lo

    def apply(index, kern):
        slot, target = table[index, 0], table[index, 1]
        l_hi = stack[slot, :PTS, :]
        l_lo = stack[slot, PTS:, :]
        k_hi = kern[:, :PTS]
        k_lo = kern[:, PTS:]
        acc[target] += mm(k_hi, l_hi) + mm(k_lo, l_hi) + mm(k_hi, l_lo)

    def step(index, kern, other):
        following = jnp.minimum(index + 1, count - 1)
        for half in range(2):
            evaluate(following, half, other)
        apply(index, kern)

    @pl.when(count > 0)
    def _():
        for half in range(2):
            evaluate(0, half, kern_a)

    for copy in loads:
        copy.wait()
    if fill is not None:
        fill(acc, stage)

    @pl.loop(0, (count + 1) // 2)
    def _(pair):
        step(2 * pair, kern_a, kern_b)

        @pl.when(2 * pair + 1 < count)
        def _():
            step(2 * pair + 1, kern_b, kern_a)


    stores = [
        pltpu.make_async_copy(acc.at[leaf], out.at[leaf], sems.at[4 + leaf]) for leaf in range(4)
    ]
    for copy in stores:
        copy.start()
    for copy in stores:
        copy.wait()


ACC = shape(4, PTS, COLS)


def block(ref, start, rows):
    return ref.at[pl.ds(start, rows)]


def own_kernel(flags, place8, loss, msg, out, *scratch):
    slots = [(loss.at[leaf], block(msg, PTS + QUAD, 16), 4 * leaf) for leaf in range(4)]
    pairs = [(s, s // 2, s % 2, t // 2, t % 2) for s in range(4) for t in range(4)]

    def fill(acc, losses):
        for leaf in range(4):
            acc[leaf] = 0.5 * losses[leaf]

    near_blocks(flags, place8, slots, pairs, None, out, scratch, fill)


def lat_kernel(flags, place8, from_y, from_c, before, out, *scratch):
    parity = lat_parity()
    slots, pairs = [], []
    for ref, place, row, own_row in (
        (from_y, 8 - 8 * parity, 3 * parity - 1, parity),
        (from_c, 8 * parity, 2 - 3 * parity, 1 - parity),
    ):
        for col in range(2):
            for own_col in range(2):
                pairs.append((len(slots), row, col, own_row, own_col))
            slots.append(
                (block(ref, col * PTS, PTS), block(ref, 2 * PTS + QUAD, 16), place + 4 * col)
            )
    near_blocks(flags, place8, slots, pairs, before, out, scratch)


def lon_kernel(flags, place8, left, right, before, out, *scratch):
    parity = lat_parity()
    at = PTS + QUAD
    slots = [
        (block(left, 0, PTS), block(left, at, 16), 8 * parity + 4),
        (block(right, 0, PTS), block(right, at, 16), 8 * parity),
    ]
    pairs = [(s, parity, 3 * s - 1, i, s) for s in range(2) for i in range(2)]
    near_blocks(flags, place8, slots, pairs, before, out, scratch)


def last_kernel(
    flags, place8, a_left, a_right, left, right, c_ends, left_c, right_c, before, out, *scratch
):
    parity = lat_parity()
    at = PTS + QUAD
    own_place, far_place = 8 - 8 * parity, 8 * parity
    slots = [
        (left, block(a_left, at, 16), own_place + 4),
        (right, block(a_right, at, 16), own_place),
        (left_c, block(c_ends, QUAD, 16), far_place + 4),
        (right_c, block(c_ends, MSG + QUAD, 16), far_place),
    ]
    pairs = [(s, 1 - parity, 3 * s - 1, i, s) for s in range(2) for i in range(2)]
    pairs += [(2 + s, 2 - 3 * parity, 3 * s - 1, 1 - parity, s) for s in range(2)]
    near_blocks(flags, place8, slots, pairs, before, out, scratch)


def near(kernel, name, n_slots, n_pairs, operands, chained=True, cost=None, scratch=()):
    return pl.pallas_call(
        kernel,
        in_specs=[scalars, whole] + [hbm] * (len(operands) - 2),
        out_specs=[hbm],
        out_shape=[ACC],
        scratch_shapes=near_scratch(n_slots, n_pairs) + list(scratch),
        input_output_aliases={len(operands) - 1: 0} if chained else {},
        compiler_params=params(),
        cost_estimate=cost or COST,
        name=name,
    )(*operands)


def window_sum(flags, weights, bands, first=0):
    total = None
    for base, cells in bands:
        for v in range(6):
            if cells[v // 2] is None:
                continue
            ref, offset = cells[v // 2]
            for a in range(2):
                start = offset + (2 * a + v % 2) * RANK
                hi, lo = split(ref[start : start + RANK, :])
                u = base + a
                w = 6 * u + v
                rows = []
                for leaf in range(4):
                    part_w = weights[leaf, w - first]
                    d_row = u - 2 - leaf // 2
                    d_col = v - 2 - leaf % 2
                    if abs(d_col) <= 1:
                        inside = (d_row >= -1) & (d_row <= 1)
                        flag = flags[leaf, 3 * jnp.clip(d_row + 1, 0, 2) + d_col + 1]
                        keep = 1 - jnp.where(inside, flag, 0)
                        part_w = (part_w.astype(f32) * keep.astype(f32)).astype(bf16)
                    rows.append(part_w)
                stacked = jnp.concatenate(rows, 0)
                part = mm(stacked, hi) + mm(stacked, lo)
                total = part if total is None else total + part
    return total


def far_kernel(
    n_lat, n_lon, flags, weights, own, left, right, from_y, from_c, devices, c_ends,
    dev_w, dev_t, group_w, leaf_t, out, weights_v, cells, rows_dev, dev_w_v, dev_t_v,
    group_row_w, leaf_t_v, sems,
):
    lat = lax.axis_index("lat")
    lon = lax.axis_index("lon")
    parity = lax.rem(lat, 2)
    side = lax.rem(lon, 2)
    group_row, group_col = lat // 2, lon // 2
    n_gcol = n_lon // 2
    size = 2 * n_lon * RANK
    copies = []
    for source, target in (
        (dev_w, dev_w_v),
        (block(devices, 2 * MSG, size), rows_dev.at[0]),
        (block(c_ends, 2 * MSG, size), rows_dev.at[1]),
        (group_w.at[group_row, group_col], group_row_w),
        (dev_t, dev_t_v),
        (leaf_t, leaf_t_v),
        (block(own, PTS, QUAD), cells.at[0]),
        (block(left, PTS, QUAD), cells.at[1]),
        (block(right, PTS, QUAD), cells.at[2]),
        (block(from_y, 2 * PTS, QUAD), cells.at[3]),
        (block(from_c, 2 * PTS, QUAD), cells.at[4]),
        (block(c_ends, 0, QUAD), cells.at[5]),
        (block(c_ends, MSG, QUAD), cells.at[6]),
        (weights.at[0], weights_v.at[0]),
        (weights.at[1], weights_v.at[1]),
        (weights.at[2], weights_v.at[2]),
        (weights.at[3], weights_v.at[3]),
    ):
        copy = pltpu.make_async_copy(source, target, sems.at[len(copies)])
        copy.start()
        copies.append(copy)
    for copy in copies[:3]:
        copy.wait()

    def device_coef(k, back, col_side):
        which = jnp.where(side == col_side, 0, 1)
        start = pl.multiple_of((4 * back + 2 * (k // 2) + which) * RANK, RANK)
        return rows_dev[k % 2, pl.ds(start, RANK), :]

    total = jnp.zeros((RANK, COLS), f32)
    for k in range(n_lat):
        other = lat + k - 2 * (lat & k)
        u = other + 2 - 2 * group_row
        for v in range(6):
            shift = 2 * group_col - 2 + v
            drop = (jnp.abs(other - lat) <= 1) & (jnp.abs(shift - lon) <= 1)
            scale = jnp.where(drop, 0.0, 1.0)
            coef = device_coef(k, (1 - v // 2) % n_gcol, v % 2)
            total = total + scale * mm2(dev_w_v[6 * u + v], coef)
    for copy in copies[3:6]:
        copy.wait()

    def group_step(step, field):
        gcol = lax.rem(group_col + step, n_gcol)
        for pair in range(n_lat // 2):
            grow = group_row + pair - 2 * (group_row & pair)
            coef = jnp.zeros((RANK, COLS), f32)
            for e in range(2):
                k = 2 * pair + e
                other = lat + k - 2 * (lat & k)
                for f in range(2):
                    cell = other * n_lon + 2 * gcol + f
                    coef = coef + mm3(dev_t_v[cell], device_coef(k, n_gcol - step, f), (0, 0))
            field = field + mm2(group_row_w[grow, gcol], coef)
        return field

    field = lax.fori_loop(2, n_gcol - 1, group_step, jnp.zeros((RANK, COLS), f32))
    total = total + mm3(dev_t_v[lat * n_lon + lon], field)
    for copy in copies[6:]:
        copy.wait()
    far = window_sum(
        flags,
        weights_v,
        (
            (2, tuple((cells.at[i], 0) for i in (1, 0, 2))),
            (4 * parity, (None, (cells.at[3], 0), None)),
            (4 - 4 * parity, tuple((cells.at[i], 0) for i in (5, 4, 6))),
        ),
    )
    for leaf in range(4):
        rows = slice(leaf * RANK, (leaf + 1) * RANK)
        out[rows, :] = far[rows, :] + mm3(leaf_t_v[leaf], total)


def far_field(n_lat, n_lon, operands):
    return pl.pallas_call(
        functools.partial(far_kernel, n_lat, n_lon),
        in_specs=[scalars] + [hbm] * 12,
        out_specs=whole,
        out_shape=shape(QUAD, COLS),
        scratch_shapes=[
            VMEM((4, 36, RANK, RANK), bf16),
            VMEM((7, QUAD, COLS), f32),
            VMEM((2, 2 * n_lon * RANK, COLS), f32),
            VMEM((36, RANK, RANK), bf16),
            VMEM((n_lat * n_lon, RANK, RANK), f32),
            VMEM((n_lat // 2, n_lon // 2, RANK, RANK), bf16),
            VMEM((4, RANK, RANK), f32),
            pltpu.SemaphoreType.DMA((17,)),
        ],
        compiler_params=params(),
        cost_estimate=LOW,
        name="far",
    )(*operands)


def pack_kernel(*refs):
    parts, (out, sems) = refs[:-2], refs[-2:]
    copies = []
    row = 0
    for index, part in enumerate(parts):
        source = block(part, PTS, MSG) if index < 2 else part
        size = source.shape[0]
        copies.append(pltpu.make_async_copy(source, block(out, row, size), sems.at[index]))
        copies[-1].start()
        row += size
    for copy in copies:
        copy.wait()


def pack(left, right, devices):
    parts = [left, right, *devices]
    rows = 2 * MSG + sum(part.shape[0] for part in devices)
    return pl.pallas_call(
        pack_kernel,
        in_specs=[hbm] * len(parts),
        out_specs=whole,
        out_shape=shape(rows, COLS),
        scratch_shapes=[pltpu.SemaphoreType.DMA((len(parts),))],
        compiler_params=params(),
        cost_estimate=LOW,
        name="pack",
    )(*parts)


def down_kernel(
    flags, place8, weights, left_y, right_y, partial, basis, before, out, *scratch
):
    parity = lat_parity()
    near_refs, (weights_v, cells, basis_v, sems) = scratch[:-4], scratch[-4:]
    at = PTS + QUAD
    copies = []
    for source, target in (
        (block(left_y, PTS, QUAD), cells.at[0]),
        (block(right_y, PTS, QUAD), cells.at[1]),
        (partial, cells.at[2]),
        (weights.at[:, pl.ds(24 * parity, 12)], weights_v),
        (basis, basis_v),
    ):
        copy = pltpu.make_async_copy(source, target, sems.at[len(copies)])
        copy.start()
        copies.append(copy)

    def fill(acc, _):
        for copy in copies:
            copy.wait()
        band = (4 * parity, ((cells.at[0], 0), None, (cells.at[1], 0)))
        far = cells[2] + window_sum(flags, weights_v, (band,), 24 * parity)
        for leaf in range(4):
            acc[leaf] += mm3(basis_v[leaf], far[leaf * RANK : (leaf + 1) * RANK, :], (0, 0))

    base = 8 - 8 * parity
    slots = [
        (block(left_y, 0, PTS), block(left_y, at, 16), base + 4),
        (block(right_y, 0, PTS), block(right_y, at, 16), base),
    ]
    pairs = [(s, 3 * parity - 1, 3 * s - 1, parity, s) for s in range(2)]
    near_blocks(flags, place8, slots, pairs, before, out, near_refs, fill)


def local(
    losses,
    positions,
    leaf_basis,
    near_flags,
    leaf_coupling,
    leaf_transfer,
    device_coupling,
    device_transfer,
    group_coupling,
):
    n_lat = lax.axis_size("lat")
    n_lon = lax.axis_size("lon")

    flat = losses.reshape(4, PTS, COLS)
    basis = jnp.swapaxes(leaf_basis, 2, 3).reshape(4, RANK, PTS)
    flags = near_flags.reshape(4, 9)
    weights = leaf_coupling.reshape(4, 36, RANK, RANK)
    transfer = leaf_transfer.reshape(4, RANK, RANK)

    to_right = [(i, (i + 1) % n_lon) for i in range(n_lon)]
    to_left = [(i, (i - 1) % n_lon) for i in range(n_lon)]
    in_chip = [(i, i ^ 1) for i in range(n_lat)]
    across = [(i, i + 1 if i % 2 else i - 1) for i in range(n_lat)]
    across = [(a, b) for a, b in across if 0 <= b < n_lat]

    across_two = [(i, i ^ 2) for i in range(n_lat)]
    partner = [(i, i ^ 1) for i in range(n_lon)]
    barrier = lax.optimization_barrier

    a_right, a_left, b_right, b_left, to_y, to_c, place8, dev = coefficients(
        flat, basis, transfer, positions.reshape(4, 2, PTS)
    )
    dev_pair = lax.ppermute(dev, "lon", partner)
    from_c = lax.ppermute(to_c, "lat", in_chip)
    dev_pair, to_y = barrier((dev_pair, to_y))
    from_y = lax.ppermute(to_y, "lat", across)

    left = lax.ppermute(a_right, "lon", to_right)
    right = lax.ppermute(a_left, "lon", to_left)
    pair = jnp.concatenate([dev, dev_pair], 0)
    pair_two = lax.ppermute(pair, "lat", across_two)
    quad = jnp.concatenate([pair, pair_two], 0)

    def rotate(step):
        return lax.ppermute(quad, "lon", [(i, (i + step) % n_lon) for i in range(n_lon)])

    first, last = rotate(2), rotate(n_lon - 2)
    from_c, quad, place8 = barrier((from_c, quad, place8))
    (acc,) = near(own_kernel, "own", 4, 16, (flags, place8, flat, a_right), chained=False)
    from_y, quad, acc = barrier((from_y, quad, acc))
    moved = [first, *(rotate(step) for step in range(4, n_lon - 2, 2)), last]
    (acc,) = near(lat_kernel, "lat", 4, 8, (flags, place8, from_y, from_c, acc), cost=LOW)
    left, right, b_right, b_left, acc = barrier((left, right, b_right, b_left, acc))
    left_b = lax.ppermute(b_right, "lon", to_right)
    right_b = lax.ppermute(b_left, "lon", to_left)
    left_y = lax.ppermute(left, "lat", across)
    right_y = lax.ppermute(right, "lat", across)
    to_c = pack(left, right, (quad, *moved))
    c_ends = lax.ppermute(to_c, "lat", in_chip)
    (acc,) = near(lon_kernel, "lon", 2, 4, (flags, place8, left, right, acc))
    c_ends, acc = barrier((c_ends, acc))
    partial = far_field(
        n_lat,
        n_lon,
        (
            flags,
            weights,
            a_right,
            left,
            right,
            from_y,
            from_c,
            to_c,
            c_ends,
            device_coupling.reshape(36, RANK, RANK),
            device_transfer.reshape(n_lat * n_lon, RANK, RANK),
            group_coupling,
            transfer,
        ),
    )
    left_y, right_y, partial = barrier((left_y, right_y, partial))
    (acc,) = near(
        down_kernel,
        "down",
        2,
        2,
        (flags, place8, weights, left_y, right_y, partial, basis, acc),
        cost=LOW,
        scratch=[
            VMEM((4, 12, RANK, RANK), bf16),
            VMEM((3, QUAD, COLS), f32),
            VMEM((4, RANK, PTS), f32),
            pltpu.SemaphoreType.DMA((5,)),
        ],
    )
    left_b, right_b, acc = barrier((left_b, right_b, acc))
    left_c = lax.ppermute(left_b, "lat", in_chip)
    right_c = lax.ppermute(right_b, "lat", in_chip)
    (acc,) = near(
        last_kernel,
        "last",
        4,
        6,
        (flags, place8, left, right, left_b, right_b, c_ends, left_c, right_c, acc),
    )
    return acc.reshape(2, 2, PTS, COLS)


def solution(mesh):
    placed = (
        P("lat", "lon", None, None),
        P("lat", "lon", None, None),
        P("lat", "lon", None, None),
        P("lat", "lon", None),
        P("lat", "lon", None, None, None),
        P("lat", "lon", None, None),
        P("lat", "lon", None, None, None),
        P(),
        P(),
    )
    return jax.shard_map(
        local, mesh=mesh, in_specs=placed, out_specs=P("lat", "lon", None, None), check_vma=False
    )
```
